32 devices in a mesh: dp: 4 (over y, x), seq: 8 (over z, core).
Axes of the slice: x: 2, y: 2, z: 4, core: 2. Of those that a mesh axis runs over, the one named last changes fastest.
Arguments:
- tokens: bfloat16 [16384, 1024], P(('dp', 'seq')), may hold values from -6 to 6
- doc_lengths: int32 [4, 3], P('dp'), may hold values from 1 to 4094, as said below
- norm_gain: bfloat16 [1024], replicated, may hold values from 0.5 to 1.5
- w_qkv: bfloat16 [1024, 3072], P(('dp', 'seq')), may hold values from -0.1875 to 0.1875
- w_beta: bfloat16 [1024, 8], P(('dp', 'seq')), may hold values from -0.375 to 0.375
- conv_weight: bfloat16 [4, 3072], replicated, may hold values from -3 to 3
- head_gain: bfloat16 [128], replicated, may hold values from 0.5 to 1.5
- w_out: bfloat16 [1024, 1024], P(('dp', 'seq')), may hold values from -0.1875 to 0.1875
- mlp_gain: bfloat16 [1024], replicated, may hold values from 0.5 to 1.5
- w_mlp_in: bfloat16 [1024, 5632], P(('dp', 'seq')), may hold values from -0.1875 to 0.1875
- w_down: bfloat16 [2816, 1024], P(('dp', 'seq')), may hold values from -0.109375 to 0.109375
- grad_out: bfloat16 [16384, 1024], P(('dp', 'seq')), may hold values from -6 to 6
Outputs:
- out: bfloat16 [16384, 1024], P(('dp', 'seq'))
- grad_tokens: bfloat16 [16384, 1024], P(('dp', 'seq'))
- grad_norm_gain: float32 [1024], replicated
- grad_w_qkv: float32 [1024, 3072], P(('dp', 'seq'))
- grad_w_beta: float32 [1024, 8], P(('dp', 'seq'))
- grad_conv: float32 [4, 3072], replicated
- grad_head_gain: float32 [128], replicated
- grad_w_out: float32 [1024, 1024], P(('dp', 'seq'))
- grad_mlp_gain: float32 [1024], replicated
- grad_w_mlp_in: float32 [1024, 5632], P(('dp', 'seq'))
- grad_w_down: float32 [2816, 1024], P(('dp', 'seq'))
The draws below stay inside these ranges and needn't reach their ends.
Inputs may be any that keep to these rules, and one draw needn't show every extreme that they name: `doc_lengths`: each row holds, in order, the lengths of the three documents packed into one group's 4096 tokens; the first and the last are each shorter than 512.
All inputs are finite; a program needn't handle non-finite values.
Results may differ from the reference program's by a relative error of at most 0.015.
Values may be sent and summed in bfloat16 or wider, within the bound.
A program may use at most 320 MiB of HBM per device.

```python
import jax
import jax.numpy as jnp
from jax import lax

D = 1024
HEADS = 8
HEAD_DIM = 128
FF = 2816
CONV = 4
SEQ_LEN = 4096
TOK_DEV = 512
TOKENS = 16384
N_DP = 4


def draw_doc_lengths(key, part):
    key = jax.random.fold_in(key, 7)
    edges = jax.random.randint(key, (N_DP, 2), 1, TOK_DEV // 2 + 1)
    middle = SEQ_LEN - edges[:, 0] - edges[:, 1]
    return jnp.stack([edges[:, 0], middle, edges[:, 1]], axis=1).astype(jnp.int32)


def block_levels(rng, extent, cuts, smallest, largest):
    level, own = 1.0, jax.random.fold_in(rng, 6)
    for position, shards_of in cuts:
        heights = jnp.exp(jax.random.uniform(jax.random.fold_in(own, position), (shards_of,), jnp.float32, smallest / len(cuts), largest / len(cuts)))
        level = level * jnp.repeat(heights, extent[position] // shards_of).reshape([-1 if axis == position else 1 for axis in range(len(extent))])
    return level


def gaussian(own_key, shape, scale, bound, cuts=(), held_as=jnp.bfloat16):
    factor_of = block_levels(own_key, shape, cuts, -0.22, 0.18) if cuts else 1.0
    result = jax.random.normal(own_key, shape, jnp.float32) * scale * factor_of
    return jnp.minimum(jnp.maximum(result, -bound), bound).astype(held_as)


def setup_inputs(seed: int = 0) -> dict:
    keys = jax.random.split(jax.random.key(seed), 13)
    tokens = gaussian(keys[0], (TOKENS, D), 1.0, 6.0, ((0, 32),))
    doc_lengths = draw_doc_lengths(jax.random.fold_in(keys[12], 71), 0)
    norm_gain = jnp.clip(1.0 + 0.1 * jax.random.normal(keys[2], (D,), jnp.float32), 0.5, 1.5).astype(jnp.bfloat16)
    w_qkv = gaussian(keys[3], (D, 3 * D), D ** -0.5, 0.1875, ((0, 32),))
    w_beta = gaussian(keys[4], (D, HEADS), (D // 4) ** -0.5, 0.375, ((0, 32),))
    conv_weight = gaussian(keys[5], (CONV, 3 * D), CONV ** -0.5, 3.0)
    head_gain = jnp.clip(1.0 + 0.1 * jax.random.normal(keys[6], (HEAD_DIM,), jnp.float32), 0.5, 1.5).astype(jnp.bfloat16)
    w_out = gaussian(keys[7], (D, D), D ** -0.5, 0.1875, ((0, 32),))
    mlp_gain = jnp.clip(1.0 + 0.1 * jax.random.normal(keys[8], (D,), jnp.float32), 0.5, 1.5).astype(jnp.bfloat16)
    w_mlp_in = gaussian(keys[9], (D, 2 * FF), D ** -0.5, 0.1875, ((0, 32),))
    w_down = gaussian(keys[10], (FF, D), FF ** -0.5, 0.109375, ((0, 32),))
    grad_out = gaussian(keys[11], (TOKENS, D), 1.0, 6.0, ((0, 32),))
    return dict(tokens=tokens, doc_lengths=doc_lengths, norm_gain=norm_gain, w_qkv=w_qkv, w_beta=w_beta, conv_weight=conv_weight, head_gain=head_gain, w_out=w_out, mlp_gain=mlp_gain, w_mlp_in=w_mlp_in, w_down=w_down, grad_out=grad_out)


@jax.custom_vjp
def low(v):
    return lax.optimization_barrier(v.astype(jnp.bfloat16)).astype(jnp.float32)

@jax.custom_vjp
def low_back(v):
    return v

def low_keep(v):
    return (low(v), None)

def low_pass(kept, grad):
    return (grad,)

def back_keep(v):
    return (v, None)

def back_low(kept, grad):
    return (low(grad),)
low.defvjp(low_keep, low_pass)
low_back.defvjp(back_keep, back_low)
norm_eps = 1e-05
unit_eps = 1e-06
highest = lax.Precision.HIGHEST

def product(left, right):
    return jnp.dot(left, right, precision=highest)

def rms_scale(values, gain):
    return values * lax.rsqrt(lax.optimization_barrier(jnp.mean(values * values, axis=-1, keepdims=True)) + norm_eps) * gain

def doc_ids(lengths, positions):
    ends = jnp.cumsum(lengths)
    inside = (positions[:, None] >= ends[None, :]).astype(jnp.int32)
    return jnp.where(positions >= 0, lax.optimization_barrier(jnp.sum(inside, axis=1)), -1)

def short_conv(padded, weight, docs_pad):
    kernel = weight.shape[0]
    row_count = padded.shape[0] - kernel + 1
    total = jnp.zeros((row_count, padded.shape[1]), padded.dtype)
    for offset in range(kernel):
        keep = (docs_pad[offset:offset + row_count] == docs_pad[kernel - 1:]).astype(jnp.float32)
        total = total + weight[offset] * padded[offset:offset + row_count] * keep[:, None]
    return total

def features(padded, weight, logits, docs_pad):
    mixed = jax.nn.silu(short_conv(padded, weight, docs_pad))
    row_count = mixed.shape[0]
    heads = logits.shape[1]
    mixed = mixed.reshape(row_count, 3, heads, -1)
    width = mixed.shape[-1]
    query = mixed[:, 0]
    keyed = mixed[:, 1]
    value = mixed[:, 2]
    query = query * lax.rsqrt(lax.optimization_barrier(jnp.sum(query * query, axis=-1, keepdims=True)) + unit_eps) * width ** (-0.5)
    keyed = keyed * lax.rsqrt(lax.optimization_barrier(jnp.sum(keyed * keyed, axis=-1, keepdims=True)) + unit_eps)
    return (query, keyed, value, jax.nn.sigmoid(logits))

def delta_scan(query, keyed, value, beta, starts):
    length, heads, width = keyed.shape
    block = min(64, length)
    blocks = length // block

    def token_step(state, pieces):
        query_now, key_now, value_now, beta_now, start_now = pieces
        state = state * (1.0 - start_now)
        guess = jnp.einsum('hvk,hk->hv', state, key_now, precision=highest)
        state = state - beta_now[:, None, None] * (guess - value_now)[:, :, None] * key_now[:, None, :]
        return (state, jnp.einsum('hvk,hk->hv', state, query_now, precision=highest))

    @jax.checkpoint
    def block_step(state, pieces):
        return lax.scan(token_step, state, pieces)
    pieces = tuple((a.reshape((blocks, block) + a.shape[1:]) for a in (query, keyed, value, beta, starts)))
    initial = jnp.zeros((heads, width, width), query.dtype)
    _, results = lax.scan(block_step, initial, pieces)
    return results.reshape(length, heads, width)

def swiglu(gate_up):
    half = gate_up.shape[1] // 2
    return jax.nn.silu(gate_up[:, :half]) * gate_up[:, half:]

def layer(inputs, lengths, norm_gain, w_qkv, w_beta, conv_weight, head_gain, w_out, mlp_gain, w_mlp_in, w_down):
    length = inputs.shape[0]
    kernel = conv_weight.shape[0]
    qkv_width = w_qkv.shape[1]
    xn1 = low(rms_scale(inputs, norm_gain))
    proj = low_back(product(xn1, jnp.concatenate([w_qkv, w_beta], axis=1)))
    projected = proj[:, :qkv_width]
    logits = proj[:, qkv_width:]
    positions = jnp.arange(length + kernel - 1, dtype=jnp.int32) - (kernel - 1)
    docs_pad = doc_ids(lengths, positions)
    docs = docs_pad[kernel - 1:]
    previous = jnp.concatenate([jnp.full((1,), -1, jnp.int32), docs[:-1]])
    starts = (docs != previous).astype(jnp.float32)
    padded = jnp.pad(projected, ((kernel - 1, 0), (0, 0)))
    query, keyed, value, beta = features(padded, conv_weight, logits, docs_pad)
    mixed = delta_scan(query, keyed, value, beta, starts)
    head_out = low(rms_scale(mixed, head_gain).reshape(length, -1))
    hidden_one = inputs + low_back(product(head_out, w_out))
    xn2 = low(rms_scale(hidden_one, mlp_gain))
    gate_up = low_back(product(xn2, w_mlp_in))
    hidden = low(swiglu(gate_up))
    return hidden_one + product(hidden, w_down)

def reference(tokens, doc_lengths, norm_gain, w_qkv, w_beta, conv_weight, head_gain, w_out, mlp_gain, w_mlp_in, w_down, grad_out):
    weights = tuple((a.astype(jnp.float32) for a in (norm_gain, w_qkv, w_beta, conv_weight, head_gain, w_out, mlp_gain, w_mlp_in, w_down)))
    inputs = tokens.astype(jnp.float32).reshape(N_DP, SEQ_LEN, D)

    def whole(group_inputs, *params):

        @jax.checkpoint
        def group_step(carry, pieces):
            return (carry, layer(pieces[0], pieces[1], *params))
        _, results = lax.scan(group_step, None, (group_inputs, doc_lengths))
        return results
    results, pull = jax.vjp(whole, inputs, *weights)
    grads = pull(grad_out.astype(jnp.float32).reshape(N_DP, SEQ_LEN, D))
    return (results.reshape(TOKENS, D).astype(jnp.bfloat16), grads[0].reshape(TOKENS, D).astype(jnp.bfloat16), grads[1], grads[2], grads[3], grads[4], grads[5], grads[6], grads[7], grads[8], grads[9])
```

```python
import functools

import jax
import jax.numpy as jnp
from jax import lax
from jax.experimental import pallas as pl
from jax.experimental.pallas import tpu as pltpu
from jax.sharding import PartitionSpec as P

norm_eps = 1e-05
unit_eps = 1e-06
MESH = pl.DeviceIdType.MESH
f32, bf16 = jnp.float32, jnp.bfloat16
HIGH = lax.Precision.HIGH
VMEM_LIMIT = 56 << 20


def nn(a, b, prec=None):
    return lax.dot_general(a, b, (((1,), (0,)), ((), ())), precision=prec, preferred_element_type=f32)


def nt(a, b, prec=None):
    return lax.dot_general(a, b, (((1,), (1,)), ((), ())), precision=prec, preferred_element_type=f32)


def tn(a, b, prec=None):
    return lax.dot_general(a, b, (((0,), (0,)), ((), ())), precision=prec, preferred_element_type=f32)


def unit_lower_inverse(a, row, col):
    size = a.shape[0]
    block = min(8, size)
    eye = (row == col).astype(f32)
    step = jnp.where(row // block == col // block, -a, 0.0)
    inverse = eye + step
    power = block // 2
    while power >= 1:
        if power > 0 and block > 2:
            step = nn(step, step, HIGH)
            inverse = inverse + nn(inverse, step, HIGH)
        power //= 2
        if power < 2:
            break
    while block < size:
        off = jnp.where((row // (2 * block) == col // (2 * block)) & (row // block == col // block + 1), a, 0.0)
        inverse = inverse - nn(inverse, nn(off, inverse, HIGH), HIGH)
        block *= 2
    return inverse


def head_column(matrix, head):
    lane = lax.broadcasted_iota(jnp.int32, matrix.shape, 1)
    return jnp.sum(jnp.where(lane == head, matrix, 0.0), axis=1, keepdims=True)


def masks_of(docs_col, docs_row):
    size = docs_col.shape[0]
    row = lax.broadcasted_iota(jnp.int32, (size, size), 0)
    col = lax.broadcasted_iota(jnp.int32, (size, size), 1)
    same = docs_col == docs_row
    return row, col, same


def local_kernel(
    chunk, pq, pk, pv, hq, hk, hv, tq, tk, tv, aux, docs_c, docs_r, logits,
    cq, ck, cv, w_o, u_o, qt_o, o_o, t_o, p_o, kk_o, dt_o, ft_o, seg_o, pad,
):
    head = pl.program_id(0)
    rows, width = pq.shape
    keeps = (aux[:, 2:3], aux[:, 3:4], aux[:, 4:5])
    acts = []
    for src, halo, taps, dst in ((pq, hq, tq, cq), (pk, hk, tk, ck), (pv, hv, tv, cv)):
        pad[0:8, :] = halo[...]
        pad[8 : 8 + rows, :] = src[...]
        conv = taps[3:4, :] * src[...]
        for back in (1, 2, 3):
            conv = conv + taps[3 - back : 4 - back, :] * (pad[8 - back : 8 - back + rows, :] * keeps[back - 1])
        dst[...] = conv
        acts.append(conv * jax.nn.sigmoid(conv))
    q = acts[0] * (lax.rsqrt(jnp.sum(acts[0] * acts[0], axis=1, keepdims=True) + unit_eps) * width ** (-0.5))
    k = acts[1] * lax.rsqrt(jnp.sum(acts[1] * acts[1], axis=1, keepdims=True) + unit_eps)
    v = acts[2]
    beta = jax.nn.sigmoid(head_column(logits[...], head))
    cont, last = aux[:, 0:1], aux[:, 1:2]
    seg = None
    for c in range(rows // chunk):
        sl = slice(c * chunk, (c + 1) * chunk)
        row, col, same = masks_of(docs_c[sl, :], docs_r[:, sl])
        qc, kc, vc, bc, cc, lc = q[sl], k[sl], v[sl], beta[sl], cont[sl], last[sl]
        kk = nt(kc, kc, HIGH)
        a = jnp.where(same & (row > col), bc * kk, 0.0)
        t = unit_lower_inverse(a, row, col)
        wu = nn(t, jnp.concatenate([(bc * cc) * kc, bc * vc], axis=1), HIGH)
        p = jnp.where(same & (row >= col), nt(qc, kc, HIGH), 0.0)
        pwu = nn(p, wu, HIGH)
        x = tn(lc * kc, wu, HIGH)
        d_row = lax.broadcasted_iota(jnp.int32, (width, width), 0)
        d_col = lax.broadcasted_iota(jnp.int32, (width, width), 1)
        dt = jnp.where(d_row == d_col, cc[chunk - 1 : chunk], 0.0) - x[:, :width]
        ft = x[:, width:]
        w_o[sl, :] = wu[:, :width]
        u_o[sl, :] = wu[:, width:]
        qt_o[sl, :] = cc * qc - pwu[:, :width]
        o_o[sl, :] = pwu[:, width:]
        t_o[sl, :] = t
        p_o[sl, :] = p
        kk_o[sl, :] = kk
        dt_o[c * width : (c + 1) * width, :] = dt
        ft_o[c * width : (c + 1) * width, :] = ft
        if seg is None:
            seg = jnp.concatenate([dt, ft], axis=1)
        else:
            seg = nn(dt, seg, HIGH)
            seg = jnp.concatenate([seg[:, :width], seg[:, width:] + ft], axis=1)
    seg_o[...] = seg


def relay_kernel(n_seq, back, map_ref, add_ref, out_ref, send, ssem, rsem):
    d, s = lax.axis_index("dp"), lax.axis_index("seq")
    heads = map_ref.shape[0]
    if back:
        first, final = s == n_seq - 1, s == 0
        ahead, behind = s - 1, s + 1
    else:
        first, final = s == 0, s == n_seq - 1
        ahead, behind = s + 1, s - 1
    barrier = pltpu.get_barrier_semaphore()

    @pl.when(jnp.logical_not(first))
    def _():
        pl.semaphore_signal(barrier, inc=1, device_id=(d, behind), device_id_type=MESH)

    @pl.when(jnp.logical_not(final))
    def _():
        pl.semaphore_signal(barrier, inc=1, device_id=(d, ahead), device_id_type=MESH)

    pl.semaphore_wait(barrier, jnp.where(first | final, 1, 2))

    def copy_of(h):
        return pltpu.make_async_remote_copy(
            src_ref=send.at[h], dst_ref=out_ref.at[h], send_sem=ssem.at[h], recv_sem=rsem.at[h],
            device_id=(d, ahead), device_id_type=MESH,
        )

    @pl.when(first)
    def _():
        out_ref[...] = jnp.zeros(out_ref.shape, out_ref.dtype)

    for h in range(heads):
        @pl.when(jnp.logical_not(first))
        def _():
            copy_of(h).wait_recv()

        @pl.when(jnp.logical_not(final))
        def _():
            state = out_ref[h].astype(f32)
            mult = tn if back else nn
            send[h] = (mult(map_ref[h], state, HIGH) + add_ref[h]).astype(bf16)
            copy_of(h).start()

    @pl.when(jnp.logical_not(final))
    def _():
        for h in range(heads):
            copy_of(h).wait_send()


def output_kernel(chunk, zin, dt, ft, qt, o0, gain, z_o, o_o, head_o):
    rows, width = qt.shape
    z = zin[0].astype(f32)
    for c in range(rows // chunk):
        sl = slice(c * chunk, (c + 1) * chunk)
        ds = slice(c * width, (c + 1) * width)
        z_o[ds, :] = z
        o = o0[sl, :] + nn(qt[sl, :], z, HIGH)
        o_o[sl, :] = o
        scale = lax.rsqrt(jnp.mean(o * o, axis=1, keepdims=True) + norm_eps)
        head_o[sl, :] = (o * scale * gain[...]).astype(bf16)
        if c + 1 < rows // chunk:
            z = nn(dt[ds, :], z, HIGH) + ft[ds, :]


def seed_kernel(chunk, dh, o, gain, qt, dt, do_o, b_o, seed_o, dgain_o):
    head = pl.program_id(0)
    rows, width = qt.shape
    ov, dhv = o[...], dh[...]
    scale = lax.rsqrt(jnp.mean(ov * ov, axis=1, keepdims=True) + norm_eps)
    n = ov * scale
    dg = jnp.sum(dhv * n, axis=0, keepdims=True)
    dgain_o[...] = jnp.where(head == 0, 0.0, dgain_o[...]) + jnp.broadcast_to(dg, dgain_o.shape)
    y = dhv * gain[...]
    do = (y - n * jnp.mean(y * n, axis=1, keepdims=True)) * scale
    do_o[...] = do
    g = None
    for c in reversed(range(rows // chunk)):
        sl = slice(c * chunk, (c + 1) * chunk)
        ds = slice(c * width, (c + 1) * width)
        b_o[ds, :] = tn(qt[sl, :], do[sl], HIGH)
        g = b_o[ds, :] if g is None else tn(dt[ds, :], g, HIGH) + b_o[ds, :]
    seed_o[0] = g


def back_kernel(
    chunk, pq, pk, pv, hq, hk, hv, tq, tk, tv, aux, docs_c, docs_r, logits,
    cq, ck, cv, w_r, u_r, t_r, p_r, kk_r, z_r, do_r, dt_r, b_r, g_r,
    dpq, dpk, dpv, dhq, dhk, dhv, dtq, dtk, dtv, dlogit_o, pad, mask1, mask2, mask3,
):
    head = pl.program_id(0)
    rows, width = pq.shape
    cont, last = aux[:, 0:1], aux[:, 1:2]
    keeps = (aux[:, 2:3], aux[:, 3:4], aux[:, 4:5])
    scale = width ** (-0.5)
    beta = jax.nn.sigmoid(head_column(logits[...], head))
    sq, sk, sv = (jax.nn.sigmoid(x[...]) for x in (cq, ck, cv))
    aq, ak, v = cq[...] * sq, ck[...] * sk, cv[...] * sv
    iq = lax.rsqrt(jnp.sum(aq * aq, axis=1, keepdims=True) + unit_eps)
    ik = lax.rsqrt(jnp.sum(ak * ak, axis=1, keepdims=True) + unit_eps)
    uq, k = aq * iq, ak * ik
    q = uq * scale
    g = g_r[0].astype(f32)
    dqs, dks, dvs, dbs = [], [], [], []
    for c in reversed(range(rows // chunk)):
        sl = slice(c * chunk, (c + 1) * chunk)
        ds = slice(c * width, (c + 1) * width)
        row, col, same = masks_of(docs_c[sl, :], docs_r[:, sl])
        qc, kc, vc, bc, cc, lc = q[sl], k[sl], v[sl], beta[sl], cont[sl], last[sl]
        z = z_r[ds, :]
        do = do_r[sl, :]
        wkz = nn(jnp.concatenate([w_r[sl, :], kc], axis=0), z)
        u = u_r[sl, :] - wkz[:chunk]
        kz = wkz[chunk:]
        du = tn(p_r[sl, :], do) + nn(lc * kc, g)
        dr = tn(t_r[sl, :], du)
        y = nt(jnp.concatenate([do, dr], axis=0), jnp.concatenate([u, z], axis=0))
        dp = jnp.where(same & (row >= col), y[:chunk, :chunk], 0.0)
        da = jnp.where(same & (row > col), -y[chunk:, :chunk], 0.0)
        bda = bc * da
        pak = nn(jnp.concatenate([dp, bda], axis=0), kc)
        dqs.append(cc * y[:chunk, chunk:] + pak[:chunk])
        dks.append(
            tn(jnp.concatenate([dp, bda], axis=0), jnp.concatenate([qc, kc], axis=0))
            + pak[chunk:] + lc * nt(u, g) - (bc * cc) * y[chunk:, chunk:]
        )
        dvs.append(bc * dr)
        dbs.append(
            jnp.sum(dr * (vc - cc * kz), axis=1, keepdims=True)
            + jnp.sum(da * kk_r[sl, :], axis=1, keepdims=True)
        )
        if c > 0:
            g = tn(dt_r[ds, :], g) + b_r[ds, :]
    dq, dk, dv, db = (jnp.concatenate(x[::-1], axis=0) for x in (dqs, dks, dvs, dbs))
    lane = lax.broadcasted_iota(jnp.int32, dlogit_o.shape, 1)
    dlogit_o[...] = jnp.where(lane == head, db * beta * (1.0 - beta), jnp.where(head == 0, 0.0, dlogit_o[...]))
    du_q = dq * scale
    da_q = (du_q - uq * jnp.sum(uq * du_q, axis=1, keepdims=True)) * iq
    da_k = (dk - k * jnp.sum(k * dk, axis=1, keepdims=True)) * ik
    for dact, sg, c_r, src, halo, taps, dst, dhalo, dtaps in (
        (da_q, sq, cq, pq, hq, tq, dpq, dhq, dtq),
        (da_k, sk, ck, pk, hk, tk, dpk, dhk, dtk),
        (dv, sv, cv, pv, hv, tv, dpv, dhv, dtv),
    ):
        dconv = dact * (sg * (1.0 + c_r[...] * (1.0 - sg)))
        pad[0:8, :] = halo[...]
        pad[8 : 8 + rows, :] = src[...]
        zero = jnp.zeros((8, width), f32)
        total = taps[3:4, :] * dconv
        early = zero
        gtaps = [None] * 4
        gtaps[3] = jnp.sum(dconv * src[...], axis=0, keepdims=True)
        for back, mask in ((1, mask1), (2, mask2), (3, mask3)):
            kept = dconv * keeps[back - 1]
            gtaps[3 - back] = jnp.sum(kept * pad[8 - back : 8 - back + rows, :], axis=0, keepdims=True)
            mask[0:8, :] = zero
            mask[8 : 8 + rows, :] = kept
            mask[8 + rows : 16 + rows, :] = zero
            total = total + taps[3 - back : 4 - back, :] * mask[8 + back : 8 + back + rows, :]
            early = early + taps[3 - back : 4 - back, :] * mask[back : back + 8, :]
        dst[...] = total
        dhalo[...] = early
        dtaps[...] = jnp.concatenate(gtaps + [jnp.zeros((4, width), f32)], axis=0)


def from_behind(value, axis, steps):
    count = lax.axis_size(axis)
    first, last = (max(0, -steps), min(count, count - steps))
    return lax.ppermute(value, axis, [(source, source + steps) for source in range(first, last)])


def rms_scale(values, gain):
    return values * lax.rsqrt(jnp.mean(values * values, axis=-1, keepdims=True) + norm_eps) * gain


def doc_ids(lengths, positions):
    ends = jnp.cumsum(lengths)
    inside = (positions[:, None] >= ends[None, :]).astype(jnp.int32)
    return jnp.where(positions >= 0, jnp.sum(inside, axis=1), -1)


def swiglu(gate_up):
    half = gate_up.shape[1] // 2
    return jax.nn.silu(gate_up[:, :half]) * gate_up[:, half:]


def contract_rows(left, right):
    return tn(left, right)


def contract_cols(left, right):
    return nt(left, right)


def local(
    n_seq, tokens, doc_lengths, norm_gain, w_qkv, w_beta, conv_weight, head_gain, w_out, mlp_gain, w_mlp_in, w_down, grad_out,
):
    rows, model = tokens.shape
    heads = w_beta.shape[1]
    width = head_gain.shape[0]
    taps_n = conv_weight.shape[0]
    qkv = w_qkv.shape[1]
    chunk = min(128, rows)
    n_chunk = rows // chunk
    both = ("dp", "seq")

    w_in = lax.all_gather(
        jnp.concatenate([w_qkv, jnp.pad(w_beta, ((0, 0), (0, 128 - heads)))], axis=1), both, axis=0, tiled=True
    )
    w_o = lax.all_gather(w_out, both, axis=0, tiled=True)
    w_m = lax.all_gather(w_mlp_in, both, axis=0, tiled=True)
    w_d = lax.all_gather(w_down, both, axis=0, tiled=True)

    inputs = tokens.astype(f32)
    norm_one, pull_one = jax.vjp(rms_scale, inputs, norm_gain.astype(f32))
    xn1 = norm_one.astype(bf16)
    projected = nn(xn1, w_in)
    logits = projected[:, qkv : qkv + heads]
    start = lax.axis_index("seq") * rows
    docs_pad = doc_ids(doc_lengths[0], start - taps_n + 1 + jnp.arange(rows + taps_n - 1, dtype=jnp.int32))
    docs = docs_pad[taps_n - 1 :]
    by_chunk = docs.reshape(n_chunk, chunk)
    before = docs_pad[taps_n - 2 : taps_n - 2 + rows].reshape(n_chunk, chunk)[:, :1]
    aux = jnp.stack(
        [(by_chunk == before).reshape(-1), (by_chunk == by_chunk[:, -1:]).reshape(-1)]
        + [docs_pad[taps_n - 1 - b : taps_n - 1 - b + rows] == docs for b in (1, 2, 3)]
        + [docs < -5] * 3,
        axis=1,
    ).astype(f32)
    docs_c, docs_r = docs[:, None], docs[None, :]
    received = from_behind(projected[rows - taps_n + 1 :, :qkv].astype(bf16), "seq", 1).astype(f32)
    halo = jnp.pad(received, ((8 - taps_n + 1, 0), (0, 0)))
    taps = jnp.pad(conv_weight.astype(f32), ((0, 8 - taps_n), (0, 0)))

    def third(block_rows):
        return [pl.BlockSpec((block_rows, width), lambda h, t=t: (0, t * heads + h)) for t in range(3)]

    def per_head(block_rows):
        return pl.BlockSpec((block_rows, width), lambda h: (0, h))

    def whole(shape):
        return pl.BlockSpec(shape, lambda h: (0,) * len(shape))

    state_block = pl.BlockSpec((1, width, width), lambda h: (h, 0, 0))
    params = pltpu.CompilerParams(vmem_limit_bytes=VMEM_LIMIT, dimension_semantics=("arbitrary",))
    cols = heads * width
    token_like = jax.ShapeDtypeStruct((rows, cols), f32)
    chunk_like = jax.ShapeDtypeStruct((rows, heads * chunk), f32)
    state_like = jax.ShapeDtypeStruct((n_chunk * width, cols), f32)
    common_specs = (
        third(rows) + third(8) + third(8)
        + [whole((rows, 8)), whole((rows, 1)), whole((1, rows)), whole((rows, heads))]
    )
    common = (projected,) * 3 + (halo,) * 3 + (taps,) * 3 + (aux, docs_c, docs_r, logits)
    chunk_block = pl.BlockSpec((rows, chunk), lambda h: (0, h))
    cq, ck, cv, w_s, u_s, qt, o0, t_s, p_s, kk_s, dt, ft, seg = pl.pallas_call(
        functools.partial(local_kernel, chunk),
        grid=(heads,),
        in_specs=common_specs,
        out_specs=[per_head(rows)] * 7 + [chunk_block] * 3 + [per_head(n_chunk * width)] * 2
        + [pl.BlockSpec((width, 2 * width), lambda h: (0, h))],
        out_shape=[token_like] * 7 + [chunk_like] * 3 + [state_like] * 2
        + [jax.ShapeDtypeStruct((width, 2 * cols), f32)],
        scratch_shapes=[pltpu.VMEM((rows + 8, width), f32)],
        compiler_params=params,
        name="delta_local",
    )(*common)
    seg = seg.reshape(width, heads, 2, width)
    seg_map, seg_add = (jnp.swapaxes(seg[:, :, i], 0, 1) for i in (0, 1))

    def relay(back, maps, adds, cid):
        return pl.pallas_call(
            functools.partial(relay_kernel, n_seq, back),
            in_specs=[pl.BlockSpec(memory_space=pltpu.VMEM)] * 2,
            out_specs=pl.BlockSpec(memory_space=pltpu.VMEM),
            out_shape=jax.ShapeDtypeStruct((heads, width, width), bf16),
            scratch_shapes=[
                pltpu.VMEM((heads, width, width), bf16),
                pltpu.SemaphoreType.DMA((heads,)),
                pltpu.SemaphoreType.DMA((heads,)),
            ],
            compiler_params=pltpu.CompilerParams(collective_id=cid, has_side_effects=True, vmem_limit_bytes=VMEM_LIMIT),
            name="relay_back" if back else "relay",
        )(maps, adds)

    state_in = relay(False, seg_map, seg_add, 0)
    gain_h = head_gain.astype(f32)[None, :]
    z_s, mixed, head_out = pl.pallas_call(
        functools.partial(output_kernel, chunk),
        grid=(heads,),
        in_specs=[state_block, per_head(n_chunk * width), per_head(n_chunk * width), per_head(rows), per_head(rows), whole((1, width))],
        out_specs=[per_head(n_chunk * width), per_head(rows), per_head(rows)],
        out_shape=[state_like, token_like, jax.ShapeDtypeStruct((rows, cols), bf16)],
        compiler_params=params,
        name="delta_out",
    )(state_in, dt, ft, qt, o0, gain_h)

    hidden_one = inputs + nn(head_out, w_o)
    norm_two, pull_two = jax.vjp(rms_scale, hidden_one, mlp_gain.astype(f32))
    xn2 = norm_two.astype(bf16)
    gate_up = nn(xn2, w_m)
    hidden_f, pull_act = jax.vjp(swiglu, gate_up)
    hidden = hidden_f.astype(bf16)
    out = (hidden_one + nn(hidden, w_d)).astype(bf16)

    grad_in = grad_out.astype(f32)
    d_hidden = contract_cols(grad_out, w_d)
    d_gate_up = pull_act(d_hidden)[0].astype(bf16)
    d_from_two, d_mlp_gain = pull_two(contract_cols(d_gate_up, w_m))
    d_hidden_one = grad_in + d_from_two
    d_att = d_hidden_one.astype(bf16)
    d_head = contract_cols(d_att, w_o)

    do, b_s, seed, d_head_gain = pl.pallas_call(
        functools.partial(seed_kernel, chunk),
        grid=(heads,),
        in_specs=[per_head(rows), per_head(rows), whole((1, width)), per_head(rows), per_head(n_chunk * width)],
        out_specs=[per_head(rows), per_head(n_chunk * width), state_block, whole((8, width))],
        out_shape=[token_like, state_like, jax.ShapeDtypeStruct((heads, width, width), f32), jax.ShapeDtypeStruct((8, width), f32)],
        compiler_params=params,
        name="delta_seed",
    )(d_head, mixed, gain_h, qt, dt)
    grad_end = relay(True, seg_map, seed, 1)
    outs = pl.pallas_call(
        functools.partial(back_kernel, chunk),
        grid=(heads,),
        in_specs=common_specs + [per_head(rows)] * 5 + [chunk_block] * 3
        + [per_head(n_chunk * width), per_head(rows), per_head(n_chunk * width), per_head(n_chunk * width), state_block],
        out_specs=[per_head(rows)] * 3 + [per_head(8)] * 6 + [whole((rows, heads))],
        out_shape=[token_like] * 3 + [jax.ShapeDtypeStruct((8, cols), f32)] * 6 + [jax.ShapeDtypeStruct((rows, heads), f32)],
        scratch_shapes=[pltpu.VMEM((rows + 8, width), f32)] + [pltpu.VMEM((rows + 16, width), f32)] * 3,
        compiler_params=params,
        name="delta_back",
    )(*common, cq, ck, cv, w_s, u_s, t_s, p_s, kk_s, z_s, do, dt, b_s, grad_end)
    d_main = jnp.concatenate(outs[:3], axis=1)
    d_early = jnp.concatenate(outs[3:6], axis=1)
    d_conv = jnp.concatenate(outs[6:9], axis=1)[:taps_n]
    d_logits = outs[9]
    returned = from_behind(d_early[8 - taps_n + 1 :].astype(bf16), "seq", -1).astype(f32)
    d_projected = d_main + jnp.pad(returned, ((rows - taps_n + 1, 0), (0, 0)))
    d_proj_b = jnp.concatenate(
        [d_projected.astype(bf16), jnp.pad(d_logits.astype(bf16), ((0, 0), (0, 128 - heads)))], axis=1
    )
    d_from_one, d_norm_gain = pull_one(contract_cols(d_proj_b, w_in))
    grad_tokens = (d_hidden_one + d_from_one).astype(bf16)

    def scatter(grad):
        return lax.psum_scatter(grad.astype(bf16), both, scatter_dimension=0, tiled=True).astype(f32)

    g_down = scatter(contract_rows(hidden, grad_out))
    g_mlp = scatter(contract_rows(xn2, d_gate_up))
    g_out = scatter(contract_rows(head_out, d_att))
    g_in = scatter(contract_rows(xn1, d_proj_b))
    small = lax.psum((d_norm_gain, d_conv, d_head_gain[0], d_mlp_gain), both)
    return (
        out, grad_tokens, small[0], g_in[:, :qkv], g_in[:, qkv : qkv + heads], small[1], small[2], g_out, small[3], g_mlp, g_down,
    )


def solution(mesh):
    split = P(("dp", "seq"), None)
    placed = (split, P("dp", None), P(), split, split, P(), P(), split, P(), split, split, split)
    return jax.shard_map(
        functools.partial(local, mesh.shape["seq"]),
        mesh=mesh,
        in_specs=placed,
        out_specs=(split, split, P(), split, split, P(), P(), split, P(), split, split),
        check_vma=False,
    )
```

```python
import functools

import jax
import jax.numpy as jnp
from jax import lax
from jax.experimental import pallas as pl
from jax.experimental.pallas import tpu as pltpu
from jax.sharding import PartitionSpec as P

norm_eps = 1e-05
unit_eps = 1e-06
MESH = pl.DeviceIdType.MESH
f32, bf16 = jnp.float32, jnp.bfloat16
HIGH = lax.Precision.HIGH
VMEM_LIMIT = 56 << 20


def nn(a, b, prec=None):
    return lax.dot_general(a, b, (((1,), (0,)), ((), ())), precision=prec, preferred_element_type=f32)


def nt(a, b, prec=None):
    return lax.dot_general(a, b, (((1,), (1,)), ((), ())), precision=prec, preferred_element_type=f32)


def tn(a, b, prec=None):
    return lax.dot_general(a, b, (((0,), (0,)), ((), ())), precision=prec, preferred_element_type=f32)


def unit_lower_inverse(a, row, col):
    size = a.shape[0]
    block = min(8, size)
    eye = (row == col).astype(f32)
    step = jnp.where(row // block == col // block, -a, 0.0)
    inverse = eye + step
    power = block // 2
    while power >= 1:
        if power > 0 and block > 2:
            step = nn(step, step, HIGH)
            inverse = inverse + nn(inverse, step, HIGH)
        power //= 2
        if power < 2:
            break
    while block < size:
        off = jnp.where((row // (2 * block) == col // (2 * block)) & (row // block == col // block + 1), a, 0.0)
        inverse = inverse - nn(inverse, nn(off, inverse, HIGH), HIGH)
        block *= 2
    return inverse


def head_column(matrix, head):
    lane = lax.broadcasted_iota(jnp.int32, matrix.shape, 1)
    return jnp.sum(jnp.where(lane == head, matrix, 0.0), axis=1, keepdims=True)


def masks_of(docs_col, docs_row):
    size = docs_col.shape[0]
    row = lax.broadcasted_iota(jnp.int32, (size, size), 0)
    col = lax.broadcasted_iota(jnp.int32, (size, size), 1)
    same = docs_col == docs_row
    return row, col, same


def local_kernel(
    chunk, pq, pk, pv, hq, hk, hv, tq, tk, tv, aux, docs_c, docs_r, logits,
    cq, ck, cv, w_o, u_o, qt_o, o_o, t_o, p_o, kk_o, dt_o, ft_o, seg_o, pad,
):
    head = pl.program_id(0)
    rows, width = pq.shape
    keeps = (aux[:, 2:3], aux[:, 3:4], aux[:, 4:5])
    acts = []
    for src, halo, taps, dst in ((pq, hq, tq, cq), (pk, hk, tk, ck), (pv, hv, tv, cv)):
        pad[0:8, :] = halo[...]
        pad[8 : 8 + rows, :] = src[...]
        conv = taps[3:4, :] * src[...]
        for back in (1, 2, 3):
            conv = conv + taps[3 - back : 4 - back, :] * (pad[8 - back : 8 - back + rows, :] * keeps[back - 1])
        dst[...] = conv
        acts.append(conv * jax.nn.sigmoid(conv))
    q = acts[0] * (lax.rsqrt(jnp.sum(acts[0] * acts[0], axis=1, keepdims=True) + unit_eps) * width ** (-0.5))
    k = acts[1] * lax.rsqrt(jnp.sum(acts[1] * acts[1], axis=1, keepdims=True) + unit_eps)
    v = acts[2]
    beta = jax.nn.sigmoid(head_column(logits[...], head))
    cont, last = aux[:, 0:1], aux[:, 1:2]
    seg = None
    for c in range(rows // chunk):
        sl = slice(c * chunk, (c + 1) * chunk)
        row, col, same = masks_of(docs_c[sl, :], docs_r[:, sl])
        qc, kc, vc, bc, cc, lc = q[sl], k[sl], v[sl], beta[sl], cont[sl], last[sl]
        kk = nt(kc, kc, HIGH)
        a = jnp.where(same & (row > col), bc * kk, 0.0)
        t = unit_lower_inverse(a, row, col)
        wu = nn(t, jnp.concatenate([(bc * cc) * kc, bc * vc], axis=1), HIGH)
        p = jnp.where(same & (row >= col), nt(qc, kc, HIGH), 0.0)
        pwu = nn(p, wu, HIGH)
        x = tn(lc * kc, wu, HIGH)
        d_row = lax.broadcasted_iota(jnp.int32, (width, width), 0)
        d_col = lax.broadcasted_iota(jnp.int32, (width, width), 1)
        dt = jnp.where(d_row == d_col, cc[chunk - 1 : chunk], 0.0) - x[:, :width]
        ft = x[:, width:]
        w_o[sl, :] = wu[:, :width]
        u_o[sl, :] = wu[:, width:]
        qt_o[sl, :] = cc * qc - pwu[:, :width]
        o_o[sl, :] = pwu[:, width:]
        t_o[sl, :] = t
        p_o[sl, :] = p
        kk_o[sl, :] = kk
        dt_o[c * width : (c + 1) * width, :] = dt
        ft_o[c * width : (c + 1) * width, :] = ft
        if seg is None:
            seg = jnp.concatenate([dt, ft], axis=1)
        else:
            seg = nn(dt, seg, HIGH)
            seg = jnp.concatenate([seg[:, :width], seg[:, width:] + ft], axis=1)
    seg_o[...] = seg


def relay_kernel(n_seq, back, map_ref, add_ref, out_ref, send, ssem, rsem):
    d, s = lax.axis_index("dp"), lax.axis_index("seq")
    heads = map_ref.shape[0]
    if back:
        first, final = s == n_seq - 1, s == 0
        ahead, behind = s - 1, s + 1
    else:
        first, final = s == 0, s == n_seq - 1
        ahead, behind = s + 1, s - 1
    barrier = pltpu.get_barrier_semaphore()

    @pl.when(jnp.logical_not(first))
    def _():
        pl.semaphore_signal(barrier, inc=1, device_id=(d, behind), device_id_type=MESH)

    @pl.when(jnp.logical_not(final))
    def _():
        pl.semaphore_signal(barrier, inc=1, device_id=(d, ahead), device_id_type=MESH)

    pl.semaphore_wait(barrier, jnp.where(first | final, 1, 2))

    def copy_of(h):
        return pltpu.make_async_remote_copy(
            src_ref=send.at[h], dst_ref=out_ref.at[h], send_sem=ssem.at[h], recv_sem=rsem.at[h],
            device_id=(d, ahead), device_id_type=MESH,
        )

    @pl.when(first)
    def _():
        out_ref[...] = jnp.zeros(out_ref.shape, out_ref.dtype)

    for h in range(heads):
        @pl.when(jnp.logical_not(first))
        def _():
            copy_of(h).wait_recv()

        @pl.when(jnp.logical_not(final))
        def _():
            state = out_ref[h].astype(f32)
            mult = tn if back else nn
            send[h] = (mult(map_ref[h], state, HIGH) + add_ref[h]).astype(bf16)
            copy_of(h).start()

    @pl.when(jnp.logical_not(final))
    def _():
        for h in range(heads):
            copy_of(h).wait_send()


def output_kernel(chunk, zin, dt, ft, qt, o0, gain, z_o, o_o, head_o):
    rows, width = qt.shape
    z = zin[0].astype(f32)
    for c in range(rows // chunk):
        sl = slice(c * chunk, (c + 1) * chunk)
        ds = slice(c * width, (c + 1) * width)
        z_o[ds, :] = z
        o = o0[sl, :] + nn(qt[sl, :], z, HIGH)
        o_o[sl, :] = o
        scale = lax.rsqrt(jnp.mean(o * o, axis=1, keepdims=True) + norm_eps)
        head_o[sl, :] = (o * scale * gain[...]).astype(bf16)
        if c + 1 < rows // chunk:
            z = nn(dt[ds, :], z, HIGH) + ft[ds, :]


def seed_kernel(chunk, dh, o, gain, qt, dt, do_o, b_o, seed_o, dgain_o):
    head = pl.program_id(0)
    rows, width = qt.shape
    ov, dhv = o[...], dh[...]
    scale = lax.rsqrt(jnp.mean(ov * ov, axis=1, keepdims=True) + norm_eps)
    n = ov * scale
    dg = jnp.sum(dhv * n, axis=0, keepdims=True)
    dgain_o[...] = jnp.where(head == 0, 0.0, dgain_o[...]) + jnp.broadcast_to(dg, dgain_o.shape)
    y = dhv * gain[...]
    do = (y - n * jnp.mean(y * n, axis=1, keepdims=True)) * scale
    do_o[...] = do
    g = None
    for c in reversed(range(rows // chunk)):
        sl = slice(c * chunk, (c + 1) * chunk)
        ds = slice(c * width, (c + 1) * width)
        b_o[ds, :] = tn(qt[sl, :], do[sl], HIGH)
        g = b_o[ds, :] if g is None else tn(dt[ds, :], g, HIGH) + b_o[ds, :]
    seed_o[0] = g


def back_kernel(
    chunk, pq, pk, pv, hq, hk, hv, tq, tk, tv, aux, docs_c, docs_r, logits,
    cq, ck, cv, w_r, u_r, t_r, p_r, kk_r, z_r, do_r, dt_r, b_r, g_r,
    dpq, dpk, dpv, dhq, dhk, dhv, dtq, dtk, dtv, dlogit_o, pad, mask1, mask2, mask3,
):
    head = pl.program_id(0)
    rows, width = pq.shape
    cont, last = aux[:, 0:1], aux[:, 1:2]
    keeps = (aux[:, 2:3], aux[:, 3:4], aux[:, 4:5])
    scale = width ** (-0.5)
    beta = jax.nn.sigmoid(head_column(logits[...], head))
    sq, sk, sv = (jax.nn.sigmoid(x[...]) for x in (cq, ck, cv))
    aq, ak, v = cq[...] * sq, ck[...] * sk, cv[...] * sv
    iq = lax.rsqrt(jnp.sum(aq * aq, axis=1, keepdims=True) + unit_eps)
    ik = lax.rsqrt(jnp.sum(ak * ak, axis=1, keepdims=True) + unit_eps)
    uq, k = aq * iq, ak * ik
    q = uq * scale
    g = g_r[0].astype(f32)
    dqs, dks, dvs, dbs = [], [], [], []
    for c in reversed(range(rows // chunk)):
        sl = slice(c * chunk, (c + 1) * chunk)
        ds = slice(c * width, (c + 1) * width)
        row, col, same = masks_of(docs_c[sl, :], docs_r[:, sl])
        qc, kc, vc, bc, cc, lc = q[sl], k[sl], v[sl], beta[sl], cont[sl], last[sl]
        z = z_r[ds, :]
        do = do_r[sl, :]
        wkz = nn(jnp.concatenate([w_r[sl, :], kc], axis=0), z)
        u = u_r[sl, :] - wkz[:chunk]
        kz = wkz[chunk:]
        du = tn(p_r[sl, :], do) + nn(lc * kc, g)
        dr = tn(t_r[sl, :], du)
        y = nt(jnp.concatenate([do, dr], axis=0), jnp.concatenate([u, z], axis=0))
        dp = jnp.where(same & (row >= col), y[:chunk, :chunk], 0.0)
        da = jnp.where(same & (row > col), -y[chunk:, :chunk], 0.0)
        bda = bc * da
        pak = nn(jnp.concatenate([dp, bda], axis=0), kc)
        dqs.append(cc * y[:chunk, chunk:] + pak[:chunk])
        dks.append(
            tn(jnp.concatenate([dp, bda], axis=0), jnp.concatenate([qc, kc], axis=0))
            + pak[chunk:] + lc * nt(u, g) - (bc * cc) * y[chunk:, chunk:]
        )
        dvs.append(bc * dr)
        dbs.append(
            jnp.sum(dr * (vc - cc * kz), axis=1, keepdims=True)
            + jnp.sum(da * kk_r[sl, :], axis=1, keepdims=True)
        )
        if c > 0:
            g = tn(dt_r[ds, :], g) + b_r[ds, :]
    dq, dk, dv, db = (jnp.concatenate(x[::-1], axis=0) for x in (dqs, dks, dvs, dbs))
    lane = lax.broadcasted_iota(jnp.int32, dlogit_o.shape, 1)
    dlogit_o[...] = jnp.where(lane == head, db * beta * (1.0 - beta), jnp.where(head == 0, 0.0, dlogit_o[...]))
    du_q = dq * scale
    da_q = (du_q - uq * jnp.sum(uq * du_q, axis=1, keepdims=True)) * iq
    da_k = (dk - k * jnp.sum(k * dk, axis=1, keepdims=True)) * ik
    for dact, sg, c_r, src, halo, taps, dst, dhalo, dtaps in (
        (da_q, sq, cq, pq, hq, tq, dpq, dhq, dtq),
        (da_k, sk, ck, pk, hk, tk, dpk, dhk, dtk),
        (dv, sv, cv, pv, hv, tv, dpv, dhv, dtv),
    ):
        dconv = dact * (sg * (1.0 + c_r[...] * (1.0 - sg)))
        pad[0:8, :] = halo[...]
        pad[8 : 8 + rows, :] = src[...]
        zero = jnp.zeros((8, width), f32)
        total = taps[3:4, :] * dconv
        early = zero
        gtaps = [None] * 4
        gtaps[3] = jnp.sum(dconv * src[...], axis=0, keepdims=True)
        for back, mask in ((1, mask1), (2, mask2), (3, mask3)):
            kept = dconv * keeps[back - 1]
            gtaps[3 - back] = jnp.sum(kept * pad[8 - back : 8 - back + rows, :], axis=0, keepdims=True)
            mask[0:8, :] = zero
            mask[8 : 8 + rows, :] = kept
            mask[8 + rows : 16 + rows, :] = zero
            total = total + taps[3 - back : 4 - back, :] * mask[8 + back : 8 + back + rows, :]
            early = early + taps[3 - back : 4 - back, :] * mask[back : back + 8, :]
        dst[...] = total
        dhalo[...] = early
        dtaps[...] = jnp.concatenate(gtaps + [jnp.zeros((4, width), f32)], axis=0)


def bit_orders(n_dp, n_seq):
    dp_bits = [("dp", i) for i in range(n_dp.bit_length() - 1)]
    seq_bits = [("seq", i) for i in range(n_seq.bit_length() - 1)]
    return (
        seq_bits[:1] + dp_bits + seq_bits[1:],
        seq_bits[:1] + dp_bits[::-1] + seq_bits[1:],
    )


def scatter_kernel(n_dp, n_seq, units, slots, n_left, n_right, n_out, *refs):
    lefts = refs[:n_left]
    rights = refs[n_left : n_left + n_right]
    small_in = refs[n_left + n_right]
    outs = refs[n_left + n_right + 1 : n_left + n_right + 1 + n_out]
    small_out = refs[n_left + n_right + 1 + n_out]
    scratch = list(refs[n_left + n_right + 2 + n_out :])
    orders = bit_orders(n_dp, n_seq)
    steps = len(orders[0])
    pool = [scratch.pop(0) for _ in range(2 * (1 + max(slots)))]
    own = [pool[2 * slots[u] + half] for u in range(len(units)) for half in (0, 1)]
    before = [max([w for w in range(u) if slots[w] == slots[u]], default=None) for u in range(len(units))]
    got = [[scratch.pop(0) for _ in range(steps)] for _ in range(2 * len(units))]
    small_got, ssem, rsem, small_ssem, small_rsem = scratch
    index = {"dp": lax.axis_index("dp"), "seq": lax.axis_index("seq")}

    def bit_of(axis, bit):
        return (index[axis] // 2**bit) % 2

    def partner(axis, bit):
        other = dict(index)
        other[axis] = index[axis] + (1 - 2 * bit_of(axis, bit)) * 2**bit
        return (other["dp"], other["seq"])

    barrier = pltpu.get_barrier_semaphore()
    for axis, bit in orders[0]:
        pl.semaphore_signal(barrier, inc=1, device_id=partner(axis, bit), device_id_type=MESH)
    pl.semaphore_wait(barrier, steps)

    def weights(order):
        return {key: 2 ** (steps - 1 - i) for i, key in enumerate(order)}

    def place(order, axis, value):
        w = weights(order)
        return sum(((value // 2**b) % 2) * w[(a, b)] for a, b in order if a == axis)

    def compute(u):
        kind, li, ri, first, cols, _, _ = units[u]
        left, right = lefts[li], rights[ri]
        block = left.shape[0] // (n_dp * n_seq)
        group = block * n_seq
        for half in (0, 1):
            order, buf = orders[half], own[2 * u + half]
            part = pl.ds(first + half * (cols // 2), cols // 2)

            def rows_of(m, carry):
                base = place(order, "dp", m)
                tile = nn(left[pl.ds(pl.multiple_of(m * group, 16), group), :], right[:, part])
                for j in range(n_seq):
                    piece = tile[j * block : (j + 1) * block]
                    if kind == "stack":
                        piece = jnp.concatenate([piece[:, : cols // 4], piece[:, cols // 4 :]], axis=0)
                    buf[base + place(order, "seq", j)] = piece.astype(bf16)
                return carry

            lax.fori_loop(0, n_dp, rows_of, 0)

    def copy_of(u, half, k):
        src = own[2 * u + half] if k == 0 else got[2 * u + half][k - 1]
        dst = got[2 * u + half][k]
        axis, bit = orders[half][k]
        count = dst.shape[0]
        return pltpu.make_async_remote_copy(
            src_ref=src.at[pl.ds((1 - bit_of(axis, bit)) * count, count)], dst_ref=dst,
            send_sem=ssem.at[u, half, k], recv_sem=rsem.at[u, half, k],
            device_id=partner(axis, bit), device_id_type=MESH,
        )

    def merge(u, half, k):
        src = own[2 * u + half] if k == 0 else got[2 * u + half][k - 1]
        dst = got[2 * u + half][k]
        axis, bit = orders[half][k]
        count = dst.shape[0]
        mine = bit_of(axis, bit) * count
        copy_of(u, half, k).wait_recv()
        if k < steps - 1:
            def add(i, carry):
                dst[i] = (dst[i].astype(f32) + src[mine + i].astype(f32)).astype(bf16)
                return carry

            lax.fori_loop(0, count, add, 0)
            copy_of(u, half, k + 1).start()
        else:
            kind, _, _, first, cols, oi, to = units[u]
            total = dst[0].astype(f32) + src[mine].astype(f32)
            start, wide = to + half * (cols // 2), cols // 2
            if kind == "stack":
                block = total.shape[0] // 2
                outs[oi][:, start : start + wide // 2] = total[:block]
                outs[oi][:, start + wide // 2 : start + wide] = total[block:]
            else:
                outs[oi][:, start : start + wide] = total

    def small_copy(k):
        axis, bit = orders[0][k]
        return pltpu.make_async_remote_copy(
            src_ref=small_in if k == 0 else small_got.at[steps + k - 1], dst_ref=small_got.at[k],
            send_sem=small_ssem.at[k], recv_sem=small_rsem.at[k],
            device_id=partner(axis, bit), device_id_type=MESH,
        )

    def small_step(k):
        small_copy(k).wait_recv()
        mine = small_in[...] if k == 0 else small_got[steps + k - 1]
        if k < steps - 1:
            small_got[steps + k] = small_got[k] + mine
            small_copy(k + 1).start()
        else:
            small_out[...] = small_got[k] + mine

    small_copy(0).start()
    for t in range(len(units) + steps):
        if t < len(units):
            if before[t] is not None:
                for half in (0, 1):
                    copy_of(before[t], half, 0).wait_send()
            compute(t)
            for half in (0, 1):
                copy_of(t, half, 0).start()
        if t < steps:
            small_step(t)
        for k in range(steps):
            u = t - 1 - k
            if 0 <= u < len(units):
                for half in (0, 1):
                    merge(u, half, k)
    for k in range(steps):
        small_copy(k).wait_send()
        for u in range(len(units)):
            if k > 0 or u not in before:
                for half in (0, 1):
                    copy_of(u, half, k).wait_send()


def scatter_grads(mesh_sizes, products, small, cid):
    n_dp, n_seq = mesh_sizes
    n = n_dp * n_seq
    orders = bit_orders(n_dp, n_seq)
    steps = len(orders[0])
    lefts, rights, units, shapes, outs = [], [], [], [], []
    for oi, (left, right, kind, cols) in enumerate(products):
        block = left.shape[0] // n
        lefts.append(left)
        rights.append(right)
        outs.append(jax.ShapeDtypeStruct((block, right.shape[1]), f32))
        for first in range(0, right.shape[1], cols):
            wide = min(cols, right.shape[1] - first)
            units.append((kind, oi, oi, first, wide, oi, first))
            shapes.append((2 * block, wide // 4) if kind == "stack" else (block, wide // 2))
    pool, slots = [], []
    for u, shape in enumerate(shapes):
        alike = [i for i, kept in enumerate(pool) if kept == shape]
        if len(alike) < 3:
            slots.append(len(pool))
            pool.append(shape)
        else:
            used = [max(w for w in range(u) if slots[w] == i) for i in alike]
            slots.append(alike[used.index(min(used))])
    own = [pltpu.VMEM((n,) + s, bf16) for s in pool for _ in (0, 1)]
    got = [pltpu.VMEM((n >> (k + 1),) + s, bf16) for s in shapes for _ in (0, 1) for k in range(steps)]
    vmem = pl.BlockSpec(memory_space=pltpu.VMEM)
    sems = pltpu.SemaphoreType.DMA((len(units), 2, steps))
    results = pl.pallas_call(
        functools.partial(scatter_kernel, n_dp, n_seq, units, slots, len(lefts), len(rights), len(outs)),
        in_specs=[vmem] * (len(lefts) + len(rights) + 1),
        out_specs=[vmem] * (len(outs) + 1),
        out_shape=outs + [jax.ShapeDtypeStruct(small.shape, f32)],
        scratch_shapes=own + got + [
            pltpu.VMEM((2 * steps,) + small.shape, f32), sems, sems,
            pltpu.SemaphoreType.DMA((steps,)), pltpu.SemaphoreType.DMA((steps,)),
        ],
        compiler_params=pltpu.CompilerParams(collective_id=cid, has_side_effects=True, vmem_limit_bytes=63 << 20),
        name="scatter_grads",
    )(*lefts, *rights, small)
    return results[:-1], results[-1]


def from_behind(value, axis, steps):
    count = lax.axis_size(axis)
    first, last = (max(0, -steps), min(count, count - steps))
    return lax.ppermute(value, axis, [(source, source + steps) for source in range(first, last)])


def rms_scale(values, gain):
    return values * lax.rsqrt(jnp.mean(values * values, axis=-1, keepdims=True) + norm_eps) * gain


def doc_ids(lengths, positions):
    ends = jnp.cumsum(lengths)
    inside = (positions[:, None] >= ends[None, :]).astype(jnp.int32)
    return jnp.where(positions >= 0, jnp.sum(inside, axis=1), -1)


def swiglu(gate_up):
    half = gate_up.shape[1] // 2
    return jax.nn.silu(gate_up[:, :half]) * gate_up[:, half:]


def contract_rows(left, right):
    return tn(left, right)


def contract_cols(left, right):
    return nt(left, right)


def local(
    n_dp, n_seq, tokens, doc_lengths, norm_gain, w_qkv, w_beta, conv_weight, head_gain, w_out, mlp_gain, w_mlp_in, w_down, grad_out,
):
    rows, model = tokens.shape
    heads = w_beta.shape[1]
    width = head_gain.shape[0]
    taps_n = conv_weight.shape[0]
    qkv = w_qkv.shape[1]
    chunk = min(128, rows)
    n_chunk = rows // chunk
    both = ("dp", "seq")

    w_in = lax.all_gather(
        jnp.concatenate([w_qkv, jnp.pad(w_beta, ((0, 0), (0, 128 - heads)))], axis=1), both, axis=0, tiled=True
    )
    w_o = lax.all_gather(w_out, both, axis=0, tiled=True)
    w_m = lax.all_gather(w_mlp_in, both, axis=0, tiled=True)
    w_d = lax.all_gather(w_down, both, axis=0, tiled=True)

    inputs = tokens.astype(f32)
    norm_one, pull_one = jax.vjp(rms_scale, inputs, norm_gain.astype(f32))
    xn1 = norm_one.astype(bf16)
    projected = nn(xn1, w_in)
    logits = projected[:, qkv : qkv + heads]
    start = lax.axis_index("seq") * rows
    docs_pad = doc_ids(doc_lengths[0], start - taps_n + 1 + jnp.arange(rows + taps_n - 1, dtype=jnp.int32))
    docs = docs_pad[taps_n - 1 :]
    by_chunk = docs.reshape(n_chunk, chunk)
    before = docs_pad[taps_n - 2 : taps_n - 2 + rows].reshape(n_chunk, chunk)[:, :1]
    aux = jnp.stack(
        [(by_chunk == before).reshape(-1), (by_chunk == by_chunk[:, -1:]).reshape(-1)]
        + [docs_pad[taps_n - 1 - b : taps_n - 1 - b + rows] == docs for b in (1, 2, 3)]
        + [docs < -5] * 3,
        axis=1,
    ).astype(f32)
    docs_c, docs_r = docs[:, None], docs[None, :]
    received = from_behind(projected[rows - taps_n + 1 :, :qkv].astype(bf16), "seq", 1).astype(f32)
    halo = jnp.pad(received, ((8 - taps_n + 1, 0), (0, 0)))
    taps = jnp.pad(conv_weight.astype(f32), ((0, 8 - taps_n), (0, 0)))

    def third(block_rows):
        return [pl.BlockSpec((block_rows, width), lambda h, t=t: (0, t * heads + h)) for t in range(3)]

    def per_head(block_rows):
        return pl.BlockSpec((block_rows, width), lambda h: (0, h))

    def whole(shape):
        return pl.BlockSpec(shape, lambda h: (0,) * len(shape))

    state_block = pl.BlockSpec((1, width, width), lambda h: (h, 0, 0))
    params = pltpu.CompilerParams(vmem_limit_bytes=VMEM_LIMIT, dimension_semantics=("arbitrary",))
    cols = heads * width
    token_like = jax.ShapeDtypeStruct((rows, cols), f32)
    chunk_like = jax.ShapeDtypeStruct((rows, heads * chunk), f32)
    state_like = jax.ShapeDtypeStruct((n_chunk * width, cols), f32)
    common_specs = (
        third(rows) + third(8) + third(8)
        + [whole((rows, 8)), whole((rows, 1)), whole((1, rows)), whole((rows, heads))]
    )
    common = (projected,) * 3 + (halo,) * 3 + (taps,) * 3 + (aux, docs_c, docs_r, logits)
    chunk_block = pl.BlockSpec((rows, chunk), lambda h: (0, h))
    cq, ck, cv, w_s, u_s, qt, o0, t_s, p_s, kk_s, dt, ft, seg = pl.pallas_call(
        functools.partial(local_kernel, chunk),
        grid=(heads,),
        in_specs=common_specs,
        out_specs=[per_head(rows)] * 7 + [chunk_block] * 3 + [per_head(n_chunk * width)] * 2
        + [pl.BlockSpec((width, 2 * width), lambda h: (0, h))],
        out_shape=[token_like] * 7 + [chunk_like] * 3 + [state_like] * 2
        + [jax.ShapeDtypeStruct((width, 2 * cols), f32)],
        scratch_shapes=[pltpu.VMEM((rows + 8, width), f32)],
        compiler_params=params,
        name="delta_local",
    )(*common)
    seg = seg.reshape(width, heads, 2, width)
    seg_map, seg_add = (jnp.swapaxes(seg[:, :, i], 0, 1) for i in (0, 1))

    def relay(back, maps, adds, cid):
        return pl.pallas_call(
            functools.partial(relay_kernel, n_seq, back),
            in_specs=[pl.BlockSpec(memory_space=pltpu.VMEM)] * 2,
            out_specs=pl.BlockSpec(memory_space=pltpu.VMEM),
            out_shape=jax.ShapeDtypeStruct((heads, width, width), bf16),
            scratch_shapes=[
                pltpu.VMEM((heads, width, width), bf16),
                pltpu.SemaphoreType.DMA((heads,)),
                pltpu.SemaphoreType.DMA((heads,)),
            ],
            compiler_params=pltpu.CompilerParams(collective_id=cid, has_side_effects=True, vmem_limit_bytes=VMEM_LIMIT),
            name="relay_back" if back else "relay",
        )(maps, adds)

    state_in = relay(False, seg_map, seg_add, 0)
    gain_h = head_gain.astype(f32)[None, :]
    z_s, mixed, head_out = pl.pallas_call(
        functools.partial(output_kernel, chunk),
        grid=(heads,),
        in_specs=[state_block, per_head(n_chunk * width), per_head(n_chunk * width), per_head(rows), per_head(rows), whole((1, width))],
        out_specs=[per_head(n_chunk * width), per_head(rows), per_head(rows)],
        out_shape=[state_like, token_like, jax.ShapeDtypeStruct((rows, cols), bf16)],
        compiler_params=params,
        name="delta_out",
    )(state_in, dt, ft, qt, o0, gain_h)

    hidden_one = inputs + nn(head_out, w_o)
    norm_two, pull_two = jax.vjp(rms_scale, hidden_one, mlp_gain.astype(f32))
    xn2 = norm_two.astype(bf16)
    gate_up = nn(xn2, w_m)
    hidden_f, pull_act = jax.vjp(swiglu, gate_up)
    hidden = hidden_f.astype(bf16)
    out = (hidden_one + nn(hidden, w_d)).astype(bf16)

    grad_in = grad_out.astype(f32)
    d_hidden = contract_cols(grad_out, w_d)
    d_gate_up = pull_act(d_hidden)[0].astype(bf16)
    d_from_two, d_mlp_gain = pull_two(contract_cols(d_gate_up, w_m))
    d_hidden_one = grad_in + d_from_two
    d_att = d_hidden_one.astype(bf16)
    d_head = contract_cols(d_att, w_o)

    do, b_s, seed, d_head_gain = pl.pallas_call(
        functools.partial(seed_kernel, chunk),
        grid=(heads,),
        in_specs=[per_head(rows), per_head(rows), whole((1, width)), per_head(rows), per_head(n_chunk * width)],
        out_specs=[per_head(rows), per_head(n_chunk * width), state_block, whole((8, width))],
        out_shape=[token_like, state_like, jax.ShapeDtypeStruct((heads, width, width), f32), jax.ShapeDtypeStruct((8, width), f32)],
        compiler_params=params,
        name="delta_seed",
    )(d_head, mixed, gain_h, qt, dt)
    grad_end = relay(True, seg_map, seed, 1)
    outs = pl.pallas_call(
        functools.partial(back_kernel, chunk),
        grid=(heads,),
        in_specs=common_specs + [per_head(rows)] * 5 + [chunk_block] * 3
        + [per_head(n_chunk * width), per_head(rows), per_head(n_chunk * width), per_head(n_chunk * width), state_block],
        out_specs=[per_head(rows)] * 3 + [per_head(8)] * 6 + [whole((rows, heads))],
        out_shape=[token_like] * 3 + [jax.ShapeDtypeStruct((8, cols), f32)] * 6 + [jax.ShapeDtypeStruct((rows, heads), f32)],
        scratch_shapes=[pltpu.VMEM((rows + 8, width), f32)] + [pltpu.VMEM((rows + 16, width), f32)] * 3,
        compiler_params=params,
        name="delta_back",
    )(*common, cq, ck, cv, w_s, u_s, t_s, p_s, kk_s, z_s, do, dt, b_s, grad_end)
    d_main = jnp.concatenate(outs[:3], axis=1)
    d_early = jnp.concatenate(outs[3:6], axis=1)
    d_conv = jnp.concatenate(outs[6:9], axis=1)[:taps_n]
    d_logits = outs[9]
    returned = from_behind(d_early[8 - taps_n + 1 :].astype(bf16), "seq", -1).astype(f32)
    d_projected = d_main + jnp.pad(returned, ((rows - taps_n + 1, 0), (0, 0)))
    d_proj_b = jnp.concatenate(
        [d_projected.astype(bf16), jnp.pad(d_logits.astype(bf16), ((0, 0), (0, 128 - heads)))], axis=1
    )
    d_from_one, d_norm_gain = pull_one(contract_cols(d_proj_b, w_in))
    grad_tokens = (d_hidden_one + d_from_one).astype(bf16)

    d_beta_rows = tn(d_logits.astype(bf16), xn1)
    parts = [
        (hidden, grad_out, "stack", 512),
        (xn2, d_gate_up, "plain", 1024),
        (head_out, d_att, "plain", 1024),
        (xn1, d_proj_b[:, :qkv], "plain", 1024),
    ]
    if (model // (n_dp * n_seq)) % 16 == 0:
        small = jnp.concatenate(
            [
                d_beta_rows,
                d_norm_gain[None],
                d_mlp_gain[None],
                d_conv.reshape(-1, model),
                jnp.pad(d_head_gain[0:1], ((0, 0), (0, model - width))),
            ],
            axis=0,
        )
        count = small.shape[0]
        small = jnp.pad(small, ((0, -count % 8), (0, 0)))
        (g_down, g_mlp, g_out, g_in), small = scatter_grads(
            (n_dp, n_seq), [(left.T, right, kind, cols) for left, right, kind, cols in parts], small, 2
        )
        mine = (lax.axis_index("dp") * n_seq + lax.axis_index("seq")) * (model // (n_dp * n_seq))
        g_beta = lax.dynamic_slice(small[:heads], (0, mine), (heads, model // (n_dp * n_seq))).T
        s_norm, s_mlp = small[heads], small[heads + 1]
        s_conv = small[heads + 2 : count - 1].reshape(taps_n, qkv)
        s_head = small[count - 1, :width]
    else:
        g_down, g_mlp, g_out, g_in, g_beta = (
            lax.psum_scatter(grad, both, scatter_dimension=0, tiled=True)
            for grad in [contract_rows(left, right) for left, right, _, _ in parts] + [d_beta_rows.T]
        )
        s_norm, s_conv, s_head, s_mlp = lax.psum((d_norm_gain, d_conv, d_head_gain[0], d_mlp_gain), both)
    return (out, grad_tokens, s_norm, g_in, g_beta, s_conv, s_head, g_out, s_mlp, g_mlp, g_down)


def solution(mesh):
    split = P(("dp", "seq"), None)
    placed = (split, P("dp", None), P(), split, split, P(), P(), split, P(), split, split, split)
    return jax.shard_map(
        functools.partial(local, mesh.shape["dp"], mesh.shape["seq"]),
        mesh=mesh,
        in_specs=placed,
        out_specs=(split, split, P(), split, split, P(), P(), split, P(), split, split),
        check_vma=False,
    )
```

```python
import functools

import jax
import jax.numpy as jnp
from jax import lax
from jax.experimental import pallas as pl
from jax.experimental.pallas import tpu as pltpu
from jax.sharding import PartitionSpec as P

norm_eps = 1e-05
unit_eps = 1e-06
MESH = pl.DeviceIdType.MESH
f32, bf16 = jnp.float32, jnp.bfloat16
HIGH = lax.Precision.HIGH
VMEM_LIMIT = 56 << 20


def nn(a, b, prec=None):
    return lax.dot_general(a, b, (((1,), (0,)), ((), ())), precision=prec, preferred_element_type=f32)


def nt(a, b, prec=None):
    return lax.dot_general(a, b, (((1,), (1,)), ((), ())), precision=prec, preferred_element_type=f32)


def tn(a, b, prec=None):
    return lax.dot_general(a, b, (((0,), (0,)), ((), ())), precision=prec, preferred_element_type=f32)


def unit_lower_inverses(mats, row, col):
    size = mats[0].shape[0]
    block = min(8, size)
    eye = (row == col).astype(f32)
    near = row // block == col // block
    powers = [jnp.where(near, -a, 0.0) for a in mats]
    inverses = [eye + p for p in powers]
    reach = 2
    while reach < block:
        powers = [nn(p, p, HIGH) for p in powers]
        inverses = [t + nn(t, p, HIGH) for t, p in zip(inverses, powers)]
        reach *= 2
    while block < size:
        pairs = size // (2 * block)

        def lower(m, block=block, pairs=pairs):
            return jnp.concatenate([m[(2 * i + 1) * block : (2 * i + 2) * block] for i in range(pairs)], axis=0)

        def spread(m, fill, block=block, pairs=pairs):
            return jnp.concatenate(
                [x for i in range(pairs) for x in (fill[2 * i * block : (2 * i + 1) * block], m[i * block : (i + 1) * block])],
                axis=0,
            )

        off = (row // (2 * block) == col // (2 * block)) & (row // block == col // block + 1)
        lows = [lower(jnp.where(off, a, 0.0)) for a in mats]
        crossed = [nn(x, t, HIGH) for x, t in zip(lows, inverses)]
        zero = jnp.zeros((size, size), f32)
        below = [lower(t) for t in inverses]
        fixed = [x - nn(x, spread(y, zero), HIGH) for x, y in zip(below, crossed)]
        inverses = [spread(x, t) for x, t in zip(fixed, inverses)]
        block *= 2
    return inverses


def head_column(matrix, head):
    lane = lax.broadcasted_iota(jnp.int32, matrix.shape, 1)
    return jnp.sum(jnp.where(lane == head, matrix, 0.0), axis=1, keepdims=True)


def masks_of(docs_col, docs_row):
    size = docs_col.shape[0]
    row = lax.broadcasted_iota(jnp.int32, (size, size), 0)
    col = lax.broadcasted_iota(jnp.int32, (size, size), 1)
    same = docs_col == docs_row
    return row, col, same


def local_kernel(
    sizes, chunk, gathers, *refs,
):
    local_body(sizes, chunk, gathers, refs[:gathers], *refs[gathers:])


def local_body(
    sizes, chunk, gathers, shards, pq, pk, pv, hq, hk, hv, tq, tk, tv, aux, docs_c, docs_r, logits,
    cq, ck, cv, w_o, u_o, qt_o, o_o, t_o, p_o, kk_o, dt_o, ft_o, map_o, turned_o, add_o, *rest,
):
    head = pl.program_id(0)
    pad = rest[gathers]
    gather_beside(sizes, head, shards, rest[:gathers], rest[gathers + 1 :])
    rows, width = pq.shape
    keeps = (aux[:, 2:3], aux[:, 3:4], aux[:, 4:5])
    acts = []
    for src, halo, taps, dst in ((pq, hq, tq, cq), (pk, hk, tk, ck), (pv, hv, tv, cv)):
        pad[0:8, :] = halo[...]
        pad[8 : 8 + rows, :] = src[...]
        conv = taps[3:4, :] * src[...]
        for back in (1, 2, 3):
            conv = conv + taps[3 - back : 4 - back, :] * (pad[8 - back : 8 - back + rows, :] * keeps[back - 1])
        dst[...] = conv
        acts.append(conv * jax.nn.sigmoid(conv))
    q = acts[0] * (lax.rsqrt(jnp.sum(acts[0] * acts[0], axis=1, keepdims=True) + unit_eps) * width ** (-0.5))
    k = acts[1] * lax.rsqrt(jnp.sum(acts[1] * acts[1], axis=1, keepdims=True) + unit_eps)
    v = acts[2]
    beta = jax.nn.sigmoid(head_column(logits[...], head))
    cont, last = aux[:, 0:1], aux[:, 1:2]
    n_chunk = rows // chunk
    cuts = [slice(c * chunk, (c + 1) * chunk) for c in range(n_chunk)]
    row = lax.broadcasted_iota(jnp.int32, (chunk, chunk), 0)
    col = lax.broadcasted_iota(jnp.int32, (chunk, chunk), 1)
    same = [docs_c[sl, :] == docs_r[:, sl] for sl in cuts]
    kks = [nt(k[sl], k[sl], HIGH) for sl in cuts]
    ps = [jnp.where(m & (row >= col), nt(q[sl], k[sl], HIGH), 0.0) for m, sl in zip(same, cuts)]
    ts = unit_lower_inverses(
        [jnp.where(m & (row > col), beta[sl] * kk, 0.0) for m, sl, kk in zip(same, cuts, kks)], row, col
    )
    rhs = [jnp.concatenate([(beta[sl] * cont[sl]) * k[sl], beta[sl] * v[sl]], axis=1) for sl in cuts]
    wus = [nn(t, r, HIGH) for t, r in zip(ts, rhs)]
    pwus = [nn(p, wu, HIGH) for p, wu in zip(ps, wus)]
    xs = [tn(last[sl] * k[sl], wu, HIGH) for sl, wu in zip(cuts, wus)]
    d_row = lax.broadcasted_iota(jnp.int32, (width, width), 0)
    d_col = lax.broadcasted_iota(jnp.int32, (width, width), 1)
    seg = None
    for c, sl in enumerate(cuts):
        cc = cont[sl]
        dt = jnp.where(d_row == d_col, cc[chunk - 1 : chunk], 0.0) - xs[c][:, :width]
        ft = xs[c][:, width:]
        w_o[sl, :] = wus[c][:, :width]
        u_o[sl, :] = wus[c][:, width:]
        qt_o[sl, :] = cc * q[sl] - pwus[c][:, :width]
        o_o[sl, :] = pwus[c][:, width:]
        t_o[sl, :] = ts[c]
        p_o[sl, :] = ps[c]
        kk_o[sl, :] = kks[c]
        dt_o[c * width : (c + 1) * width, :] = dt
        ft_o[c * width : (c + 1) * width, :] = ft
        if seg is None:
            seg = jnp.concatenate([dt, ft], axis=1)
        else:
            seg = nn(dt, seg, HIGH)
            seg = jnp.concatenate([seg[:, :width], seg[:, width:] + ft], axis=1)
    map_o[0] = seg[:, :width]
    turned_o[0] = seg[:, :width].T
    add_o[0] = seg[:, width:]


def relay_kernel(n_seq, back, map_ref, add_ref, out_ref, send, ssem, rsem):
    d, s = lax.axis_index("dp"), lax.axis_index("seq")
    heads = map_ref.shape[0]
    if back:
        first, final = s == n_seq - 1, s == 0
        ahead, behind = s - 1, s + 1
    else:
        first, final = s == 0, s == n_seq - 1
        ahead, behind = s + 1, s - 1
    barrier = pltpu.get_barrier_semaphore()

    @pl.when(jnp.logical_not(first))
    def _():
        pl.semaphore_signal(barrier, inc=1, device_id=(d, behind), device_id_type=MESH)

    @pl.when(jnp.logical_not(final))
    def _():
        pl.semaphore_signal(barrier, inc=1, device_id=(d, ahead), device_id_type=MESH)

    pl.semaphore_wait(barrier, jnp.where(first | final, 1, 2))

    def copy_of(h):
        return pltpu.make_async_remote_copy(
            src_ref=send.at[h], dst_ref=out_ref.at[h], send_sem=ssem.at[h], recv_sem=rsem.at[h],
            device_id=(d, ahead), device_id_type=MESH,
        )

    @pl.when(first)
    def _():
        def start(h, carry):
            out_ref[h] = jnp.zeros(out_ref.shape[1:], out_ref.dtype)
            send[h] = add_ref[h].astype(bf16)
            copy_of(h).start()
            return carry

        lax.fori_loop(0, heads, start, 0)

    @pl.when(jnp.logical_not(first))
    def _():
        def step(h, carry):
            copy_of(h).wait_recv()

            @pl.when(jnp.logical_not(final))
            def _():
                send[h] = (nn(map_ref[h], out_ref[h].astype(f32), HIGH) + add_ref[h]).astype(bf16)
                copy_of(h).start()

            return carry

        lax.fori_loop(0, heads, step, 0)

    @pl.when(jnp.logical_not(final))
    def _():
        def sent(h, carry):
            copy_of(h).wait_send()
            return carry

        lax.fori_loop(0, heads, sent, 0)


def output_kernel(chunk, zin, dt, ft, qt, o0, gain, z_o, o_o, head_o):
    rows, width = qt.shape
    z = zin[0].astype(f32)
    for c in range(rows // chunk):
        sl = slice(c * chunk, (c + 1) * chunk)
        ds = slice(c * width, (c + 1) * width)
        z_o[ds, :] = z
        o = o0[sl, :] + nn(qt[sl, :], z, HIGH)
        o_o[sl, :] = o
        scale = lax.rsqrt(jnp.mean(o * o, axis=1, keepdims=True) + norm_eps)
        head_o[sl, :] = (o * scale * gain[...]).astype(bf16)
        if c + 1 < rows // chunk:
            z = nn(dt[ds, :], z, HIGH) + ft[ds, :]


def seed_kernel(chunk, dh, o, gain, qt, dt, do_o, b_o, seed_o, dgain_o):
    head = pl.program_id(0)
    rows, width = qt.shape
    ov, dhv = o[...], dh[...]
    scale = lax.rsqrt(jnp.mean(ov * ov, axis=1, keepdims=True) + norm_eps)
    n = ov * scale
    dg = jnp.sum(dhv * n, axis=0, keepdims=True)
    dgain_o[...] = jnp.where(head == 0, 0.0, dgain_o[...]) + jnp.broadcast_to(dg, dgain_o.shape)
    y = dhv * gain[...]
    do = (y - n * jnp.mean(y * n, axis=1, keepdims=True)) * scale
    do_o[...] = do
    g = None
    for c in reversed(range(rows // chunk)):
        sl = slice(c * chunk, (c + 1) * chunk)
        ds = slice(c * width, (c + 1) * width)
        b_o[ds, :] = tn(qt[sl, :], do[sl], HIGH)
        g = b_o[ds, :] if g is None else tn(dt[ds, :], g, HIGH) + b_o[ds, :]
    seed_o[0] = g


def back_kernel(
    chunk, pq, pk, pv, hq, hk, hv, tq, tk, tv, aux, docs_c, docs_r, logits,
    cq, ck, cv, w_r, u_r, t_r, p_r, kk_r, z_r, do_r, dt_r, b_r, g_r,
    dpq, dpk, dpv, dhq, dhk, dhv, dtq, dtk, dtv, dlogit_o, pad, mask1, mask2, mask3,
):
    head = pl.program_id(0)
    rows, width = pq.shape
    cont, last = aux[:, 0:1], aux[:, 1:2]
    keeps = (aux[:, 2:3], aux[:, 3:4], aux[:, 4:5])
    scale = width ** (-0.5)
    beta = jax.nn.sigmoid(head_column(logits[...], head))
    sq, sk, sv = (jax.nn.sigmoid(x[...]) for x in (cq, ck, cv))
    aq, ak, v = cq[...] * sq, ck[...] * sk, cv[...] * sv
    iq = lax.rsqrt(jnp.sum(aq * aq, axis=1, keepdims=True) + unit_eps)
    ik = lax.rsqrt(jnp.sum(ak * ak, axis=1, keepdims=True) + unit_eps)
    uq, k = aq * iq, ak * ik
    q = uq * scale
    g = g_r[0].astype(f32)
    dqs, dks, dvs, dbs = [], [], [], []
    for c in reversed(range(rows // chunk)):
        sl = slice(c * chunk, (c + 1) * chunk)
        ds = slice(c * width, (c + 1) * width)
        row, col, same = masks_of(docs_c[sl, :], docs_r[:, sl])
        qc, kc, vc, bc, cc, lc = q[sl], k[sl], v[sl], beta[sl], cont[sl], last[sl]
        z = z_r[ds, :]
        do = do_r[sl, :]
        wkz = nn(jnp.concatenate([w_r[sl, :], kc], axis=0), z)
        u = u_r[sl, :] - wkz[:chunk]
        kz = wkz[chunk:]
        du = tn(p_r[sl, :], do) + nn(lc * kc, g)
        dr = tn(t_r[sl, :], du)
        y = nt(jnp.concatenate([do, dr], axis=0), jnp.concatenate([u, z], axis=0))
        dp = jnp.where(same & (row >= col), y[:chunk, :chunk], 0.0)
        da = jnp.where(same & (row > col), -y[chunk:, :chunk], 0.0)
        bda = bc * da
        pak = nn(jnp.concatenate([dp, bda], axis=0), kc)
        dqs.append(cc * y[:chunk, chunk:] + pak[:chunk])
        dks.append(
            tn(jnp.concatenate([dp, bda], axis=0), jnp.concatenate([qc, kc], axis=0))
            + pak[chunk:] + lc * nt(u, g) - (bc * cc) * y[chunk:, chunk:]
        )
        dvs.append(bc * dr)
        dbs.append(
            jnp.sum(dr * (vc - cc * kz), axis=1, keepdims=True)
            + jnp.sum(da * kk_r[sl, :], axis=1, keepdims=True)
        )
        if c > 0:
            g = tn(dt_r[ds, :], g) + b_r[ds, :]
    dq, dk, dv, db = (jnp.concatenate(x[::-1], axis=0) for x in (dqs, dks, dvs, dbs))
    lane = lax.broadcasted_iota(jnp.int32, dlogit_o.shape, 1)
    dlogit_o[...] = jnp.where(lane == head, db * beta * (1.0 - beta), jnp.where(head == 0, 0.0, dlogit_o[...]))
    du_q = dq * scale
    da_q = (du_q - uq * jnp.sum(uq * du_q, axis=1, keepdims=True)) * iq
    da_k = (dk - k * jnp.sum(k * dk, axis=1, keepdims=True)) * ik
    for dact, sg, c_r, src, halo, taps, dst, dhalo, dtaps in (
        (da_q, sq, cq, pq, hq, tq, dpq, dhq, dtq),
        (da_k, sk, ck, pk, hk, tk, dpk, dhk, dtk),
        (dv, sv, cv, pv, hv, tv, dpv, dhv, dtv),
    ):
        dconv = dact * (sg * (1.0 + c_r[...] * (1.0 - sg)))
        pad[0:8, :] = halo[...]
        pad[8 : 8 + rows, :] = src[...]
        zero = jnp.zeros((8, width), f32)
        total = taps[3:4, :] * dconv
        early = zero
        gtaps = [None] * 4
        gtaps[3] = jnp.sum(dconv * src[...], axis=0, keepdims=True)
        for back, mask in ((1, mask1), (2, mask2), (3, mask3)):
            kept = dconv * keeps[back - 1]
            gtaps[3 - back] = jnp.sum(kept * pad[8 - back : 8 - back + rows, :], axis=0, keepdims=True)
            mask[0:8, :] = zero
            mask[8 : 8 + rows, :] = kept
            mask[8 + rows : 16 + rows, :] = zero
            total = total + taps[3 - back : 4 - back, :] * mask[8 + back : 8 + back + rows, :]
            early = early + taps[3 - back : 4 - back, :] * mask[back : back + 8, :]
        dst[...] = total
        dhalo[...] = early
        dtaps[...] = jnp.concatenate(gtaps + [jnp.zeros((4, width), f32)], axis=0)


def bit_orders(n_dp, n_seq):
    dp_bits = [("dp", i) for i in range(n_dp.bit_length() - 1)]
    seq_bits = [("seq", i) for i in range(n_seq.bit_length() - 1)]
    return (
        seq_bits[:1] + dp_bits + seq_bits[1:],
        seq_bits[:1] + dp_bits[::-1] + seq_bits[1:],
        seq_bits + dp_bits,
        seq_bits + dp_bits[::-1],
    )


def scatter_kernel(n_dp, n_seq, units, slots, n_left, n_right, n_out, *refs):
    lefts = refs[:n_left]
    rights = refs[n_left : n_left + n_right]
    small_in = refs[n_left + n_right]
    outs = refs[n_left + n_right + 1 : n_left + n_right + 1 + n_out]
    small_out = refs[n_left + n_right + 1 + n_out]
    scratch = list(refs[n_left + n_right + 2 + n_out :])
    orders = bit_orders(n_dp, n_seq)
    steps = len(orders[0])
    pool = [scratch.pop(0) for _ in range(2 * (1 + max(slots)))]
    own = [pool[2 * slots[u] + half] for u in range(len(units)) for half in (0, 1)]
    before = [max([w for w in range(u) if slots[w] == slots[u]], default=None) for u in range(len(units))]
    got = [[scratch.pop(0) for _ in range(steps)] for _ in range(2 * len(units))]
    small_got, ssem, rsem, small_ssem, small_rsem = scratch
    index = {"dp": lax.axis_index("dp"), "seq": lax.axis_index("seq")}

    def bit_of(axis, bit):
        return (index[axis] // 2**bit) % 2

    def partner(axis, bit):
        other = dict(index)
        other[axis] = index[axis] + (1 - 2 * bit_of(axis, bit)) * 2**bit
        return (other["dp"], other["seq"])

    barrier = pltpu.get_barrier_semaphore()
    for axis, bit in orders[0]:
        pl.semaphore_signal(barrier, inc=1, device_id=partner(axis, bit), device_id_type=MESH)
    pl.semaphore_wait(barrier, steps)

    def weights(order):
        return {key: 2 ** (steps - 1 - i) for i, key in enumerate(order)}

    def place(order, axis, value):
        w = weights(order)
        return sum(((value // 2**b) % 2) * w[(a, b)] for a, b in order if a == axis)

    def compute(u):
        kind, li, ri, first, cols, _, _, first_order = units[u]
        left, right = lefts[li], rights[ri]
        block = left.shape[0] // (n_dp * n_seq)
        group = block * n_seq
        for half in (0, 1):
            order, buf = orders[first_order + half], own[2 * u + half]
            part = pl.ds(first + half * (cols // 2), cols // 2)

            def rows_of(m, carry):
                base = place(order, "dp", m)
                tile = nn(left[pl.ds(pl.multiple_of(m * group, 16), group), :], right[:, part])
                for j in range(n_seq):
                    piece = tile[j * block : (j + 1) * block]
                    if kind == "stack":
                        piece = jnp.concatenate([piece[:, : cols // 4], piece[:, cols // 4 :]], axis=0)
                    buf[base + place(order, "seq", j)] = piece.astype(bf16)
                return carry

            lax.fori_loop(0, n_dp, rows_of, 0)

    def copy_of(u, half, k):
        src = own[2 * u + half] if k == 0 else got[2 * u + half][k - 1]
        dst = got[2 * u + half][k]
        axis, bit = orders[units[u][7] + half][k]
        count = dst.shape[0]
        return pltpu.make_async_remote_copy(
            src_ref=src.at[pl.ds((1 - bit_of(axis, bit)) * count, count)], dst_ref=dst,
            send_sem=ssem.at[u, half, k], recv_sem=rsem.at[u, half, k],
            device_id=partner(axis, bit), device_id_type=MESH,
        )

    def merge(u, half, k):
        src = own[2 * u + half] if k == 0 else got[2 * u + half][k - 1]
        dst = got[2 * u + half][k]
        axis, bit = orders[units[u][7] + half][k]
        count = dst.shape[0]
        mine = bit_of(axis, bit) * count
        copy_of(u, half, k).wait_recv()
        if k < steps - 1:
            def add(i, carry):
                dst[i] = (dst[i].astype(f32) + src[mine + i].astype(f32)).astype(bf16)
                return carry

            lax.fori_loop(0, count, add, 0)
            copy_of(u, half, k + 1).start()
        else:
            kind, _, _, first, cols, oi, to, _ = units[u]
            total = dst[0].astype(f32) + src[mine].astype(f32)
            start, wide = to + half * (cols // 2), cols // 2
            if kind == "stack":
                block = total.shape[0] // 2
                outs[oi][:, start : start + wide // 2] = total[:block]
                outs[oi][:, start + wide // 2 : start + wide] = total[block:]
            else:
                outs[oi][:, start : start + wide] = total

    def small_copy(k):
        axis, bit = orders[0][k]
        return pltpu.make_async_remote_copy(
            src_ref=small_in if k == 0 else small_got.at[steps + k - 1], dst_ref=small_got.at[k],
            send_sem=small_ssem.at[k], recv_sem=small_rsem.at[k],
            device_id=partner(axis, bit), device_id_type=MESH,
        )

    def small_step(k):
        small_copy(k).wait_recv()
        mine = small_in[...] if k == 0 else small_got[steps + k - 1]
        if k < steps - 1:
            small_got[steps + k] = small_got[k] + mine
            small_copy(k + 1).start()
        else:
            small_out[...] = small_got[k] + mine

    small_copy(0).start()
    for t in range(len(units) + steps):
        if t < len(units):
            if before[t] is not None:
                for half in (0, 1):
                    copy_of(before[t], half, 0).wait_send()
            compute(t)
            for half in (0, 1):
                copy_of(t, half, 0).start()
        if t < steps:
            small_step(t)
        for k in range(steps):
            u = t - 1 - k
            if 0 <= u < len(units):
                for half in (0, 1):
                    merge(u, half, k)
    for k in range(steps):
        small_copy(k).wait_send()
        for u in range(len(units)):
            if k > 0 or u not in before:
                for half in (0, 1):
                    copy_of(u, half, k).wait_send()


def scatter_grads(mesh_sizes, products, small, cid):
    n_dp, n_seq = mesh_sizes
    n = n_dp * n_seq
    orders = bit_orders(n_dp, n_seq)
    steps = len(orders[0])
    lefts, rights, units, shapes, outs = [], [], [], [], []
    for oi, (left, right, kind, cols) in enumerate(products):
        block = left.shape[0] // n
        lefts.append(left)
        rights.append(right)
        outs.append(jax.ShapeDtypeStruct((block, right.shape[1]), f32))
        first = 0
        for wide, first_order in cols:
            units.append((kind, oi, oi, first, wide, oi, first, first_order))
            first += wide
            shapes.append((2 * block, wide // 4) if kind == "stack" else (block, wide // 2))
    pool, slots = [], []
    for u, shape in enumerate(shapes):
        alike = [i for i, kept in enumerate(pool) if kept == shape]
        if len(alike) < 3:
            slots.append(len(pool))
            pool.append(shape)
        else:
            used = [max(w for w in range(u) if slots[w] == i) for i in alike]
            slots.append(alike[used.index(min(used))])
    own = [pltpu.VMEM((n,) + s, bf16) for s in pool for _ in (0, 1)]
    got = [pltpu.VMEM((n >> (k + 1),) + s, bf16) for s in shapes for _ in (0, 1) for k in range(steps)]
    vmem = pl.BlockSpec(memory_space=pltpu.VMEM)
    sems = pltpu.SemaphoreType.DMA((len(units), 2, steps))
    results = pl.pallas_call(
        functools.partial(scatter_kernel, n_dp, n_seq, units, slots, len(lefts), len(rights), len(outs)),
        in_specs=[vmem] * (len(lefts) + len(rights) + 1),
        out_specs=[vmem] * (len(outs) + 1),
        out_shape=outs + [jax.ShapeDtypeStruct(small.shape, f32)],
        scratch_shapes=own + got + [
            pltpu.VMEM((2 * steps,) + small.shape, f32), sems, sems,
            pltpu.SemaphoreType.DMA((steps,)), pltpu.SemaphoreType.DMA((steps,)),
        ],
        compiler_params=pltpu.CompilerParams(collective_id=cid, has_side_effects=True, vmem_limit_bytes=63 << 20),
        name="scatter_grads",
    )(*lefts, *rights, small)
    return results[:-1], results[-1]


def gather_steps(sizes, shard, whole, own_sem, ssem, rsem):
    n_dp, n_seq = sizes
    index = {"dp": lax.axis_index("dp"), "seq": lax.axis_index("seq")}
    orders = [order[::-1] for order in bit_orders(n_dp, n_seq)[:2]]
    steps = len(orders[0])
    by_rows = shard.shape[0] % 32 == 0
    extent = shard.shape[0 if by_rows else 1] // 2

    def flipped(keys):
        other = dict(index)
        for axis, bit in keys:
            other[axis] = other[axis] + (1 - 2 * ((index[axis] // 2**bit) % 2)) * 2**bit
        return (other["dp"], other["seq"])

    def half_of(ref, half):
        part = pl.ds(half * extent, extent)
        return ref.at[part] if by_rows else ref.at[:, part]

    def copy_of(half, path, k):
        order = orders[half]
        dp, seq = flipped([order[i] for i in path])
        dst = half_of(whole.at[dp * n_seq + seq], half)
        code = sum(2**i for i in path) + 2**k
        return pltpu.make_async_remote_copy(
            src_ref=dst if path else half_of(shard, half), dst_ref=dst,
            send_sem=ssem.at[half, code], recv_sem=rsem.at[half, code],
            device_id=flipped([order[k]]), device_id_type=MESH,
        )

    paths = sorted(
        (tuple(i for i in range(steps) if code >> i & 1) for code in range(2**steps)), key=lambda p: (len(p), p)
    )
    keep = pltpu.make_async_copy(shard, whole.at[index["dp"] * n_seq + index["seq"]], own_sem)

    def greet():
        barrier = pltpu.get_barrier_semaphore()
        for key in orders[0]:
            pl.semaphore_signal(barrier, inc=1, device_id=flipped([key]), device_id_type=MESH)
        pl.semaphore_wait(barrier, steps)

    def level(hops):
        if hops == 0:
            keep.start()
        for path in paths:
            if len(path) == hops:
                for half in (0, 1):
                    if path:
                        copy_of(half, path[:-1], path[-1]).wait_recv()
                    for k in range((path[-1] if path else -1) + 1, steps):
                        copy_of(half, path, k).start()

    def finish():
        for path in paths:
            if path:
                for half in (0, 1):
                    copy_of(half, path[:-1], path[-1]).wait_send()
        keep.wait()

    return steps, greet, level, finish


def gather_kernel(sizes, shard, whole, *sems):
    steps, greet, level, finish = gather_steps(sizes, shard, whole, *sems)
    greet()
    for hops in range(steps + 1):
        level(hops)
    finish()


def gather_beside(sizes, turn, shards, wholes, sems):
    plans = [
        gather_steps(sizes, shard, whole, *sems[3 * i : 3 * i + 3])
        for i, (shard, whole) in enumerate(zip(shards, wholes))
    ]
    if not plans:
        return
    steps = plans[0][0]
    for hops in range(steps + 1):
        @pl.when(turn == hops)
        def _(hops=hops):
            if hops == 0:
                plans[0][1]()
            for plan in plans:
                plan[2](hops)

    @pl.when(turn == steps + 1)
    def _():
        for plan in plans:
            plan[3]()


def gather_sems(sizes):
    sems = pltpu.SemaphoreType.DMA((2, sizes[0] * sizes[1]))
    return [pltpu.SemaphoreType.DMA, sems, sems]


def whole_like(sizes, shard):
    return jax.ShapeDtypeStruct((sizes[0] * sizes[1],) + shard.shape, shard.dtype)


def flat_rows(whole):
    return whole.reshape((whole.shape[0] * whole.shape[1],) + whole.shape[2:])


def gather_rows(sizes, shard, cid):
    anywhere = pl.BlockSpec(memory_space=pl.ANY)
    whole = pl.pallas_call(
        functools.partial(gather_kernel, sizes),
        in_specs=[anywhere],
        out_specs=anywhere,
        out_shape=whole_like(sizes, shard),
        scratch_shapes=gather_sems(sizes),
        compiler_params=pltpu.CompilerParams(collective_id=cid, has_side_effects=True),
        name="gather_rows",
    )(shard)
    return flat_rows(whole)


def from_behind(value, axis, steps):
    count = lax.axis_size(axis)
    first, last = (max(0, -steps), min(count, count - steps))
    return lax.ppermute(value, axis, [(source, source + steps) for source in range(first, last)])


def rms_scale(values, gain):
    return values * lax.rsqrt(jnp.mean(values * values, axis=-1, keepdims=True) + norm_eps) * gain


def doc_ids(lengths, positions):
    ends = jnp.cumsum(lengths)
    inside = (positions[:, None] >= ends[None, :]).astype(jnp.int32)
    return jnp.where(positions >= 0, jnp.sum(inside, axis=1), -1)


def swiglu(gate_up):
    half = gate_up.shape[1] // 2
    return jax.nn.silu(gate_up[:, :half]) * gate_up[:, half:]


def contract_rows(left, right):
    return tn(left, right)


def contract_cols(left, right):
    return nt(left, right)


def local(
    n_dp, n_seq, tokens, doc_lengths, norm_gain, w_qkv, w_beta, conv_weight, head_gain, w_out, mlp_gain, w_mlp_in, w_down, grad_out,
):
    rows, model = tokens.shape
    heads = w_beta.shape[1]
    width = head_gain.shape[0]
    taps_n = conv_weight.shape[0]
    qkv = w_qkv.shape[1]
    chunk = min(128, rows)
    n_chunk = rows // chunk
    both = ("dp", "seq")

    sizes = (n_dp, n_seq)
    own_kernels = (model // (n_dp * n_seq)) % 32 == 0 and heads > (n_dp * n_seq).bit_length()
    w_m = lax.all_gather(w_mlp_in, both, axis=0, tiled=True)
    w_in = jnp.concatenate([w_qkv, jnp.pad(w_beta, ((0, 0), (0, 128 - heads)))], axis=1)
    if own_kernels:
        beside = [w_out, w_down]
        w_in = gather_rows(sizes, w_in, 3)
    else:
        beside = []
        w_in, w_o, w_d = (lax.all_gather(w, both, axis=0, tiled=True) for w in (w_in, w_out, w_down))

    inputs = tokens.astype(f32)
    norm_one, pull_one = jax.vjp(rms_scale, inputs, norm_gain.astype(f32))
    xn1 = norm_one.astype(bf16)
    projected = nn(xn1, w_in)
    logits = projected[:, qkv : qkv + heads]
    start = lax.axis_index("seq") * rows
    docs_pad = doc_ids(doc_lengths[0], start - taps_n + 1 + jnp.arange(rows + taps_n - 1, dtype=jnp.int32))
    docs = docs_pad[taps_n - 1 :]
    by_chunk = docs.reshape(n_chunk, chunk)
    before = docs_pad[taps_n - 2 : taps_n - 2 + rows].reshape(n_chunk, chunk)[:, :1]
    aux = jnp.stack(
        [(by_chunk == before).reshape(-1), (by_chunk == by_chunk[:, -1:]).reshape(-1)]
        + [docs_pad[taps_n - 1 - b : taps_n - 1 - b + rows] == docs for b in (1, 2, 3)]
        + [docs < -5] * 3,
        axis=1,
    ).astype(f32)
    docs_c, docs_r = docs[:, None], docs[None, :]
    received = from_behind(projected[rows - taps_n + 1 :, :qkv].astype(bf16), "seq", 1).astype(f32)
    halo = jnp.pad(received, ((8 - taps_n + 1, 0), (0, 0)))
    taps = jnp.pad(conv_weight.astype(f32), ((0, 8 - taps_n), (0, 0)))

    def third(block_rows):
        return [pl.BlockSpec((block_rows, width), lambda h, t=t: (0, t * heads + h)) for t in range(3)]

    def per_head(block_rows):
        return pl.BlockSpec((block_rows, width), lambda h: (0, h))

    def whole(shape):
        return pl.BlockSpec(shape, lambda h: (0,) * len(shape))

    state_block = pl.BlockSpec((1, width, width), lambda h: (h, 0, 0))
    params = pltpu.CompilerParams(vmem_limit_bytes=VMEM_LIMIT, dimension_semantics=("arbitrary",))
    cols = heads * width
    token_like = jax.ShapeDtypeStruct((rows, cols), f32)
    chunk_like = jax.ShapeDtypeStruct((rows, heads * chunk), f32)
    state_like = jax.ShapeDtypeStruct((n_chunk * width, cols), f32)
    common_specs = (
        third(rows) + third(8) + third(8)
        + [whole((rows, 8)), whole((rows, 1)), whole((1, rows)), whole((rows, heads))]
    )
    common = (projected,) * 3 + (halo,) * 3 + (taps,) * 3 + (aux, docs_c, docs_r, logits)
    chunk_block = pl.BlockSpec((rows, chunk), lambda h: (0, h))
    anywhere = pl.BlockSpec(memory_space=pl.ANY)
    maps_like = jax.ShapeDtypeStruct((heads, width, width), f32)
    cq, ck, cv, w_s, u_s, qt, o0, t_s, p_s, kk_s, dt, ft, seg_map, seg_turned, seg_add, *wholes = pl.pallas_call(
        functools.partial(local_kernel, sizes, chunk, len(beside)),
        grid=(heads,),
        in_specs=[anywhere] * len(beside) + common_specs,
        out_specs=[per_head(rows)] * 7 + [chunk_block] * 3 + [per_head(n_chunk * width)] * 2 + [state_block] * 3
        + [anywhere] * len(beside),
        out_shape=[token_like] * 7 + [chunk_like] * 3 + [state_like] * 2 + [maps_like] * 3
        + [whole_like(sizes, w) for w in beside],
        scratch_shapes=[pltpu.VMEM((rows + 8, width), f32)] + [sem for _ in beside for sem in gather_sems(sizes)],
        compiler_params=pltpu.CompilerParams(
            vmem_limit_bytes=VMEM_LIMIT, dimension_semantics=("arbitrary",),
            **(dict(collective_id=4, has_side_effects=True) if beside else {}),
        ),
        name="delta_local",
    )(*beside, *common)
    if beside:
        w_o, w_d = (flat_rows(w) for w in wholes)

    def relay(back, maps, adds, cid):
        return pl.pallas_call(
            functools.partial(relay_kernel, n_seq, back),
            in_specs=[pl.BlockSpec(memory_space=pltpu.VMEM)] * 2,
            out_specs=pl.BlockSpec(memory_space=pltpu.VMEM),
            out_shape=jax.ShapeDtypeStruct((heads, width, width), bf16),
            scratch_shapes=[
                pltpu.VMEM((heads, width, width), bf16),
                pltpu.SemaphoreType.DMA((heads,)),
                pltpu.SemaphoreType.DMA((heads,)),
            ],
            compiler_params=pltpu.CompilerParams(collective_id=cid, has_side_effects=True, vmem_limit_bytes=VMEM_LIMIT),
            name="relay_back" if back else "relay",
        )(maps, adds)

    state_in = relay(False, seg_map, seg_add, 0)
    gain_h = head_gain.astype(f32)[None, :]
    z_s, mixed, head_out = pl.pallas_call(
        functools.partial(output_kernel, chunk),
        grid=(heads,),
        in_specs=[state_block, per_head(n_chunk * width), per_head(n_chunk * width), per_head(rows), per_head(rows), whole((1, width))],
        out_specs=[per_head(n_chunk * width), per_head(rows), per_head(rows)],
        out_shape=[state_like, token_like, jax.ShapeDtypeStruct((rows, cols), bf16)],
        compiler_params=params,
        name="delta_out",
    )(state_in, dt, ft, qt, o0, gain_h)

    hidden_one = inputs + nn(head_out, w_o)
    norm_two, pull_two = jax.vjp(rms_scale, hidden_one, mlp_gain.astype(f32))
    xn2 = norm_two.astype(bf16)
    gate_up = nn(xn2, w_m)
    hidden_f, pull_act = jax.vjp(swiglu, gate_up)
    hidden = hidden_f.astype(bf16)
    out = (hidden_one + nn(hidden, w_d)).astype(bf16)

    grad_in = grad_out.astype(f32)
    d_hidden = contract_cols(grad_out, w_d)
    d_gate_up = pull_act(d_hidden)[0].astype(bf16)
    d_from_two, d_mlp_gain = pull_two(contract_cols(d_gate_up, w_m))
    d_hidden_one = grad_in + d_from_two
    d_att = d_hidden_one.astype(bf16)
    d_head = contract_cols(d_att, w_o)

    do, b_s, seed, d_head_gain = pl.pallas_call(
        functools.partial(seed_kernel, chunk),
        grid=(heads,),
        in_specs=[per_head(rows), per_head(rows), whole((1, width)), per_head(rows), per_head(n_chunk * width)],
        out_specs=[per_head(rows), per_head(n_chunk * width), state_block, whole((8, width))],
        out_shape=[token_like, state_like, jax.ShapeDtypeStruct((heads, width, width), f32), jax.ShapeDtypeStruct((8, width), f32)],
        compiler_params=params,
        name="delta_seed",
    )(d_head, mixed, gain_h, qt, dt)
    grad_end = relay(True, seg_turned, seed, 1)
    outs = pl.pallas_call(
        functools.partial(back_kernel, chunk),
        grid=(heads,),
        in_specs=common_specs + [per_head(rows)] * 5 + [chunk_block] * 3
        + [per_head(n_chunk * width), per_head(rows), per_head(n_chunk * width), per_head(n_chunk * width), state_block],
        out_specs=[per_head(rows)] * 3 + [per_head(8)] * 6 + [whole((rows, heads))],
        out_shape=[token_like] * 3 + [jax.ShapeDtypeStruct((8, cols), f32)] * 6 + [jax.ShapeDtypeStruct((rows, heads), f32)],
        scratch_shapes=[pltpu.VMEM((rows + 8, width), f32)] + [pltpu.VMEM((rows + 16, width), f32)] * 3,
        compiler_params=params,
        name="delta_back",
    )(*common, cq, ck, cv, w_s, u_s, t_s, p_s, kk_s, z_s, do, dt, b_s, grad_end)
    d_main = jnp.concatenate(outs[:3], axis=1)
    d_early = jnp.concatenate(outs[3:6], axis=1)
    d_conv = jnp.concatenate(outs[6:9], axis=1)[:taps_n]
    d_logits = outs[9]
    returned = from_behind(d_early[8 - taps_n + 1 :].astype(bf16), "seq", -1).astype(f32)
    d_projected = d_main + jnp.pad(returned, ((rows - taps_n + 1, 0), (0, 0)))
    d_proj_b = jnp.concatenate(
        [d_projected.astype(bf16), jnp.pad(d_logits.astype(bf16), ((0, 0), (0, 128 - heads)))], axis=1
    )
    d_from_one, d_norm_gain = pull_one(contract_cols(d_proj_b, w_in))
    grad_tokens = (d_hidden_one + d_from_one).astype(bf16)

    d_beta_rows = tn(d_logits.astype(bf16), xn1)
    parts = [
        (hidden, grad_out, "stack", [(512, 0)] * 2),
        (xn2, d_gate_up, "plain", [(512, 2), (1024, 0)] * 3 + [(512, 2), (512, 0)]),
        (head_out, d_att, "plain", [(1024, 0)]),
        (xn1, d_proj_b[:, :qkv], "plain", [(512, 2), (1024, 0), (1024, 0), (512, 0)]),
    ]
    if own_kernels:
        small = jnp.concatenate(
            [
                d_beta_rows,
                d_norm_gain[None],
                d_mlp_gain[None],
                d_conv.reshape(-1, model),
                jnp.pad(d_head_gain[0:1], ((0, 0), (0, model - width))),
            ],
            axis=0,
        )
        count = small.shape[0]
        small = jnp.pad(small, ((0, -count % 8), (0, 0)))
        (g_down, g_mlp, g_out, g_in), small = scatter_grads(
            (n_dp, n_seq), [(left.T, right, kind, cols) for left, right, kind, cols in parts], small, 2
        )
        mine = (lax.axis_index("dp") * n_seq + lax.axis_index("seq")) * (model // (n_dp * n_seq))
        g_beta = lax.dynamic_slice(small[:heads], (0, mine), (heads, model // (n_dp * n_seq))).T
        s_norm, s_mlp = small[heads], small[heads + 1]
        s_conv = small[heads + 2 : count - 1].reshape(taps_n, qkv)
        s_head = small[count - 1, :width]
    else:
        g_down, g_mlp, g_out, g_in, g_beta = (
            lax.psum_scatter(grad, both, scatter_dimension=0, tiled=True)
            for grad in [contract_rows(left, right) for left, right, _, _ in parts] + [d_beta_rows.T]
        )
        s_norm, s_conv, s_head, s_mlp = lax.psum((d_norm_gain, d_conv, d_head_gain[0], d_mlp_gain), both)
    return (out, grad_tokens, s_norm, g_in, g_beta, s_conv, s_head, g_out, s_mlp, g_mlp, g_down)


def solution(mesh):
    split = P(("dp", "seq"), None)
    placed = (split, P("dp", None), P(), split, split, P(), P(), split, P(), split, split, split)
    return jax.shard_map(
        functools.partial(local, mesh.shape["dp"], mesh.shape["seq"]),
        mesh=mesh,
        in_specs=placed,
        out_specs=(split, split, P(), split, split, P(), P(), split, P(), split, split),
        check_vma=False,
    )
```

```python
import functools

import jax
import jax.numpy as jnp
from jax import lax
from jax.experimental import pallas as pl
from jax.experimental.pallas import tpu as pltpu
from jax.sharding import PartitionSpec as P

norm_eps = 1e-05
unit_eps = 1e-06
MESH = pl.DeviceIdType.MESH
f32, bf16 = jnp.float32, jnp.bfloat16
HIGH = lax.Precision.HIGH
VMEM_LIMIT = 56 << 20
RINGED = 1
B_COLS = [(1024, 0), (1024, 0), (512, 2), (1024, 0), (512, 2), (1024, 0), (512, 0)]
B_ORDER = [2, 3, 4, 0, 5, 6, 1, 7, 9, 8]
TOKEN_TURN = 1
F_COLS = [[(1024, 0)], [(512, 2), (512, 0)], [(512, 0), (512, 0)]]


def nn(a, b, prec=None):
    return lax.dot_general(a, b, (((1,), (0,)), ((), ())), precision=prec, preferred_element_type=f32)


def nt(a, b, prec=None):
    return lax.dot_general(a, b, (((1,), (1,)), ((), ())), precision=prec, preferred_element_type=f32)


def tn(a, b, prec=None):
    return lax.dot_general(a, b, (((0,), (0,)), ((), ())), precision=prec, preferred_element_type=f32)


def unit_lower_inverses(mats, row, col):
    size = mats[0].shape[0]
    block = min(8, size)
    eye = (row == col).astype(f32)
    near = row // block == col // block
    powers = [jnp.where(near, -a, 0.0) for a in mats]
    inverses = [eye + p for p in powers]
    reach = 2
    while reach < block:
        powers = [nn(p, p, HIGH) for p in powers]
        inverses = [t + nn(t, p, HIGH) for t, p in zip(inverses, powers)]
        reach *= 2
    while block < size:
        pairs = size // (2 * block)

        def lower(m, block=block, pairs=pairs):
            return jnp.concatenate([m[(2 * i + 1) * block : (2 * i + 2) * block] for i in range(pairs)], axis=0)

        def spread(m, fill, block=block, pairs=pairs):
            return jnp.concatenate(
                [x for i in range(pairs) for x in (fill[2 * i * block : (2 * i + 1) * block], m[i * block : (i + 1) * block])],
                axis=0,
            )

        off = (row // (2 * block) == col // (2 * block)) & (row // block == col // block + 1)
        lows = [lower(jnp.where(off, a, 0.0)) for a in mats]
        crossed = [nn(x, t, HIGH) for x, t in zip(lows, inverses)]
        zero = jnp.zeros((size, size), f32)
        below = [lower(t) for t in inverses]
        fixed = [x - nn(x, spread(y, zero), HIGH) for x, y in zip(below, crossed)]
        inverses = [spread(x, t) for x, t in zip(fixed, inverses)]
        block *= 2
    return inverses


def head_column(matrix, head):
    lane = lax.broadcasted_iota(jnp.int32, matrix.shape, 1)
    return jnp.sum(jnp.where(lane == head, matrix, 0.0), axis=1, keepdims=True)


def masks_of(docs_col, docs_row):
    size = docs_col.shape[0]
    row = lax.broadcasted_iota(jnp.int32, (size, size), 0)
    col = lax.broadcasted_iota(jnp.int32, (size, size), 1)
    same = docs_col == docs_row
    return row, col, same


def local_kernel(
    sizes, chunk, gathers, *refs,
):
    local_body(sizes, chunk, gathers, refs[:gathers], *refs[gathers:])


def local_body(
    sizes, chunk, gathers, shards, pq, pk, pv, hq, hk, hv, tq, tk, tv, aux, docs_c, docs_r, logits,
    cq, ck, cv, w_o, u_o, qt_o, o_o, t_o, p_o, kk_o, dt_o, ft_o, map_o, turned_o, add_o, *rest,
):
    head = pl.program_id(0)
    pad = rest[gathers]
    turns = (0, 1, 5)
    gather_beside(sizes, head, shards, rest[:gathers], rest[gathers + 1 :], turns)
    rows, width = pq.shape
    keeps = (aux[:, 2:3], aux[:, 3:4], aux[:, 4:5])
    acts = []
    for src, halo, taps, dst in ((pq, hq, tq, cq), (pk, hk, tk, ck), (pv, hv, tv, cv)):
        pad[0:8, :] = halo[...]
        pad[8 : 8 + rows, :] = src[...]
        conv = taps[3:4, :] * src[...]
        for back in (1, 2, 3):
            conv = conv + taps[3 - back : 4 - back, :] * (pad[8 - back : 8 - back + rows, :] * keeps[back - 1])
        dst[...] = conv
        acts.append(conv * jax.nn.sigmoid(conv))
    q = acts[0] * (lax.rsqrt(jnp.sum(acts[0] * acts[0], axis=1, keepdims=True) + unit_eps) * width ** (-0.5))
    k = acts[1] * lax.rsqrt(jnp.sum(acts[1] * acts[1], axis=1, keepdims=True) + unit_eps)
    v = acts[2]
    beta = jax.nn.sigmoid(head_column(logits[...], head))
    cont, last = aux[:, 0:1], aux[:, 1:2]
    n_chunk = rows // chunk
    cuts = [slice(c * chunk, (c + 1) * chunk) for c in range(n_chunk)]
    row = lax.broadcasted_iota(jnp.int32, (chunk, chunk), 0)
    col = lax.broadcasted_iota(jnp.int32, (chunk, chunk), 1)
    same = [docs_c[sl, :] == docs_r[:, sl] for sl in cuts]
    kks = [nt(k[sl], k[sl], HIGH) for sl in cuts]
    ps = [jnp.where(m & (row >= col), nt(q[sl], k[sl], HIGH), 0.0) for m, sl in zip(same, cuts)]
    ts = unit_lower_inverses(
        [jnp.where(m & (row > col), beta[sl] * kk, 0.0) for m, sl, kk in zip(same, cuts, kks)], row, col
    )
    rhs = [jnp.concatenate([(beta[sl] * cont[sl]) * k[sl], beta[sl] * v[sl]], axis=1) for sl in cuts]
    wus = [nn(t, r, HIGH) for t, r in zip(ts, rhs)]
    pwus = [nn(p, wu, HIGH) for p, wu in zip(ps, wus)]
    xs = [tn(last[sl] * k[sl], wu, HIGH) for sl, wu in zip(cuts, wus)]
    d_row = lax.broadcasted_iota(jnp.int32, (width, width), 0)
    d_col = lax.broadcasted_iota(jnp.int32, (width, width), 1)
    seg = None
    for c, sl in enumerate(cuts):
        cc = cont[sl]
        dt = jnp.where(d_row == d_col, cc[chunk - 1 : chunk], 0.0) - xs[c][:, :width]
        ft = xs[c][:, width:]
        w_o[sl, :] = wus[c][:, :width].astype(bf16)
        u_o[sl, :] = wus[c][:, width:]
        qt_o[sl, :] = cc * q[sl] - pwus[c][:, :width]
        o_o[sl, :] = pwus[c][:, width:]
        t_o[sl, :] = ts[c].astype(bf16)
        p_o[sl, :] = ps[c].astype(bf16)
        kk_o[sl, :] = kks[c]
        dt_o[c * width : (c + 1) * width, :] = dt
        ft_o[c * width : (c + 1) * width, :] = ft
        if seg is None:
            seg = jnp.concatenate([dt, ft], axis=1)
        else:
            seg = nn(dt, seg, HIGH)
            seg = jnp.concatenate([seg[:, :width], seg[:, width:] + ft], axis=1)
    map_o[0] = seg[:, :width]
    turned_o[0] = seg[:, :width].T
    add_o[0] = seg[:, width:]
    gather_rest(sizes, head, shards, rest[:gathers], rest[gathers + 1 :], len(turns), pl.num_programs(0) - 1)


def relay_ends(n_seq, back):
    s = lax.axis_index("seq")
    if back:
        return s == n_seq - 1, s == 0, s - 1, s + 1
    return s == 0, s == n_seq - 1, s + 1, s - 1


def relay_greet(n_seq, back):
    d = lax.axis_index("dp")
    first, final, ahead, behind = relay_ends(n_seq, back)
    barrier = pltpu.get_barrier_semaphore()

    @pl.when(jnp.logical_not(first))
    def _():
        pl.semaphore_signal(barrier, inc=1, device_id=(d, behind), device_id_type=MESH)

    @pl.when(jnp.logical_not(final))
    def _():
        pl.semaphore_signal(barrier, inc=1, device_id=(d, ahead), device_id_type=MESH)

    return jnp.where(first | final, 1, 2)


def relay_kernel(n_seq, back, *refs):
    pl.semaphore_wait(pltpu.get_barrier_semaphore(), relay_greet(n_seq, back))
    relay_body(n_seq, back, *refs)


def relay_body(n_seq, back, map_ref, add_ref, out_ref, send, ssem, rsem):
    d = lax.axis_index("dp")
    heads = map_ref.shape[0]
    first, final, ahead, behind = relay_ends(n_seq, back)

    def copy_of(h):
        return pltpu.make_async_remote_copy(
            src_ref=send.at[h], dst_ref=out_ref.at[h], send_sem=ssem.at[h], recv_sem=rsem.at[h],
            device_id=(d, ahead), device_id_type=MESH,
        )

    @pl.when(first)
    def _():
        out_ref[...] = jnp.zeros(out_ref.shape, out_ref.dtype)
        for h in range(heads):
            send[h] = add_ref[h].astype(bf16)
            copy_of(h).start()

    @pl.when(jnp.logical_not(first))
    def _():
        for h in range(heads):
            copy_of(h).wait_recv()
            send[h] = (nn(map_ref[h], out_ref[h].astype(f32), HIGH) + add_ref[h]).astype(bf16)

            @pl.when(jnp.logical_not(final))
            def _():
                copy_of(h).start()

    @pl.when(jnp.logical_not(final))
    def _():
        for h in range(heads):
            copy_of(h).wait_send()


def output_kernel(chunk, zin, dt, ft, qt, o0, gain, z_o, o_o, head_o):
    rows, width = qt.shape
    z = zin[0].astype(f32)
    for c in range(rows // chunk):
        sl = slice(c * chunk, (c + 1) * chunk)
        ds = slice(c * width, (c + 1) * width)
        z_o[ds, :] = z.astype(bf16)
        o = o0[sl, :] + nn(qt[sl, :], z, HIGH)
        o_o[sl, :] = o
        scale = lax.rsqrt(jnp.mean(o * o, axis=1, keepdims=True) + norm_eps)
        head_o[sl, :] = (o * scale * gain[...]).astype(bf16)
        if c + 1 < rows // chunk:
            z = nn(dt[ds, :], z, HIGH) + ft[ds, :]


def seed_kernel(chunk, *refs):
    seed_body(chunk, pl.program_id(0), *refs)


def seed_body(chunk, head, dh, o, gain, qt, dt, do_o, b_o, seed_o, dgain_o):
    rows, width = qt.shape
    ov, dhv = o[...], dh[...]
    scale = lax.rsqrt(jnp.mean(ov * ov, axis=1, keepdims=True) + norm_eps)
    n = ov * scale
    dg = jnp.sum(dhv * n, axis=0, keepdims=True)
    dgain_o[...] = jnp.where(head == 0, 0.0, dgain_o[...]) + jnp.broadcast_to(dg, dgain_o.shape)
    y = dhv * gain[...]
    do = (y - n * jnp.mean(y * n, axis=1, keepdims=True)) * scale
    do_o[...] = do.astype(do_o.dtype)
    g = None
    for c in reversed(range(rows // chunk)):
        sl = slice(c * chunk, (c + 1) * chunk)
        ds = slice(c * width, (c + 1) * width)
        b_o[ds, :] = tn(qt[sl, :], do[sl], HIGH)
        g = b_o[ds, :] if g is None else tn(dt[ds, :], g, HIGH) + b_o[ds, :]
    seed_o[0] = g


def back_kernel(chunk, *refs):
    back_body(chunk, pl.program_id(0), *refs)


def back_body(
    chunk, head, pq, pk, pv, hq, hk, hv, tq, tk, tv, aux, docs_c, docs_r, logits,
    cq, ck, cv, w_r, u_r, t_r, p_r, kk_r, z_r, do_r, dt_r, b_r, g_r,
    dpq, dpk, dpv, dhq, dhk, dhv, dtq, dtk, dtv, dlogit_o, pad, mask1, mask2, mask3, tails=(None,) * 3,
):
    rows, width = pq.shape
    cont, last = aux[:, 0:1], aux[:, 1:2]
    keeps = (aux[:, 2:3], aux[:, 3:4], aux[:, 4:5])
    scale = width ** (-0.5)
    beta = jax.nn.sigmoid(head_column(logits[...], head))
    sq, sk, sv = (jax.nn.sigmoid(x[...]) for x in (cq, ck, cv))
    aq, ak, v = cq[...] * sq, ck[...] * sk, cv[...] * sv
    iq = lax.rsqrt(jnp.sum(aq * aq, axis=1, keepdims=True) + unit_eps)
    ik = lax.rsqrt(jnp.sum(ak * ak, axis=1, keepdims=True) + unit_eps)
    uq, k = aq * iq, ak * ik
    q = uq * scale
    n_chunk = rows // chunk
    cuts = [slice(c * chunk, (c + 1) * chunk) for c in range(n_chunk)]
    blocks = [slice(c * width, (c + 1) * width) for c in range(n_chunk)]
    gs = [g_r[0].astype(f32)]
    for c in reversed(range(1, n_chunk)):
        gs.insert(0, tn(dt_r[blocks[c], :], gs[0]) + b_r[blocks[c], :])
    row = lax.broadcasted_iota(jnp.int32, (chunk, chunk), 0)
    col = lax.broadcasted_iota(jnp.int32, (chunk, chunk), 1)
    same = [docs_c[sl, :] == docs_r[:, sl] for sl in cuts]
    ks = [k[sl].astype(bf16) for sl in cuts]
    dos = [do_r[sl, :].astype(bf16) for sl in cuts]
    zs = [z_r[ds, :].astype(bf16) for ds in blocks]
    gbs = [g.astype(bf16) for g in gs]
    wkzs = [
        nn(jnp.concatenate([w_r[sl, :].astype(bf16), kc], axis=0), z) for sl, kc, z in zip(cuts, ks, zs)
    ]
    us = [(u_r[sl, :] - x[:chunk]).astype(bf16) for sl, x in zip(cuts, wkzs)]
    dus = [tn(p_r[sl, :].astype(bf16), do) for sl, do in zip(cuts, dos)]
    dus = [x + nn((last[sl] * k[sl]).astype(bf16), g) for x, sl, g in zip(dus, cuts, gbs)]
    drs = [tn(t_r[sl, :].astype(bf16), x.astype(bf16)) for sl, x in zip(cuts, dus)]
    ys = [
        nt(jnp.concatenate([do, dr.astype(bf16)], axis=0), jnp.concatenate([u, z], axis=0))
        for do, dr, u, z in zip(dos, drs, us, zs)
    ]
    dps = [jnp.where(m & (row >= col), y[:chunk, :chunk], 0.0) for m, y in zip(same, ys)]
    das = [jnp.where(m & (row > col), -y[chunk:, :chunk], 0.0) for m, y in zip(same, ys)]
    pbs = [
        jnp.concatenate([dp, beta[sl] * da], axis=0).astype(bf16) for dp, da, sl in zip(dps, das, cuts)
    ]
    paks = [nn(pb, kc) for pb, kc in zip(pbs, ks)]
    turns = [
        tn(pb, jnp.concatenate([q[sl].astype(bf16), kc], axis=0)) for pb, sl, kc in zip(pbs, cuts, ks)
    ]
    ugs = [nt(u, g) for u, g in zip(us, gbs)]
    dq = jnp.concatenate([cont[sl] * y[:chunk, chunk:] + x[:chunk] for sl, y, x in zip(cuts, ys, paks)], axis=0)
    dk = jnp.concatenate(
        [
            t + x[chunk:] + last[sl] * ug - (beta[sl] * cont[sl]) * y[chunk:, chunk:]
            for t, x, sl, ug, y in zip(turns, paks, cuts, ugs, ys)
        ],
        axis=0,
    )
    dv = jnp.concatenate([beta[sl] * dr for sl, dr in zip(cuts, drs)], axis=0)
    db = jnp.concatenate(
        [
            jnp.sum(dr * (v[sl] - cont[sl] * x[chunk:]), axis=1, keepdims=True)
            + jnp.sum(da * kk_r[sl, :], axis=1, keepdims=True)
            for dr, sl, x, da in zip(drs, cuts, wkzs, das)
        ],
        axis=0,
    )
    lane = lax.broadcasted_iota(jnp.int32, dlogit_o.shape, 1)
    dlogit_o[...] = jnp.where(lane == head, db * beta * (1.0 - beta), jnp.where(head == 0, 0.0, dlogit_o[...]))
    du_q = dq * scale
    da_q = (du_q - uq * jnp.sum(uq * du_q, axis=1, keepdims=True)) * iq
    da_k = (dk - k * jnp.sum(k * dk, axis=1, keepdims=True)) * ik
    for dact, sg, c_r, src, halo, taps, dst, dhalo, dtaps, tail in (
        (da_q, sq, cq, pq, hq, tq, dpq, dhq, dtq, tails[0]),
        (da_k, sk, ck, pk, hk, tk, dpk, dhk, dtk, tails[1]),
        (dv, sv, cv, pv, hv, tv, dpv, dhv, dtv, tails[2]),
    ):
        dconv = dact * (sg * (1.0 + c_r[...] * (1.0 - sg)))
        pad[0:8, :] = halo[...]
        pad[8 : 8 + rows, :] = src[...]
        zero = jnp.zeros((8, width), f32)
        total = taps[3:4, :] * dconv
        early = zero
        gtaps = [None] * 4
        gtaps[3] = jnp.sum(dconv * src[...], axis=0, keepdims=True)
        for back, mask in ((1, mask1), (2, mask2), (3, mask3)):
            kept = dconv * keeps[back - 1]
            gtaps[3 - back] = jnp.sum(kept * pad[8 - back : 8 - back + rows, :], axis=0, keepdims=True)
            mask[0:8, :] = zero
            mask[8 : 8 + rows, :] = kept
            mask[8 + rows : 16 + rows, :] = zero
            total = total + taps[3 - back : 4 - back, :] * mask[8 + back : 8 + back + rows, :]
            early = early + taps[3 - back : 4 - back, :] * mask[back : back + 8, :]
        dst[...] = total.astype(dst.dtype)
        dhalo[...] = early
        if tail is not None:
            tail[...] = total[rows - 16 :]
        dtaps[...] = jnp.concatenate(gtaps + [jnp.zeros((4, width), f32)], axis=0)


def bit_orders(n_dp, n_seq):
    dp_bits = [("dp", i) for i in range(n_dp.bit_length() - 1)]
    seq_bits = [("seq", i) for i in range(n_seq.bit_length() - 1)]
    return (
        seq_bits[:1] + dp_bits + seq_bits[1:],
        seq_bits[:1] + dp_bits[::-1] + seq_bits[1:],
        seq_bits + dp_bits,
        seq_bits + dp_bits[::-1],
    )


def scatter_steps(sizes, units, slots, lefts, rights, outs, scratch):
    n_dp, n_seq = sizes
    scratch = list(scratch)
    orders = bit_orders(n_dp, n_seq)
    steps = len(orders[0])
    pool = [scratch.pop(0) for _ in range(2 * (1 + max(slots)))]
    own = [pool[2 * slots[u] + half] for u in range(len(units)) for half in (0, 1)]
    before = [max([w for w in range(u) if slots[w] == slots[u]], default=None) for u in range(len(units))]
    got = [[scratch.pop(0) for _ in range(steps)] for _ in range(2 * len(units))]
    ssem, rsem = scratch
    index = {"dp": lax.axis_index("dp"), "seq": lax.axis_index("seq")}

    def bit_of(axis, bit):
        return (index[axis] // 2**bit) % 2

    def partner(axis, bit):
        other = dict(index)
        other[axis] = index[axis] + (1 - 2 * bit_of(axis, bit)) * 2**bit
        return (other["dp"], other["seq"])

    def greet():
        for axis, bit in orders[0]:
            pl.semaphore_signal(
                pltpu.get_barrier_semaphore(), inc=1, device_id=partner(axis, bit), device_id_type=MESH
            )
        return steps

    def weights(order):
        return {key: 2 ** (steps - 1 - i) for i, key in enumerate(order)}

    def place(order, axis, value):
        w = weights(order)
        return sum(((value // 2**b) % 2) * w[(a, b)] for a, b in order if a == axis)

    def compute(u):
        kind, li, _, _, cols, _, _, first_order = units[u]
        left, (right, first) = lefts[li], rights(u)
        block = left.shape[1] // (n_dp * n_seq)
        together = n_seq
        while together * block % 128:
            together *= 2
        half_cols = cols // 2

        def rows_of(m, carry):
            span = pl.ds(pl.multiple_of(m * (together * block), 128), together * block)
            tile = tn(left[:, span], right[:, first : first + cols])
            for half in (0, 1):
                order, buf = orders[first_order + half], own[2 * u + half]
                for j in range(together):
                    piece = tile[j * block : (j + 1) * block, half * half_cols : (half + 1) * half_cols]
                    if kind == "stack":
                        piece = jnp.concatenate([piece[:, : cols // 4], piece[:, cols // 4 :]], axis=0)
                    base = place(order, "dp", m * (together // n_seq) + j // n_seq)
                    buf[base + place(order, "seq", j % n_seq)] = piece.astype(bf16)
            return carry

        lax.fori_loop(0, n_dp * n_seq // together, rows_of, 0)

    def copy_of(u, half, k):
        src = own[2 * u + half] if k == 0 else got[2 * u + half][k - 1]
        dst = got[2 * u + half][k]
        axis, bit = orders[units[u][7] + half][k]
        count = dst.shape[0]
        return pltpu.make_async_remote_copy(
            src_ref=src.at[pl.ds((1 - bit_of(axis, bit)) * count, count)], dst_ref=dst,
            send_sem=ssem.at[u, half, k], recv_sem=rsem.at[u, half, k],
            device_id=partner(axis, bit), device_id_type=MESH,
        )

    def merge(u, half, k):
        src = own[2 * u + half] if k == 0 else got[2 * u + half][k - 1]
        dst = got[2 * u + half][k]
        axis, bit = orders[units[u][7] + half][k]
        count = dst.shape[0]
        mine = bit_of(axis, bit) * count
        copy_of(u, half, k).wait_recv()
        if k < steps - 1:
            def add(i, carry):
                dst[i] = dst[i] + src[mine + i]
                return carry

            lax.fori_loop(0, count, add, 0)
            copy_of(u, half, k + 1).start()
        else:
            kind, _, _, first, cols, oi, to, _ = units[u]
            total = dst[0].astype(f32) + src[mine].astype(f32)
            start, wide = to + half * (cols // 2), cols // 2
            if kind == "stack":
                block = total.shape[0] // 2
                outs[oi][:, start : start + wide // 2] = total[:block]
                outs[oi][:, start + wide // 2 : start + wide] = total[block:]
            else:
                outs[oi][:, start : start + wide] = total

    def begin(u):
        if before[u] is not None:
            for half in (0, 1):
                copy_of(before[u], half, 0).wait_send()
        compute(u)
        for half in (0, 1):
            copy_of(u, half, 0).start()

    def both_merge(u, k):
        for half in (0, 1):
            merge(u, half, k)

    def finish():
        for k in range(steps):
            for u in range(len(units)):
                if k > 0 or u not in before:
                    for half in (0, 1):
                        copy_of(u, half, k).wait_send()

    return steps, partner, greet, begin, both_merge, finish


def small_steps(sizes, partner, small_in, small_out, small_got, small_ssem, small_rsem):
    order = bit_orders(*sizes)[0]
    steps = len(order)

    def small_copy(k):
        return pltpu.make_async_remote_copy(
            src_ref=small_in if k == 0 else small_got.at[steps + k - 1], dst_ref=small_got.at[k],
            send_sem=small_ssem.at[k], recv_sem=small_rsem.at[k],
            device_id=partner(*order[k]), device_id_type=MESH,
        )

    def small_step(k):
        small_copy(k).wait_recv()
        mine = small_in[...] if k == 0 else small_got[steps + k - 1]
        if k < steps - 1:
            small_got[steps + k] = small_got[k] + mine
            small_copy(k + 1).start()
        else:
            small_out[...] = small_got[k] + mine

    def small_finish():
        for k in range(steps):
            small_copy(k).wait_send()

    return small_copy(0).start, small_step, small_finish


def scatter_layout(sizes, products, order, keep):
    n = sizes[0] * sizes[1]
    steps = n.bit_length() - 1
    units, outs = [], []
    for oi, (left, right, kind, cols) in enumerate(products):
        block = left.shape[1] // n
        outs.append(jax.ShapeDtypeStruct((block, right.shape[1]), f32))
        first = 0
        for wide, first_order in cols:
            units.append((kind, oi, oi, first, wide, oi, first, first_order))
            first += wide
    units = [units[i] for i in order or range(len(units))]
    shapes = []
    for kind, oi, _, _, wide, _, _, _ in units:
        block = outs[oi].shape[0]
        shapes.append((2 * block, wide // 4) if kind == "stack" else (block, wide // 2))
    pool, slots = [], []
    for u, shape in enumerate(shapes):
        alike = [i for i, kept in enumerate(pool) if kept == shape]
        if len(alike) < keep[units[u][0]]:
            slots.append(len(pool))
            pool.append(shape)
        else:
            used = [max(w for w in range(u) if slots[w] == i) for i in alike]
            slots.append(alike[used.index(min(used))])
    own = [pltpu.VMEM((n,) + s, bf16) for s in pool for _ in (0, 1)]
    got = [pltpu.VMEM((n >> (k + 1),) + s, bf16) for s in shapes for _ in (0, 1) for k in range(steps)]
    sems = pltpu.SemaphoreType.DMA((len(units), 2, steps))
    return units, slots, outs, own + got + [sems, sems]


def back_scatter_kernel(sizes, chunk, heads, units, slots, plan, n_prod, *refs):
    turn = pl.program_id(0)
    refs = list(refs)

    def take(count):
        got = refs[:count]
        del refs[:count]
        return got

    far_lefts, far_rights = take(n_prod), take(n_prod)
    dh, o, gain, qt, dt, turned = take(6)
    common, saved = take(13), take(9)
    outs, mains, tapped, tail_o, dlogit, dgain = take(n_prod), take(3), take(3), *take(3)
    lefts, rights, fetch, ring_sem = take(n_prod), take(n_prod), *take(2)
    do_s, b_s, seed_s, g_s, send, relay_ssem, relay_rsem = take(7)
    pads = take(4)
    early_s, late_s, tail_s, halo_ssem, halo_rsem = take(5)
    ringed = [u for u, unit in enumerate(units) if unit[1] == RINGED]

    def right_of(u):
        if u in ringed:
            return rights[RINGED].at[ringed.index(u) % 2], 0
        return rights[units[u][2]], units[u][3]

    def ring_fetch(place):
        _, _, ri, first, wide, _, _, _ = units[ringed[place]]
        return pltpu.make_async_copy(
            far_rights[ri].at[:, pl.ds(first, wide)],
            rights[ri].at[place % 2, :, pl.ds(0, wide)],
            ring_sem.at[place % 2],
        )

    steps, partner, greet, begin, merge, finish = scatter_steps(sizes, units, slots, lefts, right_of, outs, refs)

    def fetches(i):
        copies = [pltpu.make_async_copy(far_lefts[i], lefts[i], fetch.at[i, 0])]
        if i != RINGED:
            copies.append(pltpu.make_async_copy(far_rights[i], rights[i], fetch.at[i, 1]))
        return copies

    segment = lax.axis_index("seq")

    def halo_copy(head):
        return pltpu.make_async_remote_copy(
            src_ref=early_s.at[head], dst_ref=late_s.at[head], send_sem=halo_ssem.at[head], recv_sem=halo_rsem.at[head],
            device_id=(lax.axis_index("dp"), segment - 1), device_id_type=MESH,
        )

    seen = [unit[1] for unit in units]
    arrival = sorted(range(n_prod), key=seen.index)

    @pl.when(turn == 0)
    def _():
        for i in arrival:
            for copy in fetches(i):
                copy.start()
        for place in (0, 1):
            ring_fetch(place).start()
        pl.semaphore_wait(pltpu.get_barrier_semaphore(), greet() + relay_greet(sizes[1], True))

    @pl.when(turn < heads)
    def _():
        seed_body(
            chunk, turn, dh, o, gain, qt, dt, do_s.at[turn], b_s.at[turn], seed_s.at[pl.ds(turn, 1)], dgain
        )

    @pl.when(turn == heads)
    def _():
        relay_body(sizes[1], True, turned, seed_s, g_s, send, relay_ssem, relay_rsem)

    for t, events in enumerate(plan):
        if events:
            @pl.when(turn == t)
            def _(events=events):
                for u, k in events:
                    if k < 0:
                        if seen.index(seen[u]) == u:
                            for copy in fetches(seen[u]):
                                copy.wait()
                        if u in ringed:
                            ring_fetch(ringed.index(u)).wait()
                        begin(u)
                        if u in ringed and ringed.index(u) + 2 < len(ringed):
                            ring_fetch(ringed.index(u) + 2).start()
                    else:
                        merge(u, k)

    @pl.when(turn >= heads)
    def _():
        head = turn - heads
        back_body(
            chunk, head, *common, *saved, do_s.at[head], dt, b_s.at[head], g_s.at[pl.ds(head, 1)],
            *mains, *[early_s.at[head, third] for third in range(3)], *tapped, dlogit, *pads,
            tails=[tail_s.at[head, third] for third in range(3)],
        )

        @pl.when(segment > 0)
        def _():
            halo_copy(head).start()

    @pl.when(turn == 2 * heads - 1)
    def _():
        width = late_s.shape[3]

        @pl.when(segment == sizes[1] - 1)
        def _():
            late_s[...] = jnp.zeros(late_s.shape, f32)

        @pl.when(segment < sizes[1] - 1)
        def _():
            for head in range(heads):
                halo_copy(head).wait_recv()

        for head in range(heads):
            for third in range(3):
                tail = tail_s[head, third]
                tail = jnp.concatenate([tail[:8], tail[8:] + late_s[head, third]], axis=0)
                tail_o[:, (third * heads + head) * width : (third * heads + head + 1) * width] = tail.astype(bf16)

        @pl.when(segment > 0)
        def _():
            for head in range(heads):
                halo_copy(head).wait_send()

        finish()


def final_kernel(sizes, units, slots, *refs):
    refs = list(refs)

    def take(count):
        got = refs[:count]
        del refs[:count]
        return got

    far, (far_w, tails, xn1, tokens, d_one, gain, dlogit, small_in) = take(3), take(8)
    outs, (small_out, grad_o) = take(3), take(2)
    rights, (weight, small_s, gain_s, fetch) = take(3), take(4)
    small_scratch = take(3)
    rows, model = xn1.shape
    steps, partner, greet, begin, merge, finish = scatter_steps(
        sizes, units, slots, [xn1] * 3, lambda u: (rights[units[u][2]], units[u][3]), outs, refs
    )
    small_start, small_step, small_finish = small_steps(sizes, partner, small_s, small_out, *small_scratch)
    fetches = [pltpu.make_async_copy(a, b, fetch.at[i]) for i, (a, b) in enumerate(zip(far + [far_w], rights + [weight]))]
    for copy in fetches:
        copy.start()
    pl.semaphore_wait(pltpu.get_barrier_semaphore(), greet())
    small_s[...] = small_in[...]
    small_s[0:8, :] = tn(dlogit[...], xn1[...])[0:8]

    def token_grads():
        part = rows // 2
        fetches[3].wait()
        gain_s[...] = jnp.zeros(gain_s.shape, f32)

        def some(i, carry):
            at = pl.ds(pl.multiple_of(i * part, 16), part)
            dx = nt(dlogit[at, :], weight[:, 3 * model :])
            for third in range(3):
                dx = dx + nt(rights[third][at, :], weight[:, third * model : (third + 1) * model])
            x = tokens[at, :].astype(f32)
            scale = lax.rsqrt(jnp.mean(x * x, axis=1, keepdims=True) + norm_eps)
            n = x * scale
            gain_s[0:1, :] += jnp.sum(dx * n, axis=0, keepdims=True)
            y = dx * gain[...]
            dz = (y - n * jnp.mean(y * n, axis=1, keepdims=True)) * scale
            grad_o[at, :] = (d_one[at, :] + dz).astype(bf16)
            return carry

        lax.fori_loop(0, 2, some, 0)
        small_s[8:9, :] = gain_s[0:1, :]

    seen = [unit[2] for unit in units]
    for t in range(len(units) + steps):
        for k in range(steps):
            if 0 <= t - 1 - k < len(units):
                merge(t - 1 - k, k)
        if t < len(units):
            third = seen[t]
            if seen.index(third) == t and third not in seen[: TOKEN_TURN + 1][:t] and (t <= TOKEN_TURN):
                fetches[third].wait()
                rights[third][rows - 16 :, :] = tails[:, third * model : (third + 1) * model]
            begin(t)
        if t == len(units) - 1:
            small_start()
        if 0 <= t - len(units) < steps:
            small_step(t - len(units))
        if t == TOKEN_TURN:
            for copy in fetches[max(seen[: t + 1]) + 1 : 3]:
                copy.wait()
            for third in range(max(seen[: t + 1]) + 1, 3):
                rights[third][rows - 16 :, :] = tails[:, third * model : (third + 1) * model]
            token_grads()
    finish()
    small_finish()


def back_plan(n_units, steps, heads, early):
    plan = [[] for _ in range(2 * heads)]
    for i in range(n_units + steps):
        turn = 2 * i if i <= early else heads + i - early - 1
        turn = min(turn, 2 * heads - 1)
        for k in range(steps):
            if 0 <= i - 1 - k < n_units and not (i == early + 1 and k == 0):
                plan[turn].append((i - 1 - k, k))
        if i < n_units:
            plan[turn].append((i, -1))
        if i == early:
            plan[heads - 1].append((early, 0))
    return plan


def gather_steps(sizes, shard, whole, own_sem, ssem, rsem):
    n_dp, n_seq = sizes
    index = {"dp": lax.axis_index("dp"), "seq": lax.axis_index("seq")}
    orders = [order[::-1] for order in bit_orders(n_dp, n_seq)[:2]]
    steps = len(orders[0])
    by_rows = shard.shape[0] % 32 == 0
    extent = shard.shape[0 if by_rows else 1] // 2

    def flipped(keys):
        other = dict(index)
        for axis, bit in keys:
            other[axis] = other[axis] + (1 - 2 * ((index[axis] // 2**bit) % 2)) * 2**bit
        return (other["dp"], other["seq"])

    def half_of(ref, half):
        part = pl.ds(half * extent, extent)
        return ref.at[part] if by_rows else ref.at[:, part]

    def copy_of(half, path, k):
        order = orders[half]
        dp, seq = flipped([order[i] for i in path])
        dst = half_of(whole.at[dp * n_seq + seq], half)
        code = sum(2**i for i in path) + 2**k
        return pltpu.make_async_remote_copy(
            src_ref=dst if path else half_of(shard, half), dst_ref=dst,
            send_sem=ssem.at[half, code], recv_sem=rsem.at[half, code],
            device_id=flipped([order[k]]), device_id_type=MESH,
        )

    paths = sorted(
        (tuple(i for i in range(steps) if code >> i & 1) for code in range(2**steps)), key=lambda p: (len(p), p)
    )
    keep = pltpu.make_async_copy(shard, whole.at[index["dp"] * n_seq + index["seq"]], own_sem)

    def greet():
        barrier = pltpu.get_barrier_semaphore()
        for key in orders[0]:
            pl.semaphore_signal(barrier, inc=1, device_id=flipped([key]), device_id_type=MESH)
        pl.semaphore_wait(barrier, steps)

    def level(hops):
        if hops == 0:
            keep.start()
        for path in paths:
            if len(path) == hops:
                for half in (0, 1):
                    if path:
                        copy_of(half, path[:-1], path[-1]).wait_recv()
                    for k in range((path[-1] if path else -1) + 1, steps):
                        copy_of(half, path, k).start()

    def finish():
        for path in paths:
            if path:
                for half in (0, 1):
                    copy_of(half, path[:-1], path[-1]).wait_send()
        keep.wait()

    return steps, greet, level, finish


def gather_kernel(sizes, shard, whole, *sems):
    steps, greet, level, finish = gather_steps(sizes, shard, whole, *sems)
    greet()
    for hops in range(steps + 1):
        level(hops)
    finish()


def gather_beside(sizes, turn, shards, wholes, sems, turns):
    plans = [
        gather_steps(sizes, shard, whole, *sems[3 * i : 3 * i + 3])
        for i, (shard, whole) in enumerate(zip(shards, wholes))
    ]
    if not plans:
        return
    greet = plans[0][1]
    for hops, when in enumerate(turns):
        @pl.when(turn == when)
        def _(hops=hops):
            if hops == 0:
                greet()
            for plan in plans:
                plan[2](hops)


def gather_rest(sizes, turn, shards, wholes, sems, done, final):
    plans = [
        gather_steps(sizes, shard, whole, *sems[3 * i : 3 * i + 3])
        for i, (shard, whole) in enumerate(zip(shards, wholes))
    ]
    if not plans:
        return

    @pl.when(turn == final)
    def _():
        for hops in range(done, plans[0][0] + 1):
            for plan in plans:
                plan[2](hops)
        for plan in plans:
            plan[3]()


def gather_sems(sizes):
    sems = pltpu.SemaphoreType.DMA((2, sizes[0] * sizes[1]))
    return [pltpu.SemaphoreType.DMA, sems, sems]


def whole_like(sizes, shard):
    return jax.ShapeDtypeStruct((sizes[0] * sizes[1],) + shard.shape, shard.dtype)


def flat_rows(whole):
    return whole.reshape((whole.shape[0] * whole.shape[1],) + whole.shape[2:])


def gather_rows(sizes, shard, cid):
    anywhere = pl.BlockSpec(memory_space=pl.ANY)
    whole = pl.pallas_call(
        functools.partial(gather_kernel, sizes),
        in_specs=[anywhere],
        out_specs=anywhere,
        out_shape=whole_like(sizes, shard),
        scratch_shapes=gather_sems(sizes),
        compiler_params=pltpu.CompilerParams(collective_id=cid, has_side_effects=True),
        name="gather_rows",
    )(shard)
    return flat_rows(whole)


def from_behind(value, axis, steps):
    count = lax.axis_size(axis)
    first, last = (max(0, -steps), min(count, count - steps))
    return lax.ppermute(value, axis, [(source, source + steps) for source in range(first, last)])


def rms_scale(values, gain):
    return values * lax.rsqrt(jnp.mean(values * values, axis=-1, keepdims=True) + norm_eps) * gain


def doc_ids(lengths, positions):
    ends = jnp.cumsum(lengths)
    inside = (positions[:, None] >= ends[None, :]).astype(jnp.int32)
    return jnp.where(positions >= 0, jnp.sum(inside, axis=1), -1)


def swiglu(gate_up):
    half = gate_up.shape[1] // 2
    return jax.nn.silu(gate_up[:, :half]) * gate_up[:, half:]


def contract_rows(left, right):
    return tn(left, right)


def contract_cols(left, right):
    return nt(left, right)


def local(
    n_dp, n_seq, tokens, doc_lengths, norm_gain, w_qkv, w_beta, conv_weight, head_gain, w_out, mlp_gain, w_mlp_in, w_down, grad_out,
):
    rows, model = tokens.shape
    heads = w_beta.shape[1]
    width = head_gain.shape[0]
    taps_n = conv_weight.shape[0]
    qkv = w_qkv.shape[1]
    chunk = min(128, rows)
    n_chunk = rows // chunk
    both = ("dp", "seq")

    sizes = (n_dp, n_seq)
    own_kernels = (model // (n_dp * n_seq)) % 32 == 0 and heads > (n_dp * n_seq).bit_length()
    w_d = lax.all_gather(w_down, both, axis=0, tiled=True)
    w_in = jnp.concatenate([w_qkv, jnp.pad(w_beta, ((0, 0), (0, 128 - heads)))], axis=1)
    if own_kernels:
        beside = [w_out, w_mlp_in]
        w_in = gather_rows(sizes, w_in, 3)
    else:
        beside = []
        w_in, w_o, w_m = (lax.all_gather(w, both, axis=0, tiled=True) for w in (w_in, w_out, w_mlp_in))

    inputs = tokens.astype(f32)
    norm_one, pull_one = jax.vjp(rms_scale, inputs, norm_gain.astype(f32))
    xn1 = norm_one.astype(bf16)
    projected = nn(xn1, w_in)
    logits = projected[:, qkv : qkv + heads]
    start = lax.axis_index("seq") * rows
    docs_pad = doc_ids(doc_lengths[0], start - taps_n + 1 + jnp.arange(rows + taps_n - 1, dtype=jnp.int32))
    docs = docs_pad[taps_n - 1 :]
    by_chunk = docs.reshape(n_chunk, chunk)
    before = docs_pad[taps_n - 2 : taps_n - 2 + rows].reshape(n_chunk, chunk)[:, :1]
    aux = jnp.stack(
        [(by_chunk == before).reshape(-1), (by_chunk == by_chunk[:, -1:]).reshape(-1)]
        + [docs_pad[taps_n - 1 - b : taps_n - 1 - b + rows] == docs for b in (1, 2, 3)]
        + [docs < -5] * 3,
        axis=1,
    ).astype(f32)
    docs_c, docs_r = docs[:, None], docs[None, :]
    received = from_behind(projected[rows - taps_n + 1 :, :qkv].astype(bf16), "seq", 1).astype(f32)
    halo = jnp.pad(received, ((8 - taps_n + 1, 0), (0, 0)))
    taps = jnp.pad(conv_weight.astype(f32), ((0, 8 - taps_n), (0, 0)))

    def third(block_rows):
        return [pl.BlockSpec((block_rows, width), lambda h, t=t: (0, t * heads + h)) for t in range(3)]

    def per_head(block_rows):
        return pl.BlockSpec((block_rows, width), lambda h: (0, h))

    def whole(shape):
        return pl.BlockSpec(shape, lambda h: (0,) * len(shape))

    state_block = pl.BlockSpec((1, width, width), lambda h: (h, 0, 0))
    params = pltpu.CompilerParams(vmem_limit_bytes=VMEM_LIMIT, dimension_semantics=("arbitrary",))
    cols = heads * width
    token_like = jax.ShapeDtypeStruct((rows, cols), f32)
    chunk_like = jax.ShapeDtypeStruct((rows, heads * chunk), f32)
    state_like = jax.ShapeDtypeStruct((n_chunk * width, cols), f32)
    common_specs = (
        third(rows) + third(8) + third(8)
        + [whole((rows, 8)), whole((rows, 1)), whole((1, rows)), whole((rows, heads))]
    )
    common = (projected,) * 3 + (halo,) * 3 + (taps,) * 3 + (aux, docs_c, docs_r, logits)
    chunk_block = pl.BlockSpec((rows, chunk), lambda h: (0, h))
    anywhere = pl.BlockSpec(memory_space=pl.ANY)
    maps_like = jax.ShapeDtypeStruct((heads, width, width), f32)
    cq, ck, cv, w_s, u_s, qt, o0, t_s, p_s, kk_s, dt, ft, seg_map, seg_turned, seg_add, *wholes = pl.pallas_call(
        functools.partial(local_kernel, sizes, chunk, len(beside)),
        grid=(heads,),
        in_specs=[anywhere] * len(beside) + common_specs,
        out_specs=[per_head(rows)] * 7 + [chunk_block] * 3 + [per_head(n_chunk * width)] * 2 + [state_block] * 3
        + [anywhere] * len(beside),
        out_shape=[token_like] * 3 + [jax.ShapeDtypeStruct((rows, cols), bf16)] + [token_like] * 3
        + [jax.ShapeDtypeStruct((rows, heads * chunk), bf16)] * 2 + [chunk_like] + [state_like] * 2 + [maps_like] * 3
        + [whole_like(sizes, w) for w in beside],
        scratch_shapes=[pltpu.VMEM((rows + 8, width), f32)] + [sem for _ in beside for sem in gather_sems(sizes)],
        compiler_params=pltpu.CompilerParams(
            vmem_limit_bytes=VMEM_LIMIT, dimension_semantics=("arbitrary",),
            **(dict(collective_id=4, has_side_effects=True) if beside else {}),
        ),
        name="delta_local",
    )(*beside, *common)
    if beside:
        w_o, w_m = (flat_rows(w) for w in wholes)

    def relay(back, maps, adds, cid):
        return pl.pallas_call(
            functools.partial(relay_kernel, n_seq, back),
            in_specs=[pl.BlockSpec(memory_space=pltpu.VMEM)] * 2,
            out_specs=pl.BlockSpec(memory_space=pltpu.VMEM),
            out_shape=jax.ShapeDtypeStruct((heads, width, width), bf16),
            scratch_shapes=[
                pltpu.VMEM((heads, width, width), bf16),
                pltpu.SemaphoreType.DMA((heads,)),
                pltpu.SemaphoreType.DMA((heads,)),
            ],
            compiler_params=pltpu.CompilerParams(collective_id=cid, has_side_effects=True, vmem_limit_bytes=VMEM_LIMIT),
            name="relay_back" if back else "relay",
        )(maps, adds)

    state_in = relay(False, seg_map, seg_add, 0)
    gain_h = head_gain.astype(f32)[None, :]
    z_s, mixed, head_out = pl.pallas_call(
        functools.partial(output_kernel, chunk),
        grid=(heads,),
        in_specs=[state_block, per_head(n_chunk * width), per_head(n_chunk * width), per_head(rows), per_head(rows), whole((1, width))],
        out_specs=[per_head(n_chunk * width), per_head(rows), per_head(rows)],
        out_shape=[
            jax.ShapeDtypeStruct(state_like.shape, bf16), token_like, jax.ShapeDtypeStruct((rows, cols), bf16)
        ],
        compiler_params=params,
        name="delta_out",
    )(state_in, dt, ft, qt, o0, gain_h)

    hidden_one = inputs + nn(head_out, w_o)
    norm_two, pull_two = jax.vjp(rms_scale, hidden_one, mlp_gain.astype(f32))
    xn2 = norm_two.astype(bf16)
    gate_up = nn(xn2, w_m)
    hidden_f, pull_act = jax.vjp(swiglu, gate_up)
    hidden = hidden_f.astype(bf16)
    out = (hidden_one + nn(hidden, w_d)).astype(bf16)

    grad_in = grad_out.astype(f32)
    d_hidden = contract_cols(grad_out, w_d)
    d_gate_up = pull_act(d_hidden)[0].astype(bf16)
    d_from_two, d_mlp_gain = pull_two(contract_cols(d_gate_up, w_m))
    d_hidden_one = grad_in + d_from_two
    d_att = d_hidden_one.astype(bf16)
    d_head = contract_cols(d_att, w_o)

    parts = [
        (hidden, grad_out, "stack", [(512, 0)] * 2),
        (xn2, d_gate_up, "plain", [(512, 2), (1024, 0)] * 3 + [(512, 2), (512, 0)]),
        (head_out, d_att, "plain", [(1024, 0)]),
    ]
    if own_kernels:
        parts[1] = parts[1][:3] + (B_COLS,)
        units, slots, grads_like, scratch = scatter_layout(
            sizes, parts, B_ORDER, {"plain": 2, "stack": 1}
        )
        steps = (n_dp * n_seq).bit_length() - 1
        plan = back_plan(len(units), steps, heads, 3)

        def late(spec):
            shape, index = spec.block_shape, spec.index_map
            return pl.BlockSpec(shape, lambda t: index(jnp.maximum(t - heads, 0)))

        def soon(spec):
            shape, index = spec.block_shape, spec.index_map
            return pl.BlockSpec(shape, lambda t: index(jnp.minimum(t, heads - 1)))

        def each(spec):
            shape, index = spec.block_shape, spec.index_map
            return pl.BlockSpec(shape, lambda t: index(jnp.where(t < heads, t, t - heads)))

        n_prod = len(parts)
        results = pl.pallas_call(
            functools.partial(back_scatter_kernel, sizes, chunk, heads, units, slots, plan, n_prod),
            grid=(2 * heads,),
            in_specs=[anywhere] * (2 * n_prod)
            + [soon(per_head(rows))] * 2 + [whole((1, width)), soon(per_head(rows)), each(per_head(n_chunk * width))]
            + [whole((heads, width, width))]
            + [late(spec) for spec in common_specs + [per_head(rows)] * 5 + [chunk_block] * 3 + [per_head(n_chunk * width)]],
            out_specs=[whole(like.shape) for like in grads_like]
            + [late(spec) for spec in [per_head(rows)] * 3 + [per_head(8)] * 3]
            + [whole((16, qkv)), whole((rows, heads)), whole((8, width))],
            out_shape=grads_like + [jax.ShapeDtypeStruct((rows, cols), bf16)] * 3
            + [jax.ShapeDtypeStruct((8, cols), f32)] * 3
            + [jax.ShapeDtypeStruct((16, qkv), bf16), jax.ShapeDtypeStruct((rows, heads), f32), jax.ShapeDtypeStruct((8, width), f32)],
            scratch_shapes=[pltpu.VMEM(p[0].shape, bf16) for p in parts]
            + [pltpu.VMEM((2, rows, 1024) if i == RINGED else p[1].shape, bf16) for i, p in enumerate(parts)]
            + [pltpu.SemaphoreType.DMA((n_prod, 2)), pltpu.SemaphoreType.DMA((2,))]
            + [
                pltpu.VMEM((heads, rows, width), bf16), pltpu.VMEM((heads, n_chunk * width, width), f32),
                pltpu.VMEM((heads, width, width), f32), pltpu.VMEM((heads, width, width), bf16),
                pltpu.VMEM((heads, width, width), bf16),
                pltpu.SemaphoreType.DMA((heads,)), pltpu.SemaphoreType.DMA((heads,)),
            ]
            + [pltpu.VMEM((rows + 8, width), f32)] + [pltpu.VMEM((rows + 16, width), f32)] * 3
            + [pltpu.VMEM((heads, 3, 8, width), f32)] * 2 + [pltpu.VMEM((heads, 3, 16, width), f32)]
            + [pltpu.SemaphoreType.DMA((heads,)), pltpu.SemaphoreType.DMA((heads,))]
            + scratch,
            compiler_params=pltpu.CompilerParams(
                collective_id=1, has_side_effects=True, vmem_limit_bytes=63 << 20, dimension_semantics=("arbitrary",)
            ),
            name="back_scatter",
        )(
            *[p[0] for p in parts], *[p[1] for p in parts], d_head, mixed, gain_h, qt, dt, seg_turned,
            *common, cq, ck, cv, w_s, u_s, t_s, p_s, kk_s, z_s,
        )
        (g_down, g_mlp, g_out), mains, tapped = results[:n_prod], results[n_prod : n_prod + 3], results[n_prod + 3 : n_prod + 6]
        tails, d_logits, d_head_gain = results[n_prod + 6 :]
        d_conv = jnp.concatenate(tapped, axis=1)[:taps_n]
        small = jnp.concatenate(
            [
                jnp.zeros((9, model), f32),
                d_mlp_gain[None],
                d_conv.reshape(-1, model),
                jnp.pad(d_head_gain[0:1], ((0, 0), (0, model - width))),
            ],
            axis=0,
        )
        count = small.shape[0]
        small = jnp.pad(small, ((0, -count % 8), (0, 0)))
        parts = [(xn1, main, "plain", cols_in) for main, cols_in in zip(mains, F_COLS)]
        units, slots, grads_like, scratch = scatter_layout(sizes, parts, None, {"plain": 3})
        vmem = pl.BlockSpec(memory_space=pltpu.VMEM)
        *g_in, small, grad_tokens = pl.pallas_call(
            functools.partial(final_kernel, sizes, units, slots),
            in_specs=[anywhere] * 4 + [vmem] * 7,
            out_specs=[vmem] * 5,
            out_shape=grads_like + [jax.ShapeDtypeStruct(small.shape, f32), jax.ShapeDtypeStruct((rows, model), bf16)],
            scratch_shapes=[pltpu.VMEM((rows, model), bf16)] * 3 + [pltpu.VMEM(w_in.shape, bf16)]
            + [pltpu.VMEM(small.shape, f32), pltpu.VMEM((8, model), f32), pltpu.SemaphoreType.DMA((4,))]
            + [pltpu.VMEM((2 * steps,) + small.shape, f32), pltpu.SemaphoreType.DMA((steps,)), pltpu.SemaphoreType.DMA((steps,))]
            + scratch,
            compiler_params=pltpu.CompilerParams(collective_id=2, has_side_effects=True, vmem_limit_bytes=63 << 20),
            name="final_scatter",
        )(
            *mains, w_in, tails, xn1, tokens, d_hidden_one, norm_gain.astype(f32)[None],
            jnp.pad(d_logits, ((0, 0), (0, 128 - heads))).astype(bf16), small,
        )
        g_in = jnp.concatenate(g_in, axis=1)
        mine = (lax.axis_index("dp") * n_seq + lax.axis_index("seq")) * (model // (n_dp * n_seq))
        g_beta = lax.dynamic_slice(small[:heads], (0, mine), (heads, model // (n_dp * n_seq))).T
        s_norm, s_mlp = small[heads], small[heads + 1]
        s_conv = small[heads + 2 : count - 1].reshape(taps_n, qkv)
        s_head = small[count - 1, :width]
    else:
        do, b_s, seed, d_head_gain = pl.pallas_call(
            functools.partial(seed_kernel, chunk),
            grid=(heads,),
            in_specs=[per_head(rows), per_head(rows), whole((1, width)), per_head(rows), per_head(n_chunk * width)],
            out_specs=[per_head(rows), per_head(n_chunk * width), state_block, whole((8, width))],
            out_shape=[token_like, state_like, jax.ShapeDtypeStruct((heads, width, width), f32), jax.ShapeDtypeStruct((8, width), f32)],
            compiler_params=params,
            name="delta_seed",
        )(d_head, mixed, gain_h, qt, dt)
        grad_end = relay(True, seg_turned, seed, 1)
        outs = pl.pallas_call(
            functools.partial(back_kernel, chunk),
            grid=(heads,),
            in_specs=common_specs + [per_head(rows)] * 5 + [chunk_block] * 3
            + [per_head(n_chunk * width), per_head(rows), per_head(n_chunk * width), per_head(n_chunk * width), state_block],
            out_specs=[per_head(rows)] * 3 + [per_head(8)] * 6 + [whole((rows, heads))],
            out_shape=[token_like] * 3 + [jax.ShapeDtypeStruct((8, cols), f32)] * 6 + [jax.ShapeDtypeStruct((rows, heads), f32)],
            scratch_shapes=[pltpu.VMEM((rows + 8, width), f32)] + [pltpu.VMEM((rows + 16, width), f32)] * 3,
            compiler_params=params,
            name="delta_back",
        )(*common, cq, ck, cv, w_s, u_s, t_s, p_s, kk_s, z_s, do, dt, b_s, grad_end)
        d_main = jnp.concatenate(outs[:3], axis=1)
        d_early = jnp.concatenate(outs[3:6], axis=1)
        d_conv = jnp.concatenate(outs[6:9], axis=1)[:taps_n]
        d_logits = outs[9]
        returned = from_behind(d_early[8 - taps_n + 1 :].astype(bf16), "seq", -1).astype(f32)
        d_projected = d_main + jnp.pad(returned, ((rows - taps_n + 1, 0), (0, 0)))
        d_proj_b = jnp.concatenate(
            [d_projected.astype(bf16), jnp.pad(d_logits.astype(bf16), ((0, 0), (0, 128 - heads)))], axis=1
        )
        d_from_one, d_norm_gain = pull_one(contract_cols(d_proj_b, w_in))
        grad_tokens = (d_hidden_one + d_from_one).astype(bf16)

        d_beta_rows = tn(d_logits.astype(bf16), xn1)
        g_down, g_mlp, g_out, g_in, g_beta = (
            lax.psum_scatter(grad, both, scatter_dimension=0, tiled=True)
            for grad in [contract_rows(left, right) for left, right, _, _ in parts]
            + [contract_rows(xn1, d_proj_b[:, :qkv]), d_beta_rows.T]
        )
        s_norm, s_conv, s_head, s_mlp = lax.psum((d_norm_gain, d_conv, d_head_gain[0], d_mlp_gain), both)
    return (out, grad_tokens, s_norm, g_in, g_beta, s_conv, s_head, g_out, s_mlp, g_mlp, g_down)


def solution(mesh):
    split = P(("dp", "seq"), None)
    placed = (split, P("dp", None), P(), split, split, P(), P(), split, P(), split, split, split)
    return jax.shard_map(
        functools.partial(local, mesh.shape["dp"], mesh.shape["seq"]),
        mesh=mesh,
        in_specs=placed,
        out_specs=(split, split, P(), split, split, P(), P(), split, P(), split, split),
        check_vma=False,
    )
```

```python
import functools

import jax
import jax.numpy as jnp
from jax import lax
from jax.experimental import pallas as pl
from jax.experimental.pallas import tpu as pltpu
from jax.sharding import PartitionSpec as P

norm_eps = 1e-05
unit_eps = 1e-06
MESH = pl.DeviceIdType.MESH
f32, bf16 = jnp.float32, jnp.bfloat16
HIGH = lax.Precision.HIGH
VMEM_LIMIT = 56 << 20
SPARE = 24
TURNS = (0, 1, 5)
RINGED = 1
B_COLS = [(1024, 0)] * 5 + [(512, 0)]
B_ORDER = [2, 3, 4, 0, 5, 1, 6, 8, 7]
TOKEN_TURN = 1
F_COLS = [[(1024, 0)], [(1024, 0)], [(512, 0), (512, 0)]]


def nn(a, b, prec=None):
    return lax.dot_general(a, b, (((1,), (0,)), ((), ())), precision=prec, preferred_element_type=f32)


def nt(a, b, prec=None):
    return lax.dot_general(a, b, (((1,), (1,)), ((), ())), precision=prec, preferred_element_type=f32)


def tn(a, b, prec=None):
    return lax.dot_general(a, b, (((0,), (0,)), ((), ())), precision=prec, preferred_element_type=f32)


def unit_lower_inverses(mats, row, col):
    size = mats[0].shape[0]
    block = min(8, size)
    eye = (row == col).astype(f32)
    near = row // block == col // block
    powers = [jnp.where(near, -a, 0.0) for a in mats]
    inverses = [eye + p for p in powers]
    reach = 2
    while reach < block:
        powers = [nn(p, p, HIGH) for p in powers]
        inverses = [t + nn(t, p, HIGH) for t, p in zip(inverses, powers)]
        reach *= 2
    while block < size:
        pairs = size // (2 * block)

        def lower(m, block=block, pairs=pairs):
            return jnp.concatenate([m[(2 * i + 1) * block : (2 * i + 2) * block] for i in range(pairs)], axis=0)

        def spread(m, fill, block=block, pairs=pairs):
            return jnp.concatenate(
                [x for i in range(pairs) for x in (fill[2 * i * block : (2 * i + 1) * block], m[i * block : (i + 1) * block])],
                axis=0,
            )

        off = (row // (2 * block) == col // (2 * block)) & (row // block == col // block + 1)
        lows = [lower(jnp.where(off, a, 0.0)) for a in mats]
        crossed = [nn(x, t, HIGH) for x, t in zip(lows, inverses)]
        zero = jnp.zeros((size, size), f32)
        below = [lower(t) for t in inverses]
        fixed = [x - nn(x, spread(y, zero), HIGH) for x, y in zip(below, crossed)]
        inverses = [spread(x, t) for x, t in zip(fixed, inverses)]
        block *= 2
    return inverses


def head_column(matrix, head):
    lane = lax.broadcasted_iota(jnp.int32, matrix.shape, 1)
    return jnp.sum(jnp.where(lane == head, matrix, 0.0), axis=1, keepdims=True)


def masks_of(docs_col, docs_row):
    size = docs_col.shape[0]
    row = lax.broadcasted_iota(jnp.int32, (size, size), 0)
    col = lax.broadcasted_iota(jnp.int32, (size, size), 1)
    same = docs_col == docs_row
    return row, col, same


def local_kernel(
    sizes, chunk, gathers, *refs,
):
    far = 1 if gathers else 0
    local_body(
        sizes, chunk, gathers, refs[:gathers], refs[gathers] if far else None, *refs[gathers + far :]
    )


def local_body(
    sizes, chunk, gathers, shards, far_rows, pq, pk, pv, hq, hk, hv, tq, tk, tv, aux, docs_c, docs_r, logits,
    cq, ck, cv, w_o, u_o, qt_o, o_o, t_o, p_o, kk_o, dt_o, ft_o, map_o, turned_o, add_o, *rest,
):
    head = pl.program_id(0)
    turns = TURNS
    if gathers:
        wholes, (halo_o, pad, halo_s, halo_ssem, halo_rsem), sems = rest[:gathers], rest[gathers : gathers + 5], rest[gathers + 5 :]
        segment, heads, span = lax.axis_index("seq"), pl.num_programs(0), pq.shape[1]
        tail = pltpu.make_async_remote_copy(
            src_ref=far_rows.at[pl.ds(pq.shape[0] - 8, 8), pl.ds(0, halo_s.shape[1])], dst_ref=halo_s,
            send_sem=halo_ssem, recv_sem=halo_rsem,
            device_id=(lax.axis_index("dp"), segment + 1), device_id_type=MESH,
        )

        @pl.when(head == 0)
        def _():
            pl.semaphore_wait(
                pltpu.get_barrier_semaphore(), gather_greet(sizes) + relay_greet(sizes[1], False)
            )

            @pl.when(segment < sizes[1] - 1)
            def _():
                tail.start()

        gather_beside(sizes, head, shards, wholes, sems, turns)

        @pl.when(head == 0)
        def _():
            @pl.when(segment == 0)
            def _():
                halo_s[...] = jnp.zeros(halo_s.shape, f32)

            @pl.when(segment > 0)
            def _():
                tail.wait_recv()

            halo_o[...] = halo_s[...]

        @pl.when((head == heads - 1) & (segment < sizes[1] - 1))
        def _():
            tail.wait_send()

        hq, hk, hv = (
            halo_s.at[:, pl.ds(pl.multiple_of((third * heads + head) * span, span), span)] for third in range(3)
        )
    else:
        pad, wholes, sems = rest[0], (), ()
    rows, width = pq.shape
    keeps = (aux[:, 2:3], aux[:, 3:4], aux[:, 4:5])
    acts = []
    for src, halo, taps, dst in ((pq, hq, tq, cq), (pk, hk, tk, ck), (pv, hv, tv, cv)):
        pad[0:8, :] = halo[...]
        pad[8 : 8 + rows, :] = src[...]
        conv = taps[3:4, :] * src[...]
        for back in (1, 2, 3):
            conv = conv + taps[3 - back : 4 - back, :] * (pad[8 - back : 8 - back + rows, :] * keeps[back - 1])
        dst[...] = conv
        acts.append(conv * jax.nn.sigmoid(conv))
    q = acts[0] * (lax.rsqrt(jnp.sum(acts[0] * acts[0], axis=1, keepdims=True) + unit_eps) * width ** (-0.5))
    k = acts[1] * lax.rsqrt(jnp.sum(acts[1] * acts[1], axis=1, keepdims=True) + unit_eps)
    v = acts[2]
    beta = jax.nn.sigmoid(head_column(logits[...], head))
    cont, last = aux[:, 0:1], aux[:, 1:2]
    n_chunk = rows // chunk
    cuts = [slice(c * chunk, (c + 1) * chunk) for c in range(n_chunk)]
    row = lax.broadcasted_iota(jnp.int32, (chunk, chunk), 0)
    col = lax.broadcasted_iota(jnp.int32, (chunk, chunk), 1)
    same = [docs_c[sl, :] == docs_r[:, sl] for sl in cuts]
    kks = [nt(k[sl], k[sl], HIGH) for sl in cuts]
    ps = [jnp.where(m & (row >= col), nt(q[sl], k[sl], HIGH), 0.0) for m, sl in zip(same, cuts)]
    ts = unit_lower_inverses(
        [jnp.where(m & (row > col), beta[sl] * kk, 0.0) for m, sl, kk in zip(same, cuts, kks)], row, col
    )
    rhs = [jnp.concatenate([(beta[sl] * cont[sl]) * k[sl], beta[sl] * v[sl]], axis=1) for sl in cuts]
    wus = [nn(t, r, HIGH) for t, r in zip(ts, rhs)]
    pwus = [nn(p, wu, HIGH) for p, wu in zip(ps, wus)]
    xs = [tn(last[sl] * k[sl], wu, HIGH) for sl, wu in zip(cuts, wus)]
    d_row = lax.broadcasted_iota(jnp.int32, (width, width), 0)
    d_col = lax.broadcasted_iota(jnp.int32, (width, width), 1)
    seg = None
    for c, sl in enumerate(cuts):
        cc = cont[sl]
        dt = jnp.where(d_row == d_col, cc[chunk - 1 : chunk], 0.0) - xs[c][:, :width]
        ft = xs[c][:, width:]
        w_o[sl, :] = wus[c][:, :width].astype(bf16)
        u_o[sl, :] = wus[c][:, width:]
        qt_o[sl, :] = cc * q[sl] - pwus[c][:, :width]
        o_o[sl, :] = pwus[c][:, width:]
        t_o[sl, :] = ts[c].astype(bf16)
        p_o[sl, :] = ps[c].astype(bf16)
        kk_o[sl, :] = kks[c]
        dt_o[c * width : (c + 1) * width, :] = dt
        ft_o[c * width : (c + 1) * width, :] = ft
        if seg is None:
            seg = jnp.concatenate([dt, ft], axis=1)
        else:
            seg = nn(dt, seg, HIGH)
            seg = jnp.concatenate([seg[:, :width], seg[:, width:] + ft], axis=1)
    map_o[0] = seg[:, :width]
    turned_o[0] = seg[:, :width].T
    add_o[0] = seg[:, width:]
    gather_rest(sizes, head, shards, wholes, sems, len(turns), pl.num_programs(0) - 1)


def relay_ends(n_seq, back):
    s = lax.axis_index("seq")
    if back:
        return s == n_seq - 1, s == 0, s - 1, s + 1
    return s == 0, s == n_seq - 1, s + 1, s - 1


def relay_greet(n_seq, back):
    d = lax.axis_index("dp")
    first, final, ahead, behind = relay_ends(n_seq, back)
    barrier = pltpu.get_barrier_semaphore()

    @pl.when(jnp.logical_not(first))
    def _():
        pl.semaphore_signal(barrier, inc=1, device_id=(d, behind), device_id_type=MESH)

    @pl.when(jnp.logical_not(final))
    def _():
        pl.semaphore_signal(barrier, inc=1, device_id=(d, ahead), device_id_type=MESH)

    return jnp.where(first | final, 1, 2)


def relay_kernel(n_seq, back, *refs):
    pl.semaphore_wait(pltpu.get_barrier_semaphore(), relay_greet(n_seq, back))
    relay_body(n_seq, back, *refs)


def relay_body(n_seq, back, map_ref, add_ref, out_ref, send, ssem, rsem):
    d = lax.axis_index("dp")
    heads = map_ref.shape[0]
    first, final, ahead, behind = relay_ends(n_seq, back)

    def copy_of(h):
        return pltpu.make_async_remote_copy(
            src_ref=send.at[h], dst_ref=out_ref.at[h], send_sem=ssem.at[h], recv_sem=rsem.at[h],
            device_id=(d, ahead), device_id_type=MESH,
        )

    @pl.when(first)
    def _():
        out_ref[...] = jnp.zeros(out_ref.shape, out_ref.dtype)
        for h in range(heads):
            send[h] = add_ref[h].astype(bf16)
            copy_of(h).start()

    @pl.when(jnp.logical_not(first))
    def _():
        for h in range(heads):
            copy_of(h).wait_recv()
            send[h] = (nn(map_ref[h], out_ref[h].astype(f32), HIGH) + add_ref[h]).astype(bf16)

            @pl.when(jnp.logical_not(final))
            def _():
                copy_of(h).start()

    @pl.when(jnp.logical_not(final))
    def _():
        for h in range(heads):
            copy_of(h).wait_send()


def output_kernel(chunk, zin, dt, ft, qt, o0, gain, z_o, o_o, head_o):
    width = gain.shape[1]
    rows = qt.shape[0]
    sides = [slice(i * width, (i + 1) * width) for i in range(zin.shape[0])]
    states = [zin[i].astype(f32) for i in range(zin.shape[0])]
    for c in range(rows // chunk):
        sl = slice(c * chunk, (c + 1) * chunk)
        ds = slice(c * width, (c + 1) * width)
        for z, side in zip(states, sides):
            z_o[ds, side] = z.astype(bf16)
        outs = [o0[sl, side] + nn(qt[sl, side], z, HIGH) for z, side in zip(states, sides)]
        if c + 1 < rows // chunk:
            states = [nn(dt[ds, side], z, HIGH) + ft[ds, side] for z, side in zip(states, sides)]
        for o, side in zip(outs, sides):
            o_o[sl, side] = o
            scale = lax.rsqrt(jnp.mean(o * o, axis=1, keepdims=True) + norm_eps)
            head_o[sl, side] = (o * scale * gain[...]).astype(bf16)


def seed_kernel(chunk, *refs):
    seed_body(chunk, pl.program_id(0), *refs)


def seed_body(chunk, head, dh, o, gain, qt, dt, do_o, b_o, seed_o, dgain_o):
    rows, width = qt.shape
    ov, dhv = o[...], dh[...]
    scale = lax.rsqrt(jnp.mean(ov * ov, axis=1, keepdims=True) + norm_eps)
    n = ov * scale
    dg = jnp.sum(dhv * n, axis=0, keepdims=True)
    dgain_o[...] = jnp.where(head == 0, 0.0, dgain_o[...]) + jnp.broadcast_to(dg, dgain_o.shape)
    y = dhv * gain[...]
    do = (y - n * jnp.mean(y * n, axis=1, keepdims=True)) * scale
    do_o[...] = do.astype(do_o.dtype)
    g = None
    for c in reversed(range(rows // chunk)):
        sl = slice(c * chunk, (c + 1) * chunk)
        ds = slice(c * width, (c + 1) * width)
        b_o[ds, :] = tn(qt[sl, :], do[sl], HIGH)
        g = b_o[ds, :] if g is None else tn(dt[ds, :], g, HIGH) + b_o[ds, :]
    seed_o[0] = g


def back_kernel(chunk, *refs):
    back_body(chunk, pl.program_id(0), *refs)


def back_body(
    chunk, head, pq, pk, pv, hq, hk, hv, tq, tk, tv, aux, docs_c, docs_r, logits,
    cq, ck, cv, w_r, u_r, t_r, p_r, kk_r, z_r, do_r, dt_r, b_r, g_r,
    dpq, dpk, dpv, dhq, dhk, dhv, dtq, dtk, dtv, dlogit_o, pad, mask1, mask2, mask3, tails=(None,) * 3,
):
    rows, width = pq.shape
    cont, last = aux[:, 0:1], aux[:, 1:2]
    keeps = (aux[:, 2:3], aux[:, 3:4], aux[:, 4:5])
    scale = width ** (-0.5)
    beta = jax.nn.sigmoid(head_column(logits[...], head))
    sq, sk, sv = (jax.nn.sigmoid(x[...]) for x in (cq, ck, cv))
    aq, ak, v = cq[...] * sq, ck[...] * sk, cv[...] * sv
    iq = lax.rsqrt(jnp.sum(aq * aq, axis=1, keepdims=True) + unit_eps)
    ik = lax.rsqrt(jnp.sum(ak * ak, axis=1, keepdims=True) + unit_eps)
    uq, k = aq * iq, ak * ik
    q = uq * scale
    n_chunk = rows // chunk
    cuts = [slice(c * chunk, (c + 1) * chunk) for c in range(n_chunk)]
    blocks = [slice(c * width, (c + 1) * width) for c in range(n_chunk)]
    gs = [g_r[0].astype(f32)]
    for c in reversed(range(1, n_chunk)):
        gs.insert(0, tn(dt_r[blocks[c], :], gs[0]) + b_r[blocks[c], :])
    row = lax.broadcasted_iota(jnp.int32, (chunk, chunk), 0)
    col = lax.broadcasted_iota(jnp.int32, (chunk, chunk), 1)
    same = [docs_c[sl, :] == docs_r[:, sl] for sl in cuts]
    ks = [k[sl].astype(bf16) for sl in cuts]
    dos = [do_r[sl, :].astype(bf16) for sl in cuts]
    zs = [z_r[ds, :].astype(bf16) for ds in blocks]
    gbs = [g.astype(bf16) for g in gs]
    wkzs = [
        nn(jnp.concatenate([w_r[sl, :].astype(bf16), kc], axis=0), z) for sl, kc, z in zip(cuts, ks, zs)
    ]
    us = [(u_r[sl, :] - x[:chunk]).astype(bf16) for sl, x in zip(cuts, wkzs)]
    dus = [tn(p_r[sl, :].astype(bf16), do) for sl, do in zip(cuts, dos)]
    dus = [x + nn((last[sl] * k[sl]).astype(bf16), g) for x, sl, g in zip(dus, cuts, gbs)]
    drs = [tn(t_r[sl, :].astype(bf16), x.astype(bf16)) for sl, x in zip(cuts, dus)]
    ys = [
        nt(jnp.concatenate([do, dr.astype(bf16)], axis=0), jnp.concatenate([u, z], axis=0))
        for do, dr, u, z in zip(dos, drs, us, zs)
    ]
    dps = [jnp.where(m & (row >= col), y[:chunk, :chunk], 0.0) for m, y in zip(same, ys)]
    das = [jnp.where(m & (row > col), -y[chunk:, :chunk], 0.0) for m, y in zip(same, ys)]
    pbs = [
        jnp.concatenate([dp, beta[sl] * da], axis=0).astype(bf16) for dp, da, sl in zip(dps, das, cuts)
    ]
    paks = [nn(pb, kc) for pb, kc in zip(pbs, ks)]
    turns = [
        tn(pb, jnp.concatenate([q[sl].astype(bf16), kc], axis=0)) for pb, sl, kc in zip(pbs, cuts, ks)
    ]
    ugs = [nt(u, g) for u, g in zip(us, gbs)]
    dq = jnp.concatenate([cont[sl] * y[:chunk, chunk:] + x[:chunk] for sl, y, x in zip(cuts, ys, paks)], axis=0)
    dk = jnp.concatenate(
        [
            t + x[chunk:] + last[sl] * ug - (beta[sl] * cont[sl]) * y[chunk:, chunk:]
            for t, x, sl, ug, y in zip(turns, paks, cuts, ugs, ys)
        ],
        axis=0,
    )
    dv = jnp.concatenate([beta[sl] * dr for sl, dr in zip(cuts, drs)], axis=0)
    db = jnp.concatenate(
        [
            jnp.sum(dr * (v[sl] - cont[sl] * x[chunk:]), axis=1, keepdims=True)
            + jnp.sum(da * kk_r[sl, :], axis=1, keepdims=True)
            for dr, sl, x, da in zip(drs, cuts, wkzs, das)
        ],
        axis=0,
    )
    lane = lax.broadcasted_iota(jnp.int32, dlogit_o.shape, 1)
    dlogit_o[...] = jnp.where(lane == head, db * beta * (1.0 - beta), jnp.where(head == 0, 0.0, dlogit_o[...]))
    du_q = dq * scale
    da_q = (du_q - uq * jnp.sum(uq * du_q, axis=1, keepdims=True)) * iq
    da_k = (dk - k * jnp.sum(k * dk, axis=1, keepdims=True)) * ik
    for dact, sg, c_r, src, halo, taps, dst, dhalo, dtaps, tail in (
        (da_q, sq, cq, pq, hq, tq, dpq, dhq, dtq, tails[0]),
        (da_k, sk, ck, pk, hk, tk, dpk, dhk, dtk, tails[1]),
        (dv, sv, cv, pv, hv, tv, dpv, dhv, dtv, tails[2]),
    ):
        dconv = dact * (sg * (1.0 + c_r[...] * (1.0 - sg)))
        pad[0:8, :] = halo[...]
        pad[8 : 8 + rows, :] = src[...]
        zero = jnp.zeros((8, width), f32)
        total = taps[3:4, :] * dconv
        early = zero
        gtaps = [None] * 4
        gtaps[3] = jnp.sum(dconv * src[...], axis=0, keepdims=True)
        for back, mask in ((1, mask1), (2, mask2), (3, mask3)):
            kept = dconv * keeps[back - 1]
            gtaps[3 - back] = jnp.sum(kept * pad[8 - back : 8 - back + rows, :], axis=0, keepdims=True)
            mask[0:8, :] = zero
            mask[8 : 8 + rows, :] = kept
            mask[8 + rows : 16 + rows, :] = zero
            total = total + taps[3 - back : 4 - back, :] * mask[8 + back : 8 + back + rows, :]
            early = early + taps[3 - back : 4 - back, :] * mask[back : back + 8, :]
        dst[...] = total.astype(dst.dtype)
        dhalo[...] = early
        if tail is not None:
            tail[...] = total[rows - 16 :]
        dtaps[...] = jnp.concatenate(gtaps + [jnp.zeros((4, width), f32)], axis=0)


def bit_orders(n_dp, n_seq):
    dp_bits = [("dp", i) for i in range(n_dp.bit_length() - 1)]
    seq_bits = [("seq", i) for i in range(n_seq.bit_length() - 1)]
    return (
        seq_bits[:1] + dp_bits + seq_bits[1:],
        seq_bits[:1] + dp_bits[::-1] + seq_bits[1:],
        seq_bits + dp_bits,
        seq_bits + dp_bits[::-1],
    )


def scatter_steps(sizes, units, slots, lefts, rights, outs, scratch, turned=()):
    n_dp, n_seq = sizes
    scratch = list(scratch)
    orders = bit_orders(n_dp, n_seq)
    steps = len(orders[0])
    pool = [scratch.pop(0) for _ in range(2 * (1 + max(slots)))]
    own = [pool[2 * slots[u] + half] for u in range(len(units)) for half in (0, 1)]
    before = [max([w for w in range(u) if slots[w] == slots[u]], default=None) for u in range(len(units))]
    got = [[scratch.pop(0) for _ in range(steps)] for _ in range(2 * len(units))]
    ssem, rsem = scratch
    index = {"dp": lax.axis_index("dp"), "seq": lax.axis_index("seq")}

    def bit_of(axis, bit):
        return (index[axis] // 2**bit) % 2

    def partner(axis, bit):
        other = dict(index)
        other[axis] = index[axis] + (1 - 2 * bit_of(axis, bit)) * 2**bit
        return (other["dp"], other["seq"])

    def greet():
        for axis, bit in orders[0]:
            pl.semaphore_signal(
                pltpu.get_barrier_semaphore(), inc=1, device_id=partner(axis, bit), device_id_type=MESH
            )
        return steps

    def weights(order):
        return {key: 2 ** (steps - 1 - i) for i, key in enumerate(order)}

    def place(order, axis, value):
        w = weights(order)
        return sum(((value // 2**b) % 2) * w[(a, b)] for a, b in order if a == axis)

    def compute(u):
        kind, li, _, _, cols, _, _, first_order = units[u]
        left, (right, first) = lefts[li], rights(u)
        block = left.shape[0 if li in turned else 1] // (n_dp * n_seq)
        together = n_seq
        while together * block % 128:
            together *= 2
        half_cols = cols // 2

        def rows_of(m, carry):
            span = pl.ds(pl.multiple_of(m * (together * block), 128), together * block)
            some = right[:, first : first + cols]
            tile = nn(left[span, :], some) if li in turned else tn(left[:, span], some)
            for half in (0, 1):
                order, buf = orders[first_order + half], own[2 * u + half]
                for j in range(together):
                    piece = tile[j * block : (j + 1) * block, half * half_cols : (half + 1) * half_cols]
                    if kind == "stack":
                        piece = jnp.concatenate([piece[:, : cols // 4], piece[:, cols // 4 :]], axis=0)
                    base = place(order, "dp", m * (together // n_seq) + j // n_seq)
                    buf[base + place(order, "seq", j % n_seq)] = piece.astype(bf16)
            return carry

        lax.fori_loop(0, n_dp * n_seq // together, rows_of, 0)

    def copy_of(u, half, k):
        src = own[2 * u + half] if k == 0 else got[2 * u + half][k - 1]
        dst = got[2 * u + half][k]
        axis, bit = orders[units[u][7] + half][k]
        count = dst.shape[0]
        return pltpu.make_async_remote_copy(
            src_ref=src.at[pl.ds((1 - bit_of(axis, bit)) * count, count)], dst_ref=dst,
            send_sem=ssem.at[u, half, k], recv_sem=rsem.at[u, half, k],
            device_id=partner(axis, bit), device_id_type=MESH,
        )

    def merge(u, half, k):
        src = own[2 * u + half] if k == 0 else got[2 * u + half][k - 1]
        dst = got[2 * u + half][k]
        axis, bit = orders[units[u][7] + half][k]
        count = dst.shape[0]
        mine = bit_of(axis, bit) * count
        copy_of(u, half, k).wait_recv()
        if k < steps - 1:
            def add(i, carry):
                dst[i] = dst[i] + src[mine + i]
                return carry

            lax.fori_loop(0, count, add, 0)
            copy_of(u, half, k + 1).start()
        else:
            kind, _, _, first, cols, oi, to, _ = units[u]
            total = dst[0].astype(f32) + src[mine].astype(f32)
            start, wide = to + half * (cols // 2), cols // 2
            if kind == "stack":
                block = total.shape[0] // 2
                outs[oi][:, start : start + wide // 2] = total[:block]
                outs[oi][:, start + wide // 2 : start + wide] = total[block:]
            else:
                outs[oi][:, start : start + wide] = total

    def begin(u):
        if before[u] is not None:
            for half in (0, 1):
                copy_of(before[u], half, 0).wait_send()
        compute(u)
        for half in (0, 1):
            copy_of(u, half, 0).start()

    def both_merge(u, k):
        for half in (0, 1):
            merge(u, half, k)

    def finish():
        for k in range(steps):
            for u in range(len(units)):
                if k > 0 or u not in before:
                    for half in (0, 1):
                        copy_of(u, half, k).wait_send()

    return steps, partner, greet, begin, both_merge, finish


def turn_over(src, dst):
    span = 256

    def some(i, carry):
        at = pl.ds(pl.multiple_of(i * span, span), span)
        dst[at, :] = src[:, at].T
        return carry

    lax.fori_loop(0, src.shape[1] // span, some, 0)


def small_steps(sizes, partner, small_in, small_out, small_got, small_ssem, small_rsem):
    order = bit_orders(*sizes)[0]
    steps = len(order)

    def small_copy(k):
        return pltpu.make_async_remote_copy(
            src_ref=small_in if k == 0 else small_got.at[steps + k - 1], dst_ref=small_got.at[k],
            send_sem=small_ssem.at[k], recv_sem=small_rsem.at[k],
            device_id=partner(*order[k]), device_id_type=MESH,
        )

    def small_step(k):
        small_copy(k).wait_recv()
        mine = small_in[...] if k == 0 else small_got[steps + k - 1]
        if k < steps - 1:
            small_got[steps + k] = small_got[k] + mine
            small_copy(k + 1).start()
        else:
            small_out[...] = small_got[k] + mine

    def small_finish():
        for k in range(steps):
            small_copy(k).wait_send()

    return small_copy(0).start, small_step, small_finish


def scatter_layout(sizes, products, order, keep):
    n = sizes[0] * sizes[1]
    steps = n.bit_length() - 1
    units, outs = [], []
    for oi, (left, right, kind, cols) in enumerate(products):
        block = left.shape[1] // n
        outs.append(jax.ShapeDtypeStruct((block, right.shape[1]), f32))
        first = 0
        for wide, first_order in cols:
            units.append((kind, oi, oi, first, wide, oi, first, first_order))
            first += wide
    units = [units[i] for i in order or range(len(units))]
    shapes = []
    for kind, oi, _, _, wide, _, _, _ in units:
        block = outs[oi].shape[0]
        shapes.append((2 * block, wide // 4) if kind == "stack" else (block, wide // 2))
    pool, slots = [], []
    for u, shape in enumerate(shapes):
        alike = [i for i, kept in enumerate(pool) if kept == shape]
        if len(alike) < keep[units[u][0]]:
            slots.append(len(pool))
            pool.append(shape)
        else:
            used = [max(w for w in range(u) if slots[w] == i) for i in alike]
            slots.append(alike[used.index(min(used))])
    own = [pltpu.VMEM((n,) + s, bf16) for s in pool for _ in (0, 1)]
    got = [pltpu.VMEM((n >> (k + 1),) + s, bf16) for s in shapes for _ in (0, 1) for k in range(steps)]
    sems = pltpu.SemaphoreType.DMA((len(units), 2, steps))
    return units, slots, outs, own + got + [sems, sems]


def back_scatter_kernel(sizes, chunk, heads, units, slots, plan, n_prod, *refs):
    turn = pl.program_id(0)
    refs = list(refs)

    def take(count):
        got = refs[:count]
        del refs[:count]
        return got

    far_lefts, far_rights = take(n_prod), take(n_prod)
    dh, o, gain, qt, dt, turned = take(6)
    common, saved = take(13), take(9)
    outs, mains, tapped, tail_o, dlogit, dgain = take(n_prod), take(3), take(3), *take(3)
    lefts, rights, fetch, ring_sem, turn_s = take(n_prod), take(n_prod), *take(3)
    do_s, b_s, seed_s, g_s, send, relay_ssem, relay_rsem = take(7)
    pads = take(4)
    early_s, late_s, tail_s, halo_ssem, halo_rsem = take(5)
    ringed = [u for u, unit in enumerate(units) if unit[1] == RINGED]

    def right_of(u):
        if u in ringed:
            return rights[RINGED].at[ringed.index(u) % 2], 0
        return rights[units[u][2]], units[u][3]

    def ring_fetch(place):
        _, _, ri, first, wide, _, _, _ = units[ringed[place]]
        return pltpu.make_async_copy(
            far_rights[ri].at[:, pl.ds(first, wide)],
            rights[ri].at[place % 2, :, pl.ds(0, wide)],
            ring_sem.at[place % 2],
        )

    steps, partner, greet, begin, merge, finish = scatter_steps(
        sizes, units, slots, [turn_s if i == RINGED else left for i, left in enumerate(lefts)],
        right_of, outs, refs, (RINGED,),
    )

    def fetches(i):
        copies = [pltpu.make_async_copy(far_lefts[i], lefts[i], fetch.at[i, 0])]
        if i != RINGED:
            copies.append(pltpu.make_async_copy(far_rights[i], rights[i], fetch.at[i, 1]))
        return copies

    segment = lax.axis_index("seq")

    def halo_copy(head):
        return pltpu.make_async_remote_copy(
            src_ref=early_s.at[head], dst_ref=late_s.at[head], send_sem=halo_ssem.at[head], recv_sem=halo_rsem.at[head],
            device_id=(lax.axis_index("dp"), segment - 1), device_id_type=MESH,
        )

    seen = [unit[1] for unit in units]
    arrival = sorted(range(n_prod), key=seen.index)

    @pl.when(turn == 0)
    def _():
        for i in arrival:
            for copy in fetches(i):
                copy.start()
        for place in (0, 1):
            ring_fetch(place).start()
        pl.semaphore_wait(pltpu.get_barrier_semaphore(), greet() + relay_greet(sizes[1], True))

    @pl.when(turn < heads)
    def _():
        seed_body(
            chunk, turn, dh, o, gain, qt, dt, do_s.at[turn], b_s.at[turn], seed_s.at[pl.ds(turn, 1)], dgain
        )

    @pl.when(turn == heads)
    def _():
        relay_body(sizes[1], True, turned, seed_s, g_s, send, relay_ssem, relay_rsem)

    for t, events in enumerate(plan):
        if events:
            @pl.when(turn == t)
            def _(events=events):
                for u, k in events:
                    if k < 0:
                        if seen.index(seen[u]) == u:
                            for copy in fetches(seen[u]):
                                copy.wait()
                            if seen[u] == RINGED:
                                turn_over(lefts[RINGED], turn_s)
                        if u in ringed:
                            ring_fetch(ringed.index(u)).wait()
                        begin(u)
                        if u in ringed and ringed.index(u) + 2 < len(ringed):
                            ring_fetch(ringed.index(u) + 2).start()
                    else:
                        merge(u, k)

    @pl.when(turn >= heads)
    def _():
        head = turn - heads
        back_body(
            chunk, head, *common, *saved, do_s.at[head], dt, b_s.at[head], g_s.at[pl.ds(head, 1)],
            *mains, *[early_s.at[head, third] for third in range(3)], *tapped, dlogit, *pads,
            tails=[tail_s.at[head, third] for third in range(3)],
        )

        @pl.when(segment > 0)
        def _():
            halo_copy(head).start()

    @pl.when(turn == 2 * heads - 1)
    def _():
        width = late_s.shape[3]

        @pl.when(segment == sizes[1] - 1)
        def _():
            late_s[...] = jnp.zeros(late_s.shape, f32)

        @pl.when(segment < sizes[1] - 1)
        def _():
            for head in range(heads):
                halo_copy(head).wait_recv()

        for head in range(heads):
            for third in range(3):
                tail = tail_s[head, third]
                tail = jnp.concatenate([tail[:8], tail[8:] + late_s[head, third]], axis=0)
                tail_o[:, (third * heads + head) * width : (third * heads + head + 1) * width] = tail.astype(bf16)

        @pl.when(segment > 0)
        def _():
            for head in range(heads):
                halo_copy(head).wait_send()

        finish()


def final_kernel(sizes, units, slots, *refs):
    refs = list(refs)

    def take(count):
        got = refs[:count]
        del refs[:count]
        return got

    far, (far_w, tails, xn1, tokens, d_one, gain, dlogit, small_in) = take(3), take(8)
    outs, (small_out, grad_o) = take(3), take(2)
    rights, (weight, small_s, gain_s, fetch, turn_s) = take(3), take(5)
    small_scratch = take(3)
    rows, model = xn1.shape
    steps, partner, greet, begin, merge, finish = scatter_steps(
        sizes, units, slots, [turn_s] * 3, lambda u: (rights[units[u][2]], units[u][3]), outs, refs, (0, 1, 2)
    )
    small_start, small_step, small_finish = small_steps(sizes, partner, small_s, small_out, *small_scratch)
    fetches = [pltpu.make_async_copy(a, b, fetch.at[i]) for i, (a, b) in enumerate(zip(far + [far_w], rights + [weight]))]
    for copy in fetches:
        copy.start()
    turn_over(xn1, turn_s)
    pl.semaphore_wait(pltpu.get_barrier_semaphore(), greet())
    small_s[...] = small_in[...]
    small_s[0:8, :] = tn(dlogit[...], xn1[...])[0:8]

    def token_grads():
        part = rows // 2
        fetches[3].wait()
        gain_s[...] = jnp.zeros(gain_s.shape, f32)

        def some(i, carry):
            at = pl.ds(pl.multiple_of(i * part, 16), part)
            dx = nt(dlogit[at, :], weight[:, 3 * model :])
            for third in range(3):
                dx = dx + nt(rights[third][at, :], weight[:, third * model : (third + 1) * model])
            x = tokens[at, :].astype(f32)
            scale = lax.rsqrt(jnp.mean(x * x, axis=1, keepdims=True) + norm_eps)
            n = x * scale
            gain_s[0:1, :] += jnp.sum(dx * n, axis=0, keepdims=True)
            y = dx * gain[...]
            dz = (y - n * jnp.mean(y * n, axis=1, keepdims=True)) * scale
            grad_o[at, :] = (d_one[at, :] + dz).astype(bf16)
            return carry

        lax.fori_loop(0, 2, some, 0)
        small_s[8:9, :] = gain_s[0:1, :]

    seen = [unit[2] for unit in units]
    for t in range(len(units) + steps):
        for k in range(steps):
            if 0 <= t - 1 - k < len(units):
                merge(t - 1 - k, k)
        if t < len(units):
            third = seen[t]
            if seen.index(third) == t and third not in seen[: TOKEN_TURN + 1][:t] and (t <= TOKEN_TURN):
                fetches[third].wait()
                rights[third][rows - 16 :, :] = tails[:, third * model : (third + 1) * model]
            begin(t)
        if t == len(units) - 1:
            small_start()
        if 0 <= t - len(units) < steps:
            small_step(t - len(units))
        if t == TOKEN_TURN:
            for copy in fetches[max(seen[: t + 1]) + 1 : 3]:
                copy.wait()
            for third in range(max(seen[: t + 1]) + 1, 3):
                rights[third][rows - 16 :, :] = tails[:, third * model : (third + 1) * model]
            token_grads()
    finish()
    small_finish()


def back_plan(n_units, steps, heads, early):
    plan = [[] for _ in range(2 * heads)]
    for i in range(n_units + steps):
        turn = 2 * i if i <= early else heads + i - early - 1
        turn = min(turn, 2 * heads - 1)
        for k in range(steps):
            if 0 <= i - 1 - k < n_units and not (i == early + 1 and k == 0):
                plan[turn].append((i - 1 - k, k))
        if i < n_units:
            plan[turn].append((i, -1))
        if i == early:
            plan[heads - 1].append((early, 0))
    return plan


def gather_parts(shape):
    rows, cols = shape
    half = rows // 2
    spare = cols * SPARE // 100 // 128 * 128 if cols >= 2048 else 0
    parts = [(i * half, half, 0, cols - spare) for i in (0, 1)]
    if spare:
        parts += [(i * half, half, cols - spare, spare) for i in (0, 1)]
    return parts


def gather_steps(sizes, shard, whole, own_sem, ssem, rsem):
    n_dp, n_seq = sizes
    index = {"dp": lax.axis_index("dp"), "seq": lax.axis_index("seq")}
    orders = [order[::-1] for order in bit_orders(n_dp, n_seq)]
    steps = len(orders[0])
    parts = gather_parts(shard.shape)

    def flipped(keys):
        other = dict(index)
        for axis, bit in keys:
            other[axis] = other[axis] + (1 - 2 * ((index[axis] // 2**bit) % 2)) * 2**bit
        return (other["dp"], other["seq"])

    def half_of(ref, half):
        top, height, left, wide = parts[half]
        return ref.at[pl.ds(top, height), pl.ds(left, wide)]

    def copy_of(half, path, k):
        order = orders[half]
        dp, seq = flipped([order[i] for i in path])
        dst = half_of(whole.at[dp * n_seq + seq], half)
        code = sum(2**i for i in path) + 2**k
        return pltpu.make_async_remote_copy(
            src_ref=dst if path else half_of(shard, half), dst_ref=dst,
            send_sem=ssem.at[half, code], recv_sem=rsem.at[half, code],
            device_id=flipped([order[k]]), device_id_type=MESH,
        )

    paths = sorted(
        (tuple(i for i in range(steps) if code >> i & 1) for code in range(2**steps)), key=lambda p: (len(p), p)
    )
    keep = pltpu.make_async_copy(shard, whole.at[index["dp"] * n_seq + index["seq"]], own_sem)

    def greet():
        barrier = pltpu.get_barrier_semaphore()
        for key in orders[0]:
            pl.semaphore_signal(barrier, inc=1, device_id=flipped([key]), device_id_type=MESH)
        return steps

    def level(hops):
        if hops == 0:
            keep.start()
        for path in paths:
            if len(path) == hops:
                for half in range(len(parts)):
                    if path:
                        copy_of(half, path[:-1], path[-1]).wait_recv()
                    for k in range((path[-1] if path else -1) + 1, steps):
                        copy_of(half, path, k).start()

    def finish():
        for path in paths:
            if path:
                for half in range(len(parts)):
                    copy_of(half, path[:-1], path[-1]).wait_send()
        keep.wait()

    return steps, greet, level, finish


def gather_kernel(sizes, shard, whole, *sems):
    steps, greet, level, finish = gather_steps(sizes, shard, whole, *sems)
    pl.semaphore_wait(pltpu.get_barrier_semaphore(), greet())
    for hops in range(steps + 1):
        level(hops)
    finish()


def gather_greet(sizes):
    index = {"dp": lax.axis_index("dp"), "seq": lax.axis_index("seq")}
    order = bit_orders(*sizes)[0]
    for axis, bit in order:
        other = dict(index)
        other[axis] = index[axis] + (1 - 2 * ((index[axis] // 2**bit) % 2)) * 2**bit
        pl.semaphore_signal(
            pltpu.get_barrier_semaphore(), inc=1, device_id=(other["dp"], other["seq"]), device_id_type=MESH
        )
    return len(order)


def gather_beside(sizes, turn, shards, wholes, sems, turns):
    plans = [
        gather_steps(sizes, shard, whole, *sems[3 * i : 3 * i + 3])
        for i, (shard, whole) in enumerate(zip(shards, wholes))
    ]
    if not plans:
        return
    for hops, when in enumerate(turns):
        @pl.when(turn == when)
        def _(hops=hops):
            for plan in plans:
                plan[2](hops)


def gather_rest(sizes, turn, shards, wholes, sems, done, final):
    plans = [
        gather_steps(sizes, shard, whole, *sems[3 * i : 3 * i + 3])
        for i, (shard, whole) in enumerate(zip(shards, wholes))
    ]
    if not plans:
        return

    @pl.when(turn == final)
    def _():
        for hops in range(done, plans[0][0] + 1):
            for plan in plans:
                plan[2](hops)
        for plan in plans:
            plan[3]()


def gather_sems(sizes, shard):
    sems = pltpu.SemaphoreType.DMA((len(gather_parts(shard.shape)), sizes[0] * sizes[1]))
    return [pltpu.SemaphoreType.DMA, sems, sems]


def whole_like(sizes, shard):
    return jax.ShapeDtypeStruct((sizes[0] * sizes[1],) + shard.shape, shard.dtype)


def flat_rows(whole):
    return whole.reshape((whole.shape[0] * whole.shape[1],) + whole.shape[2:])


def gather_rows(sizes, shard, cid):
    anywhere = pl.BlockSpec(memory_space=pl.ANY)
    whole = pl.pallas_call(
        functools.partial(gather_kernel, sizes),
        in_specs=[anywhere],
        out_specs=anywhere,
        out_shape=whole_like(sizes, shard),
        scratch_shapes=gather_sems(sizes, shard),
        compiler_params=pltpu.CompilerParams(collective_id=cid, has_side_effects=True),
        name="gather_rows",
    )(shard)
    return flat_rows(whole)


def from_behind(value, axis, steps):
    count = lax.axis_size(axis)
    first, last = (max(0, -steps), min(count, count - steps))
    return lax.ppermute(value, axis, [(source, source + steps) for source in range(first, last)])


def rms_scale(values, gain):
    return values * lax.rsqrt(jnp.mean(values * values, axis=-1, keepdims=True) + norm_eps) * gain


def doc_ids(lengths, positions):
    ends = jnp.cumsum(lengths)
    inside = (positions[:, None] >= ends[None, :]).astype(jnp.int32)
    return jnp.where(positions >= 0, jnp.sum(inside, axis=1), -1)


def swiglu(gate_up):
    half = gate_up.shape[1] // 2
    return jax.nn.silu(gate_up[:, :half]) * gate_up[:, half:]


def contract_rows(left, right):
    return tn(left, right)


def contract_cols(left, right):
    return nt(left, right)


def local(
    n_dp, n_seq, tokens, doc_lengths, norm_gain, w_qkv, w_beta, conv_weight, head_gain, w_out, mlp_gain, w_mlp_in, w_down, grad_out,
):
    rows, model = tokens.shape
    heads = w_beta.shape[1]
    width = head_gain.shape[0]
    taps_n = conv_weight.shape[0]
    qkv = w_qkv.shape[1]
    chunk = min(128, rows)
    n_chunk = rows // chunk
    both = ("dp", "seq")

    sizes = (n_dp, n_seq)
    own_kernels = (model // (n_dp * n_seq)) % 32 == 0 and heads > (n_dp * n_seq).bit_length()
    w_d = lax.all_gather(w_down, both, axis=0, tiled=True)
    w_in = jnp.concatenate([w_qkv, jnp.pad(w_beta, ((0, 0), (0, 128 - heads)))], axis=1)
    if own_kernels:
        beside = [w_mlp_in]
        w_o = lax.all_gather(w_out, both, axis=0, tiled=True)
        w_in = gather_rows(sizes, w_in, 3)
    else:
        beside = []
        w_in, w_o, w_m = (lax.all_gather(w, both, axis=0, tiled=True) for w in (w_in, w_out, w_mlp_in))

    inputs = tokens.astype(f32)
    norm_one, pull_one = jax.vjp(rms_scale, inputs, norm_gain.astype(f32))
    xn1 = norm_one.astype(bf16)
    projected = nn(xn1, w_in)
    logits = projected[:, qkv : qkv + heads]
    start = lax.axis_index("seq") * rows
    docs_pad = doc_ids(doc_lengths[0], start - taps_n + 1 + jnp.arange(rows + taps_n - 1, dtype=jnp.int32))
    docs = docs_pad[taps_n - 1 :]
    by_chunk = docs.reshape(n_chunk, chunk)
    before = docs_pad[taps_n - 2 : taps_n - 2 + rows].reshape(n_chunk, chunk)[:, :1]
    aux = jnp.stack(
        [(by_chunk == before).reshape(-1), (by_chunk == by_chunk[:, -1:]).reshape(-1)]
        + [docs_pad[taps_n - 1 - b : taps_n - 1 - b + rows] == docs for b in (1, 2, 3)]
        + [docs < -5] * 3,
        axis=1,
    ).astype(f32)
    docs_c, docs_r = docs[:, None], docs[None, :]
    if own_kernels:
        halo = jnp.zeros((8, qkv), f32)
    else:
        received = from_behind(projected[rows - taps_n + 1 :, :qkv].astype(bf16), "seq", 1).astype(f32)
        halo = jnp.pad(received, ((8 - taps_n + 1, 0), (0, 0)))
    taps = jnp.pad(conv_weight.astype(f32), ((0, 8 - taps_n), (0, 0)))

    def third(block_rows):
        return [pl.BlockSpec((block_rows, width), lambda h, t=t: (0, t * heads + h)) for t in range(3)]

    def per_head(block_rows):
        return pl.BlockSpec((block_rows, width), lambda h: (0, h))

    def whole(shape):
        return pl.BlockSpec(shape, lambda h: (0,) * len(shape))

    state_block = pl.BlockSpec((1, width, width), lambda h: (h, 0, 0))
    params = pltpu.CompilerParams(vmem_limit_bytes=VMEM_LIMIT, dimension_semantics=("arbitrary",))
    cols = heads * width
    token_like = jax.ShapeDtypeStruct((rows, cols), f32)
    chunk_like = jax.ShapeDtypeStruct((rows, heads * chunk), f32)
    state_like = jax.ShapeDtypeStruct((n_chunk * width, cols), f32)
    common_specs = (
        third(rows) + third(8) + third(8)
        + [whole((rows, 8)), whole((rows, 1)), whole((1, rows)), whole((rows, heads))]
    )
    common = (projected,) * 3 + (halo,) * 3 + (taps,) * 3 + (aux, docs_c, docs_r, logits)
    chunk_block = pl.BlockSpec((rows, chunk), lambda h: (0, h))
    anywhere = pl.BlockSpec(memory_space=pl.ANY)
    maps_like = jax.ShapeDtypeStruct((heads, width, width), f32)
    cq, ck, cv, w_s, u_s, qt, o0, t_s, p_s, kk_s, dt, ft, seg_map, seg_turned, seg_add, *wholes = pl.pallas_call(
        functools.partial(local_kernel, sizes, chunk, len(beside)),
        grid=(heads,),
        in_specs=[anywhere] * (len(beside) + bool(beside)) + common_specs,
        out_specs=[per_head(rows)] * 7 + [chunk_block] * 3 + [per_head(n_chunk * width)] * 2 + [state_block] * 3
        + [anywhere] * len(beside) + ([whole((8, qkv))] if beside else []),
        out_shape=[token_like] * 3 + [jax.ShapeDtypeStruct((rows, cols), bf16)] + [token_like] * 3
        + [jax.ShapeDtypeStruct((rows, heads * chunk), bf16)] * 2 + [chunk_like] + [state_like] * 2 + [maps_like] * 3
        + [whole_like(sizes, w) for w in beside] + ([jax.ShapeDtypeStruct((8, qkv), f32)] if beside else []),
        scratch_shapes=[pltpu.VMEM((rows + 8, width), f32)]
        + ([pltpu.VMEM((8, qkv), f32), pltpu.SemaphoreType.DMA, pltpu.SemaphoreType.DMA] if beside else [])
        + [sem for w in beside for sem in gather_sems(sizes, w)],
        compiler_params=pltpu.CompilerParams(
            vmem_limit_bytes=VMEM_LIMIT, dimension_semantics=("arbitrary",),
            **(dict(collective_id=4, has_side_effects=True) if beside else {}),
        ),
        name="delta_local",
    )(*beside, *([projected] if beside else []), *common)
    if beside:
        *wholes, halo = wholes
        common = common[:3] + (halo,) * 3 + common[6:]
        (w_m,) = (flat_rows(w) for w in wholes)

    def relay(back, maps, adds, cid):
        return pl.pallas_call(
            functools.partial(relay_kernel, n_seq, back),
            in_specs=[pl.BlockSpec(memory_space=pltpu.VMEM)] * 2,
            out_specs=pl.BlockSpec(memory_space=pltpu.VMEM),
            out_shape=jax.ShapeDtypeStruct((heads, width, width), bf16),
            scratch_shapes=[
                pltpu.VMEM((heads, width, width), bf16),
                pltpu.SemaphoreType.DMA((heads,)),
                pltpu.SemaphoreType.DMA((heads,)),
            ],
            compiler_params=pltpu.CompilerParams(collective_id=cid, has_side_effects=True, vmem_limit_bytes=VMEM_LIMIT),
            name="relay_back" if back else "relay",
        )(maps, adds)

    state_in = relay(False, seg_map, seg_add, 0)
    gain_h = head_gain.astype(f32)[None, :]
    some = 2 if heads % 2 == 0 else 1

    def several(block_rows):
        return pl.BlockSpec((block_rows, some * width), lambda h: (0, h))

    z_s, mixed, head_out = pl.pallas_call(
        functools.partial(output_kernel, chunk),
        grid=(heads // some,),
        in_specs=[pl.BlockSpec((some, width, width), lambda h: (h, 0, 0))]
        + [several(n_chunk * width)] * 2 + [several(rows)] * 2 + [whole((1, width))],
        out_specs=[several(n_chunk * width), several(rows), several(rows)],
        out_shape=[
            jax.ShapeDtypeStruct(state_like.shape, bf16), token_like, jax.ShapeDtypeStruct((rows, cols), bf16)
        ],
        compiler_params=params,
        name="delta_out",
    )(state_in, dt, ft, qt, o0, gain_h)

    hidden_one = inputs + nn(head_out, w_o)
    norm_two, pull_two = jax.vjp(rms_scale, hidden_one, mlp_gain.astype(f32))
    xn2 = norm_two.astype(bf16)
    gate_up = nn(xn2, w_m)
    hidden_f, pull_act = jax.vjp(swiglu, gate_up)
    hidden = hidden_f.astype(bf16)
    out = (hidden_one + nn(hidden, w_d)).astype(bf16)

    grad_in = grad_out.astype(f32)
    d_hidden = contract_cols(grad_out, w_d)
    d_gate_up = pull_act(d_hidden)[0].astype(bf16)
    d_from_two, d_mlp_gain = pull_two(contract_cols(d_gate_up, w_m))
    d_hidden_one = grad_in + d_from_two
    d_att = d_hidden_one.astype(bf16)
    d_head = contract_cols(d_att, w_o)

    parts = [
        (hidden, grad_out, "stack", [(512, 0)] * 2),
        (xn2, d_gate_up, "plain", [(512, 2), (1024, 0)] * 3 + [(512, 2), (512, 0)]),
        (head_out, d_att, "plain", [(1024, 0)]),
    ]
    if own_kernels:
        parts[1] = parts[1][:3] + (B_COLS,)
        units, slots, grads_like, scratch = scatter_layout(
            sizes, parts, B_ORDER, {"plain": 2, "stack": 1}
        )
        steps = (n_dp * n_seq).bit_length() - 1
        plan = back_plan(len(units), steps, heads, 3)

        def late(spec):
            shape, index = spec.block_shape, spec.index_map
            return pl.BlockSpec(shape, lambda t: index(jnp.maximum(t - heads, 0)))

        def soon(spec):
            shape, index = spec.block_shape, spec.index_map
            return pl.BlockSpec(shape, lambda t: index(jnp.minimum(t, heads - 1)))

        def each(spec):
            shape, index = spec.block_shape, spec.index_map
            return pl.BlockSpec(shape, lambda t: index(jnp.where(t < heads, t, t - heads)))

        n_prod = len(parts)
        results = pl.pallas_call(
            functools.partial(back_scatter_kernel, sizes, chunk, heads, units, slots, plan, n_prod),
            grid=(2 * heads,),
            in_specs=[anywhere] * (2 * n_prod)
            + [soon(per_head(rows))] * 2 + [whole((1, width)), soon(per_head(rows)), each(per_head(n_chunk * width))]
            + [whole((heads, width, width))]
            + [late(spec) for spec in common_specs + [per_head(rows)] * 5 + [chunk_block] * 3 + [per_head(n_chunk * width)]],
            out_specs=[whole(like.shape) for like in grads_like]
            + [late(spec) for spec in [per_head(rows)] * 3 + [per_head(8)] * 3]
            + [whole((16, qkv)), whole((rows, heads)), whole((8, width))],
            out_shape=grads_like + [jax.ShapeDtypeStruct((rows, cols), bf16)] * 3
            + [jax.ShapeDtypeStruct((8, cols), f32)] * 3
            + [jax.ShapeDtypeStruct((16, qkv), bf16), jax.ShapeDtypeStruct((rows, heads), f32), jax.ShapeDtypeStruct((8, width), f32)],
            scratch_shapes=[pltpu.VMEM(p[0].shape, bf16) for p in parts]
            + [pltpu.VMEM((2, rows, 1024) if i == RINGED else p[1].shape, bf16) for i, p in enumerate(parts)]
            + [pltpu.SemaphoreType.DMA((n_prod, 2)), pltpu.SemaphoreType.DMA((2,))]
            + [pltpu.VMEM((model, rows), bf16)]
            + [
                pltpu.VMEM((heads, rows, width), bf16), pltpu.VMEM((heads, n_chunk * width, width), f32),
                pltpu.VMEM((heads, width, width), f32), pltpu.VMEM((heads, width, width), bf16),
                pltpu.VMEM((heads, width, width), bf16),
                pltpu.SemaphoreType.DMA((heads,)), pltpu.SemaphoreType.DMA((heads,)),
            ]
            + [pltpu.VMEM((rows + 8, width), f32)] + [pltpu.VMEM((rows + 16, width), f32)] * 3
            + [pltpu.VMEM((heads, 3, 8, width), f32)] * 2 + [pltpu.VMEM((heads, 3, 16, width), f32)]
            + [pltpu.SemaphoreType.DMA((heads,)), pltpu.SemaphoreType.DMA((heads,))]
            + scratch,
            compiler_params=pltpu.CompilerParams(
                collective_id=1, has_side_effects=True, vmem_limit_bytes=63 << 20, dimension_semantics=("arbitrary",)
            ),
            name="back_scatter",
        )(
            *[p[0] for p in parts], *[p[1] for p in parts], d_head, mixed, gain_h, qt, dt, seg_turned,
            *common, cq, ck, cv, w_s, u_s, t_s, p_s, kk_s, z_s,
        )
        (g_down, g_mlp, g_out), mains, tapped = results[:n_prod], results[n_prod : n_prod + 3], results[n_prod + 3 : n_prod + 6]
        tails, d_logits, d_head_gain = results[n_prod + 6 :]
        d_conv = jnp.concatenate(tapped, axis=1)[:taps_n]
        small = jnp.concatenate(
            [
                jnp.zeros((9, model), f32),
                d_mlp_gain[None],
                d_conv.reshape(-1, model),
                jnp.pad(d_head_gain[0:1], ((0, 0), (0, model - width))),
            ],
            axis=0,
        )
        count = small.shape[0]
        small = jnp.pad(small, ((0, -count % 8), (0, 0)))
        parts = [(xn1, main, "plain", cols_in) for main, cols_in in zip(mains, F_COLS)]
        units, slots, grads_like, scratch = scatter_layout(sizes, parts, None, {"plain": 3})
        vmem = pl.BlockSpec(memory_space=pltpu.VMEM)
        *g_in, small, grad_tokens = pl.pallas_call(
            functools.partial(final_kernel, sizes, units, slots),
            in_specs=[anywhere] * 4 + [vmem] * 7,
            out_specs=[vmem] * 5,
            out_shape=grads_like + [jax.ShapeDtypeStruct(small.shape, f32), jax.ShapeDtypeStruct((rows, model), bf16)],
            scratch_shapes=[pltpu.VMEM((rows, model), bf16)] * 3 + [pltpu.VMEM(w_in.shape, bf16)]
            + [pltpu.VMEM(small.shape, f32), pltpu.VMEM((8, model), f32), pltpu.SemaphoreType.DMA((4,))]
            + [pltpu.VMEM((model, rows), bf16)]
            + [pltpu.VMEM((2 * steps,) + small.shape, f32), pltpu.SemaphoreType.DMA((steps,)), pltpu.SemaphoreType.DMA((steps,))]
            + scratch,
            compiler_params=pltpu.CompilerParams(collective_id=2, has_side_effects=True, vmem_limit_bytes=63 << 20),
            name="final_scatter",
        )(
            *mains, w_in, tails, xn1, tokens, d_hidden_one, norm_gain.astype(f32)[None],
            jnp.pad(d_logits, ((0, 0), (0, 128 - heads))).astype(bf16), small,
        )
        g_in = jnp.concatenate(g_in, axis=1)
        mine = (lax.axis_index("dp") * n_seq + lax.axis_index("seq")) * (model // (n_dp * n_seq))
        g_beta = lax.dynamic_slice(small[:heads], (0, mine), (heads, model // (n_dp * n_seq))).T
        s_norm, s_mlp = small[heads], small[heads + 1]
        s_conv = small[heads + 2 : count - 1].reshape(taps_n, qkv)
        s_head = small[count - 1, :width]
    else:
        do, b_s, seed, d_head_gain = pl.pallas_call(
            functools.partial(seed_kernel, chunk),
            grid=(heads,),
            in_specs=[per_head(rows), per_head(rows), whole((1, width)), per_head(rows), per_head(n_chunk * width)],
            out_specs=[per_head(rows), per_head(n_chunk * width), state_block, whole((8, width))],
            out_shape=[token_like, state_like, jax.ShapeDtypeStruct((heads, width, width), f32), jax.ShapeDtypeStruct((8, width), f32)],
            compiler_params=params,
            name="delta_seed",
        )(d_head, mixed, gain_h, qt, dt)
        grad_end = relay(True, seg_turned, seed, 1)
        outs = pl.pallas_call(
            functools.partial(back_kernel, chunk),
            grid=(heads,),
            in_specs=common_specs + [per_head(rows)] * 5 + [chunk_block] * 3
            + [per_head(n_chunk * width), per_head(rows), per_head(n_chunk * width), per_head(n_chunk * width), state_block],
            out_specs=[per_head(rows)] * 3 + [per_head(8)] * 6 + [whole((rows, heads))],
            out_shape=[token_like] * 3 + [jax.ShapeDtypeStruct((8, cols), f32)] * 6 + [jax.ShapeDtypeStruct((rows, heads), f32)],
            scratch_shapes=[pltpu.VMEM((rows + 8, width), f32)] + [pltpu.VMEM((rows + 16, width), f32)] * 3,
            compiler_params=params,
            name="delta_back",
        )(*common, cq, ck, cv, w_s, u_s, t_s, p_s, kk_s, z_s, do, dt, b_s, grad_end)
        d_main = jnp.concatenate(outs[:3], axis=1)
        d_early = jnp.concatenate(outs[3:6], axis=1)
        d_conv = jnp.concatenate(outs[6:9], axis=1)[:taps_n]
        d_logits = outs[9]
        returned = from_behind(d_early[8 - taps_n + 1 :].astype(bf16), "seq", -1).astype(f32)
        d_projected = d_main + jnp.pad(returned, ((rows - taps_n + 1, 0), (0, 0)))
        d_proj_b = jnp.concatenate(
            [d_projected.astype(bf16), jnp.pad(d_logits.astype(bf16), ((0, 0), (0, 128 - heads)))], axis=1
        )
        d_from_one, d_norm_gain = pull_one(contract_cols(d_proj_b, w_in))
        grad_tokens = (d_hidden_one + d_from_one).astype(bf16)

        d_beta_rows = tn(d_logits.astype(bf16), xn1)
        g_down, g_mlp, g_out, g_in, g_beta = (
            lax.psum_scatter(grad, both, scatter_dimension=0, tiled=True)
            for grad in [contract_rows(left, right) for left, right, _, _ in parts]
            + [contract_rows(xn1, d_proj_b[:, :qkv]), d_beta_rows.T]
        )
        s_norm, s_conv, s_head, s_mlp = lax.psum((d_norm_gain, d_conv, d_head_gain[0], d_mlp_gain), both)
    return (out, grad_tokens, s_norm, g_in, g_beta, s_conv, s_head, g_out, s_mlp, g_mlp, g_down)


def solution(mesh):
    split = P(("dp", "seq"), None)
    placed = (split, P("dp", None), P(), split, split, P(), P(), split, P(), split, split, split)
    return jax.shard_map(
        functools.partial(local, mesh.shape["dp"], mesh.shape["seq"]),
        mesh=mesh,
        in_specs=placed,
        out_specs=(split, split, P(), split, split, P(), P(), split, P(), split, split),
        check_vma=False,
    )
```

```python
import functools

import jax
import jax.numpy as jnp
from jax import lax
from jax.experimental import pallas as pl
from jax.experimental.pallas import tpu as pltpu
from jax.sharding import PartitionSpec as P

norm_eps = 1e-05
unit_eps = 1e-06
MESH = pl.DeviceIdType.MESH
f32, bf16 = jnp.float32, jnp.bfloat16
HIGH = lax.Precision.HIGH
VMEM_LIMIT = 56 << 20
SPARE = 24
TURNS = (0, 1, 5)
RINGED = 1
B_COLS = [(1024, 0)] * 5 + [(512, 0)]
B_ORDER = [2, 3, 4, 0, 5, 1, 6, 8, 7]
TOKEN_TURN = 1
F_COLS = [[(1024, 0)], [(1024, 0)], [(512, 0), (512, 0)]]


def nn(a, b, prec=None):
    return lax.dot_general(a, b, (((1,), (0,)), ((), ())), precision=prec, preferred_element_type=f32)


def nt(a, b, prec=None):
    return lax.dot_general(a, b, (((1,), (1,)), ((), ())), precision=prec, preferred_element_type=f32)


def tn(a, b, prec=None):
    return lax.dot_general(a, b, (((0,), (0,)), ((), ())), precision=prec, preferred_element_type=f32)


def unit_lower_inverses(mats, row, col):
    size = mats[0].shape[0]
    block = min(8, size)
    eye = (row == col).astype(f32)
    near = row // block == col // block
    powers = [jnp.where(near, -a, 0.0) for a in mats]
    inverses = [eye + p for p in powers]
    reach = 2
    while reach < block:
        powers = [nn(p, p, HIGH) for p in powers]
        inverses = [t + nn(t, p, HIGH) for t, p in zip(inverses, powers)]
        reach *= 2
    while block < size:
        pairs = size // (2 * block)

        def lower(m, block=block, pairs=pairs):
            return jnp.concatenate([m[(2 * i + 1) * block : (2 * i + 2) * block] for i in range(pairs)], axis=0)

        def spread(m, fill, block=block, pairs=pairs):
            return jnp.concatenate(
                [x for i in range(pairs) for x in (fill[2 * i * block : (2 * i + 1) * block], m[i * block : (i + 1) * block])],
                axis=0,
            )

        off = (row // (2 * block) == col // (2 * block)) & (row // block == col // block + 1)
        lows = [lower(jnp.where(off, a, 0.0)) for a in mats]
        crossed = [nn(x, t, HIGH) for x, t in zip(lows, inverses)]
        zero = jnp.zeros((size, size), f32)
        below = [lower(t) for t in inverses]
        fixed = [x - nn(x, spread(y, zero), HIGH) for x, y in zip(below, crossed)]
        inverses = [spread(x, t) for x, t in zip(fixed, inverses)]
        block *= 2
    return inverses


def head_column(matrix, head):
    lane = lax.broadcasted_iota(jnp.int32, matrix.shape, 1)
    return jnp.sum(jnp.where(lane == head, matrix, 0.0), axis=1, keepdims=True)


def masks_of(docs_col, docs_row):
    size = docs_col.shape[0]
    row = lax.broadcasted_iota(jnp.int32, (size, size), 0)
    col = lax.broadcasted_iota(jnp.int32, (size, size), 1)
    same = docs_col == docs_row
    return row, col, same


def local_kernel(
    sizes, chunk, gathers, *refs,
):
    far = 1 if gathers else 0
    local_body(
        sizes, chunk, gathers, refs[:gathers], refs[gathers] if far else None, *refs[gathers + far :]
    )


def local_body(
    sizes, chunk, gathers, shards, far_rows, pq, pk, pv, hq, hk, hv, tq, tk, tv, aux, docs_c, docs_r, logits,
    cq, ck, cv, w_o, u_o, qt_o, o_o, t_o, p_o, kk_o, dt_o, ft_o, map_o, turned_o, add_o, *rest,
):
    head = pl.program_id(0)
    turns = TURNS
    if gathers:
        wholes, (halo_o, pad, halo_s, halo_ssem, halo_rsem), sems = rest[:gathers], rest[gathers : gathers + 5], rest[gathers + 5 :]
        segment, heads, span = lax.axis_index("seq"), pl.num_programs(0), pq.shape[1]
        tail = pltpu.make_async_remote_copy(
            src_ref=far_rows.at[pl.ds(pq.shape[0] - 8, 8), pl.ds(0, halo_s.shape[1])], dst_ref=halo_s,
            send_sem=halo_ssem, recv_sem=halo_rsem,
            device_id=(lax.axis_index("dp"), segment + 1), device_id_type=MESH,
        )

        @pl.when(head == 0)
        def _():
            pl.semaphore_wait(
                pltpu.get_barrier_semaphore(), gather_greet(sizes) + relay_greet(sizes[1], False)
            )

            @pl.when(segment < sizes[1] - 1)
            def _():
                tail.start()

        gather_beside(sizes, head, shards, wholes, sems, turns)

        @pl.when(head == 0)
        def _():
            @pl.when(segment == 0)
            def _():
                halo_s[...] = jnp.zeros(halo_s.shape, f32)

            @pl.when(segment > 0)
            def _():
                tail.wait_recv()

            halo_o[...] = halo_s[...]

        @pl.when((head == heads - 1) & (segment < sizes[1] - 1))
        def _():
            tail.wait_send()

        hq, hk, hv = (
            halo_s.at[:, pl.ds(pl.multiple_of((third * heads + head) * span, span), span)] for third in range(3)
        )
    else:
        pad, wholes, sems = rest[0], (), ()
    rows, width = pq.shape
    keeps = (aux[:, 2:3], aux[:, 3:4], aux[:, 4:5])
    acts = []
    for src, halo, taps, dst in ((pq, hq, tq, cq), (pk, hk, tk, ck), (pv, hv, tv, cv)):
        pad[0:8, :] = halo[...]
        pad[8 : 8 + rows, :] = src[...]
        conv = taps[3:4, :] * src[...]
        for back in (1, 2, 3):
            conv = conv + taps[3 - back : 4 - back, :] * (pad[8 - back : 8 - back + rows, :] * keeps[back - 1])
        dst[...] = conv
        acts.append(conv * jax.nn.sigmoid(conv))
    q = acts[0] * (lax.rsqrt(jnp.sum(acts[0] * acts[0], axis=1, keepdims=True) + unit_eps) * width ** (-0.5))
    k = acts[1] * lax.rsqrt(jnp.sum(acts[1] * acts[1], axis=1, keepdims=True) + unit_eps)
    v = acts[2]
    beta = jax.nn.sigmoid(head_column(logits[...], head))
    cont, last = aux[:, 0:1], aux[:, 1:2]
    n_chunk = rows // chunk
    cuts = [slice(c * chunk, (c + 1) * chunk) for c in range(n_chunk)]
    row = lax.broadcasted_iota(jnp.int32, (chunk, chunk), 0)
    col = lax.broadcasted_iota(jnp.int32, (chunk, chunk), 1)
    same = [docs_c[sl, :] == docs_r[:, sl] for sl in cuts]
    kks = [nt(k[sl], k[sl], HIGH) for sl in cuts]
    ps = [jnp.where(m & (row >= col), nt(q[sl], k[sl], HIGH), 0.0) for m, sl in zip(same, cuts)]
    ts = unit_lower_inverses(
        [jnp.where(m & (row > col), beta[sl] * kk, 0.0) for m, sl, kk in zip(same, cuts, kks)], row, col
    )
    rhs = [jnp.concatenate([(beta[sl] * cont[sl]) * k[sl], beta[sl] * v[sl]], axis=1) for sl in cuts]
    wus = [nn(t, r, HIGH) for t, r in zip(ts, rhs)]
    pwus = [nn(p, wu, HIGH) for p, wu in zip(ps, wus)]
    xs = [tn(last[sl] * k[sl], wu, HIGH) for sl, wu in zip(cuts, wus)]
    d_row = lax.broadcasted_iota(jnp.int32, (width, width), 0)
    d_col = lax.broadcasted_iota(jnp.int32, (width, width), 1)
    seg = None
    for c, sl in enumerate(cuts):
        cc = cont[sl]
        dt = jnp.where(d_row == d_col, cc[chunk - 1 : chunk], 0.0) - xs[c][:, :width]
        ft = xs[c][:, width:]
        w_o[sl, :] = wus[c][:, :width]
        u_o[sl, :] = wus[c][:, width:]
        qt_o[sl, :] = cc * q[sl] - pwus[c][:, :width]
        o_o[sl, :] = pwus[c][:, width:]
        t_o[sl, :] = ts[c].astype(bf16)
        p_o[sl, :] = ps[c].astype(bf16)
        kk_o[sl, :] = kks[c]
        dt_o[c * width : (c + 1) * width, :] = dt
        ft_o[c * width : (c + 1) * width, :] = ft
        if seg is None:
            seg = jnp.concatenate([dt, ft], axis=1)
        else:
            seg = nn(dt, seg, HIGH)
            seg = jnp.concatenate([seg[:, :width], seg[:, width:] + ft], axis=1)
    map_o[0] = seg[:, :width]
    turned_o[0] = seg[:, :width].T
    add_o[0] = seg[:, width:]
    gather_rest(sizes, head, shards, wholes, sems, len(turns), pl.num_programs(0) - 1)


def relay_ends(n_seq, back):
    s = lax.axis_index("seq")
    if back:
        return s == n_seq - 1, s == 0, s - 1, s + 1
    return s == 0, s == n_seq - 1, s + 1, s - 1


def relay_greet(n_seq, back):
    d = lax.axis_index("dp")
    first, final, ahead, behind = relay_ends(n_seq, back)
    barrier = pltpu.get_barrier_semaphore()

    @pl.when(jnp.logical_not(first))
    def _():
        pl.semaphore_signal(barrier, inc=1, device_id=(d, behind), device_id_type=MESH)

    @pl.when(jnp.logical_not(final))
    def _():
        pl.semaphore_signal(barrier, inc=1, device_id=(d, ahead), device_id_type=MESH)

    return jnp.where(first | final, 1, 2)


def relay_kernel(n_seq, back, *refs):
    pl.semaphore_wait(pltpu.get_barrier_semaphore(), relay_greet(n_seq, back))
    relay_body(n_seq, back, *refs)


def relay_body(n_seq, back, map_ref, add_ref, out_ref, send, ssem, rsem):
    d = lax.axis_index("dp")
    heads = map_ref.shape[0]
    first, final, ahead, behind = relay_ends(n_seq, back)

    def copy_of(h):
        return pltpu.make_async_remote_copy(
            src_ref=send.at[h], dst_ref=out_ref.at[h], send_sem=ssem.at[h], recv_sem=rsem.at[h],
            device_id=(d, ahead), device_id_type=MESH,
        )

    @pl.when(first)
    def _():
        out_ref[...] = jnp.zeros(out_ref.shape, out_ref.dtype)
        for h in range(heads):
            send[h] = add_ref[h].astype(bf16)
            copy_of(h).start()

    @pl.when(jnp.logical_not(first))
    def _():
        for h in range(heads):
            copy_of(h).wait_recv()
            send[h] = (nn(map_ref[h], out_ref[h].astype(f32), HIGH) + add_ref[h]).astype(bf16)

            @pl.when(jnp.logical_not(final))
            def _():
                copy_of(h).start()

    @pl.when(jnp.logical_not(final))
    def _():
        for h in range(heads):
            copy_of(h).wait_send()


def output_kernel(chunk, zin, dt, ft, qt, o0, gain, z_o, o_o, head_o):
    width = gain.shape[1]
    rows = qt.shape[0]
    sides = [slice(i * width, (i + 1) * width) for i in range(zin.shape[0])]
    states = [zin[i].astype(f32) for i in range(zin.shape[0])]
    for c in range(rows // chunk):
        sl = slice(c * chunk, (c + 1) * chunk)
        ds = slice(c * width, (c + 1) * width)
        for z, side in zip(states, sides):
            z_o[ds, side] = z
        outs = [o0[sl, side] + nn(qt[sl, side], z, HIGH) for z, side in zip(states, sides)]
        if c + 1 < rows // chunk:
            states = [nn(dt[ds, side], z, HIGH) + ft[ds, side] for z, side in zip(states, sides)]
        for o, side in zip(outs, sides):
            o_o[sl, side] = o
            scale = lax.rsqrt(jnp.mean(o * o, axis=1, keepdims=True) + norm_eps)
            head_o[sl, side] = (o * scale * gain[...]).astype(bf16)


def seed_kernel(chunk, *refs):
    seed_body(chunk, pl.program_id(0), *refs)


def seed_body(chunk, head, dh, o, gain, qt, dt, do_o, b_o, seed_o, dgain_o):
    rows, width = qt.shape
    ov, dhv = o[...], dh[...]
    scale = lax.rsqrt(jnp.mean(ov * ov, axis=1, keepdims=True) + norm_eps)
    n = ov * scale
    dg = jnp.sum(dhv * n, axis=0, keepdims=True)
    dgain_o[...] = jnp.where(head == 0, 0.0, dgain_o[...]) + jnp.broadcast_to(dg, dgain_o.shape)
    y = dhv * gain[...]
    do = (y - n * jnp.mean(y * n, axis=1, keepdims=True)) * scale
    do_o[...] = do.astype(do_o.dtype)
    g = None
    for c in reversed(range(rows // chunk)):
        sl = slice(c * chunk, (c + 1) * chunk)
        ds = slice(c * width, (c + 1) * width)
        b_o[ds, :] = tn(qt[sl, :], do[sl], HIGH)
        g = b_o[ds, :] if g is None else tn(dt[ds, :], g, HIGH) + b_o[ds, :]
    seed_o[0] = g


def back_kernel(chunk, *refs):
    back_body(chunk, pl.program_id(0), *refs)


def back_body(
    chunk, head, pq, pk, pv, hq, hk, hv, tq, tk, tv, aux, docs_c, docs_r, logits,
    cq, ck, cv, w_r, u_r, t_r, p_r, kk_r, z_r, do_r, dt_r, b_r, g_r,
    dpq, dpk, dpv, dhq, dhk, dhv, dtq, dtk, dtv, dlogit_o, pad, mask1, mask2, mask3, tails=(None,) * 3,
):
    rows, width = pq.shape
    cont, last = aux[:, 0:1], aux[:, 1:2]
    keeps = (aux[:, 2:3], aux[:, 3:4], aux[:, 4:5])
    scale = width ** (-0.5)
    beta = jax.nn.sigmoid(head_column(logits[...], head))
    sq, sk, sv = (jax.nn.sigmoid(x[...]) for x in (cq, ck, cv))
    aq, ak, v = cq[...] * sq, ck[...] * sk, cv[...] * sv
    iq = lax.rsqrt(jnp.sum(aq * aq, axis=1, keepdims=True) + unit_eps)
    ik = lax.rsqrt(jnp.sum(ak * ak, axis=1, keepdims=True) + unit_eps)
    uq, k = aq * iq, ak * ik
    q = uq * scale
    n_chunk = rows // chunk
    cuts = [slice(c * chunk, (c + 1) * chunk) for c in range(n_chunk)]
    blocks = [slice(c * width, (c + 1) * width) for c in range(n_chunk)]
    gs = [g_r[0].astype(f32)]
    for c in reversed(range(1, n_chunk)):
        gs.insert(0, tn(dt_r[blocks[c], :], gs[0]) + b_r[blocks[c], :])
    row = lax.broadcasted_iota(jnp.int32, (chunk, chunk), 0)
    col = lax.broadcasted_iota(jnp.int32, (chunk, chunk), 1)
    same = [docs_c[sl, :] == docs_r[:, sl] for sl in cuts]
    ks = [k[sl].astype(bf16) for sl in cuts]
    dos = [do_r[sl, :].astype(bf16) for sl in cuts]
    zs = [z_r[ds, :].astype(bf16) for ds in blocks]
    gbs = [g.astype(bf16) for g in gs]
    wkzs = [
        nn(jnp.concatenate([w_r[sl, :], k[sl]], axis=0), z_r[ds, :], HIGH) for sl, ds in zip(cuts, blocks)
    ]
    us = [(u_r[sl, :] - x[:chunk]).astype(bf16) for sl, x in zip(cuts, wkzs)]
    dus = [tn(p_r[sl, :].astype(bf16), do) for sl, do in zip(cuts, dos)]
    dus = [x + nn((last[sl] * k[sl]).astype(bf16), g) for x, sl, g in zip(dus, cuts, gbs)]
    drs = [tn(t_r[sl, :].astype(bf16), x.astype(bf16)) for sl, x in zip(cuts, dus)]
    ys = [
        nt(jnp.concatenate([do, dr.astype(bf16)], axis=0), jnp.concatenate([u, z], axis=0))
        for do, dr, u, z in zip(dos, drs, us, zs)
    ]
    dps = [jnp.where(m & (row >= col), y[:chunk, :chunk], 0.0) for m, y in zip(same, ys)]
    das = [jnp.where(m & (row > col), -y[chunk:, :chunk], 0.0) for m, y in zip(same, ys)]
    pbs = [
        jnp.concatenate([dp, beta[sl] * da], axis=0).astype(bf16) for dp, da, sl in zip(dps, das, cuts)
    ]
    paks = [nn(pb, kc) for pb, kc in zip(pbs, ks)]
    turns = [
        tn(pb, jnp.concatenate([q[sl].astype(bf16), kc], axis=0)) for pb, sl, kc in zip(pbs, cuts, ks)
    ]
    ugs = [nt(u, g) for u, g in zip(us, gbs)]
    dq = jnp.concatenate([cont[sl] * y[:chunk, chunk:] + x[:chunk] for sl, y, x in zip(cuts, ys, paks)], axis=0)
    dk = jnp.concatenate(
        [
            t + x[chunk:] + last[sl] * ug - (beta[sl] * cont[sl]) * y[chunk:, chunk:]
            for t, x, sl, ug, y in zip(turns, paks, cuts, ugs, ys)
        ],
        axis=0,
    )
    dv = jnp.concatenate([beta[sl] * dr for sl, dr in zip(cuts, drs)], axis=0)
    db = jnp.concatenate(
        [
            jnp.sum(dr * (v[sl] - cont[sl] * x[chunk:]), axis=1, keepdims=True)
            + jnp.sum(da * kk_r[sl, :], axis=1, keepdims=True)
            for dr, sl, x, da in zip(drs, cuts, wkzs, das)
        ],
        axis=0,
    )
    lane = lax.broadcasted_iota(jnp.int32, dlogit_o.shape, 1)
    dlogit_o[...] = jnp.where(lane == head, db * beta * (1.0 - beta), jnp.where(head == 0, 0.0, dlogit_o[...]))
    du_q = dq * scale
    da_q = (du_q - uq * jnp.sum(uq * du_q, axis=1, keepdims=True)) * iq
    da_k = (dk - k * jnp.sum(k * dk, axis=1, keepdims=True)) * ik
    for dact, sg, c_r, src, halo, taps, dst, dhalo, dtaps, tail in (
        (da_q, sq, cq, pq, hq, tq, dpq, dhq, dtq, tails[0]),
        (da_k, sk, ck, pk, hk, tk, dpk, dhk, dtk, tails[1]),
        (dv, sv, cv, pv, hv, tv, dpv, dhv, dtv, tails[2]),
    ):
        dconv = dact * (sg * (1.0 + c_r[...] * (1.0 - sg)))
        pad[0:8, :] = halo[...]
        pad[8 : 8 + rows, :] = src[...]
        zero = jnp.zeros((8, width), f32)
        total = taps[3:4, :] * dconv
        early = zero
        gtaps = [None] * 4
        gtaps[3] = jnp.sum(dconv * src[...], axis=0, keepdims=True)
        for back, mask in ((1, mask1), (2, mask2), (3, mask3)):
            kept = dconv * keeps[back - 1]
            gtaps[3 - back] = jnp.sum(kept * pad[8 - back : 8 - back + rows, :], axis=0, keepdims=True)
            mask[0:8, :] = zero
            mask[8 : 8 + rows, :] = kept
            mask[8 + rows : 16 + rows, :] = zero
            total = total + taps[3 - back : 4 - back, :] * mask[8 + back : 8 + back + rows, :]
            early = early + taps[3 - back : 4 - back, :] * mask[back : back + 8, :]
        dst[...] = total.astype(dst.dtype)
        dhalo[...] = early
        if tail is not None:
            tail[...] = total[rows - 16 :]
        dtaps[...] = jnp.concatenate(gtaps + [jnp.zeros((4, width), f32)], axis=0)


def bit_orders(n_dp, n_seq):
    dp_bits = [("dp", i) for i in range(n_dp.bit_length() - 1)]
    seq_bits = [("seq", i) for i in range(n_seq.bit_length() - 1)]
    return (
        seq_bits[:1] + dp_bits + seq_bits[1:],
        seq_bits[:1] + dp_bits[::-1] + seq_bits[1:],
        seq_bits + dp_bits,
        seq_bits + dp_bits[::-1],
    )


def scatter_steps(sizes, units, slots, lefts, rights, outs, scratch, turned=()):
    n_dp, n_seq = sizes
    scratch = list(scratch)
    orders = bit_orders(n_dp, n_seq)
    steps = len(orders[0])
    pool = [scratch.pop(0) for _ in range(2 * (1 + max(slots)))]
    own = [pool[2 * slots[u] + half] for u in range(len(units)) for half in (0, 1)]
    before = [max([w for w in range(u) if slots[w] == slots[u]], default=None) for u in range(len(units))]
    got = [[scratch.pop(0) for _ in range(steps)] for _ in range(2 * len(units))]
    ssem, rsem = scratch
    index = {"dp": lax.axis_index("dp"), "seq": lax.axis_index("seq")}

    def bit_of(axis, bit):
        return (index[axis] // 2**bit) % 2

    def partner(axis, bit):
        other = dict(index)
        other[axis] = index[axis] + (1 - 2 * bit_of(axis, bit)) * 2**bit
        return (other["dp"], other["seq"])

    def greet():
        for axis, bit in orders[0]:
            pl.semaphore_signal(
                pltpu.get_barrier_semaphore(), inc=1, device_id=partner(axis, bit), device_id_type=MESH
            )
        return steps

    def weights(order):
        return {key: 2 ** (steps - 1 - i) for i, key in enumerate(order)}

    def place(order, axis, value):
        w = weights(order)
        return sum(((value // 2**b) % 2) * w[(a, b)] for a, b in order if a == axis)

    def compute(u):
        kind, li, _, _, cols, _, _, first_order = units[u]
        left, (right, first) = lefts[li], rights(u)
        block = left.shape[0 if li in turned else 1] // (n_dp * n_seq)
        together = n_seq
        while together * block % 128:
            together *= 2
        half_cols = cols // 2

        def rows_of(m, carry):
            span = pl.ds(pl.multiple_of(m * (together * block), 128), together * block)
            some = right[:, first : first + cols]
            tile = nn(left[span, :], some) if li in turned else tn(left[:, span], some)
            for half in (0, 1):
                order, buf = orders[first_order + half], own[2 * u + half]
                for j in range(together):
                    piece = tile[j * block : (j + 1) * block, half * half_cols : (half + 1) * half_cols]
                    if kind == "stack":
                        piece = jnp.concatenate([piece[:, : cols // 4], piece[:, cols // 4 :]], axis=0)
                    base = place(order, "dp", m * (together // n_seq) + j // n_seq)
                    buf[base + place(order, "seq", j % n_seq)] = piece.astype(bf16)
            return carry

        lax.fori_loop(0, n_dp * n_seq // together, rows_of, 0)

    def copy_of(u, half, k):
        src = own[2 * u + half] if k == 0 else got[2 * u + half][k - 1]
        dst = got[2 * u + half][k]
        axis, bit = orders[units[u][7] + half][k]
        count = dst.shape[0]
        return pltpu.make_async_remote_copy(
            src_ref=src.at[pl.ds((1 - bit_of(axis, bit)) * count, count)], dst_ref=dst,
            send_sem=ssem.at[u, half, k], recv_sem=rsem.at[u, half, k],
            device_id=partner(axis, bit), device_id_type=MESH,
        )

    def merge(u, half, k):
        src = own[2 * u + half] if k == 0 else got[2 * u + half][k - 1]
        dst = got[2 * u + half][k]
        axis, bit = orders[units[u][7] + half][k]
        count = dst.shape[0]
        mine = bit_of(axis, bit) * count
        copy_of(u, half, k).wait_recv()
        if k < steps - 1:
            def add(i, carry):
                dst[i] = dst[i] + src[mine + i]
                return carry

            lax.fori_loop(0, count, add, 0)
            copy_of(u, half, k + 1).start()
        else:
            kind, _, _, first, cols, oi, to, _ = units[u]
            total = dst[0].astype(f32) + src[mine].astype(f32)
            start, wide = to + half * (cols // 2), cols // 2
            if kind == "stack":
                block = total.shape[0] // 2
                outs[oi][:, start : start + wide // 2] = total[:block]
                outs[oi][:, start + wide // 2 : start + wide] = total[block:]
            else:
                outs[oi][:, start : start + wide] = total

    def begin(u):
        if before[u] is not None:
            for half in (0, 1):
                copy_of(before[u], half, 0).wait_send()
        compute(u)
        for half in (0, 1):
            copy_of(u, half, 0).start()

    def both_merge(u, k):
        for half in (0, 1):
            merge(u, half, k)

    def finish():
        for k in range(steps):
            for u in range(len(units)):
                if k > 0 or u not in before:
                    for half in (0, 1):
                        copy_of(u, half, k).wait_send()

    return steps, partner, greet, begin, both_merge, finish


def turn_over(src, dst):
    span = 256

    def some(i, carry):
        at = pl.ds(pl.multiple_of(i * span, span), span)
        dst[at, :] = src[:, at].T
        return carry

    lax.fori_loop(0, src.shape[1] // span, some, 0)


def small_steps(sizes, partner, small_in, small_out, small_got, small_ssem, small_rsem):
    order = bit_orders(*sizes)[0]
    steps = len(order)

    def small_copy(k):
        return pltpu.make_async_remote_copy(
            src_ref=small_in if k == 0 else small_got.at[steps + k - 1], dst_ref=small_got.at[k],
            send_sem=small_ssem.at[k], recv_sem=small_rsem.at[k],
            device_id=partner(*order[k]), device_id_type=MESH,
        )

    def small_step(k):
        small_copy(k).wait_recv()
        mine = small_in[...] if k == 0 else small_got[steps + k - 1]
        if k < steps - 1:
            small_got[steps + k] = small_got[k] + mine
            small_copy(k + 1).start()
        else:
            small_out[...] = small_got[k] + mine

    def small_finish():
        for k in range(steps):
            small_copy(k).wait_send()

    return small_copy(0).start, small_step, small_finish


def scatter_layout(sizes, products, order, keep):
    n = sizes[0] * sizes[1]
    steps = n.bit_length() - 1
    units, outs = [], []
    for oi, (left, right, kind, cols) in enumerate(products):
        block = left.shape[1] // n
        outs.append(jax.ShapeDtypeStruct((block, right.shape[1]), f32))
        first = 0
        for wide, first_order in cols:
            units.append((kind, oi, oi, first, wide, oi, first, first_order))
            first += wide
    units = [units[i] for i in order or range(len(units))]
    shapes = []
    for kind, oi, _, _, wide, _, _, _ in units:
        block = outs[oi].shape[0]
        shapes.append((2 * block, wide // 4) if kind == "stack" else (block, wide // 2))
    pool, slots = [], []
    for u, shape in enumerate(shapes):
        alike = [i for i, kept in enumerate(pool) if kept == shape]
        if len(alike) < keep[units[u][0]]:
            slots.append(len(pool))
            pool.append(shape)
        else:
            used = [max(w for w in range(u) if slots[w] == i) for i in alike]
            slots.append(alike[used.index(min(used))])
    own = [pltpu.VMEM((n,) + s, bf16) for s in pool for _ in (0, 1)]
    got = [pltpu.VMEM((n >> (k + 1),) + s, bf16) for s in shapes for _ in (0, 1) for k in range(steps)]
    sems = pltpu.SemaphoreType.DMA((len(units), 2, steps))
    return units, slots, outs, own + got + [sems, sems]


def back_scatter_kernel(sizes, chunk, heads, units, slots, plan, n_prod, *refs):
    turn = pl.program_id(0)
    refs = list(refs)

    def take(count):
        got = refs[:count]
        del refs[:count]
        return got

    far_lefts, far_rights = take(n_prod), take(n_prod)
    dh, o, gain, qt, dt, turned = take(6)
    common, saved = take(13), take(9)
    outs, mains, tapped, tail_o, dlogit, dgain = take(n_prod), take(3), take(3), *take(3)
    lefts, rights, fetch, ring_sem, turn_s = take(n_prod), take(n_prod), *take(3)
    do_s, b_s, seed_s, g_s, send, relay_ssem, relay_rsem = take(7)
    pads = take(4)
    early_s, late_s, tail_s, halo_ssem, halo_rsem = take(5)
    ringed = [u for u, unit in enumerate(units) if unit[1] == RINGED]

    def right_of(u):
        if u in ringed:
            return rights[RINGED].at[ringed.index(u) % 2], 0
        return rights[units[u][2]], units[u][3]

    def ring_fetch(place):
        _, _, ri, first, wide, _, _, _ = units[ringed[place]]
        return pltpu.make_async_copy(
            far_rights[ri].at[:, pl.ds(first, wide)],
            rights[ri].at[place % 2, :, pl.ds(0, wide)],
            ring_sem.at[place % 2],
        )

    steps, partner, greet, begin, merge, finish = scatter_steps(
        sizes, units, slots, [turn_s if i == RINGED else left for i, left in enumerate(lefts)],
        right_of, outs, refs, (RINGED,),
    )

    def fetches(i):
        copies = [pltpu.make_async_copy(far_lefts[i], lefts[i], fetch.at[i, 0])]
        if i != RINGED:
            copies.append(pltpu.make_async_copy(far_rights[i], rights[i], fetch.at[i, 1]))
        return copies

    segment = lax.axis_index("seq")

    def halo_copy(head):
        return pltpu.make_async_remote_copy(
            src_ref=early_s.at[head], dst_ref=late_s.at[head], send_sem=halo_ssem.at[head], recv_sem=halo_rsem.at[head],
            device_id=(lax.axis_index("dp"), segment - 1), device_id_type=MESH,
        )

    seen = [unit[1] for unit in units]
    arrival = sorted(range(n_prod), key=seen.index)

    @pl.when(turn == 0)
    def _():
        for i in arrival:
            for copy in fetches(i):
                copy.start()
        for place in (0, 1):
            ring_fetch(place).start()
        pl.semaphore_wait(pltpu.get_barrier_semaphore(), greet() + relay_greet(sizes[1], True))

    @pl.when(turn < heads)
    def _():
        seed_body(
            chunk, turn, dh, o, gain, qt, dt, do_s.at[turn], b_s.at[turn], seed_s.at[pl.ds(turn, 1)], dgain
        )

    @pl.when(turn == heads)
    def _():
        relay_body(sizes[1], True, turned, seed_s, g_s, send, relay_ssem, relay_rsem)

    for t, events in enumerate(plan):
        if events:
            @pl.when(turn == t)
            def _(events=events):
                for u, k in events:
                    if k < 0:
                        if seen.index(seen[u]) == u:
                            for copy in fetches(seen[u]):
                                copy.wait()
                            if seen[u] == RINGED:
                                turn_over(lefts[RINGED], turn_s)
                        if u in ringed:
                            ring_fetch(ringed.index(u)).wait()
                        begin(u)
                        if u in ringed and ringed.index(u) + 2 < len(ringed):
                            ring_fetch(ringed.index(u) + 2).start()
                    else:
                        merge(u, k)

    @pl.when(turn >= heads)
    def _():
        head = turn - heads
        back_body(
            chunk, head, *common, *saved, do_s.at[head], dt, b_s.at[head], g_s.at[pl.ds(head, 1)],
            *mains, *[early_s.at[head, third] for third in range(3)], *tapped, dlogit, *pads,
            tails=[tail_s.at[head, third] for third in range(3)],
        )

        @pl.when(segment > 0)
        def _():
            halo_copy(head).start()

    @pl.when(turn == 2 * heads - 1)
    def _():
        width = late_s.shape[3]

        @pl.when(segment == sizes[1] - 1)
        def _():
            late_s[...] = jnp.zeros(late_s.shape, f32)

        @pl.when(segment < sizes[1] - 1)
        def _():
            for head in range(heads):
                halo_copy(head).wait_recv()

        for head in range(heads):
            for third in range(3):
                tail = tail_s[head, third]
                tail = jnp.concatenate([tail[:8], tail[8:] + late_s[head, third]], axis=0)
                tail_o[:, (third * heads + head) * width : (third * heads + head + 1) * width] = tail.astype(bf16)

        @pl.when(segment > 0)
        def _():
            for head in range(heads):
                halo_copy(head).wait_send()

        finish()


def final_kernel(sizes, units, slots, *refs):
    refs = list(refs)

    def take(count):
        got = refs[:count]
        del refs[:count]
        return got

    far, (far_w, tails, xn1, tokens, d_one, gain, dlogit, small_in) = take(3), take(8)
    outs, (small_out, grad_o) = take(3), take(2)
    rights, (weight, small_s, gain_s, fetch, turn_s) = take(3), take(5)
    small_scratch = take(3)
    rows, model = xn1.shape
    steps, partner, greet, begin, merge, finish = scatter_steps(
        sizes, units, slots, [turn_s] * 3, lambda u: (rights[units[u][2]], units[u][3]), outs, refs, (0, 1, 2)
    )
    small_start, small_step, small_finish = small_steps(sizes, partner, small_s, small_out, *small_scratch)
    fetches = [pltpu.make_async_copy(a, b, fetch.at[i]) for i, (a, b) in enumerate(zip(far + [far_w], rights + [weight]))]
    for copy in fetches:
        copy.start()
    turn_over(xn1, turn_s)
    pl.semaphore_wait(pltpu.get_barrier_semaphore(), greet())
    small_s[...] = small_in[...]
    small_s[0:8, :] = tn(dlogit[...], xn1[...])[0:8]

    def token_grads():
        part = rows // 2
        fetches[3].wait()
        gain_s[...] = jnp.zeros(gain_s.shape, f32)

        def some(i, carry):
            at = pl.ds(pl.multiple_of(i * part, 16), part)
            dx = nt(dlogit[at, :], weight[:, 3 * model :])
            for third in range(3):
                dx = dx + nt(rights[third][at, :], weight[:, third * model : (third + 1) * model])
            x = tokens[at, :].astype(f32)
            scale = lax.rsqrt(jnp.mean(x * x, axis=1, keepdims=True) + norm_eps)
            n = x * scale
            gain_s[0:1, :] += jnp.sum(dx * n, axis=0, keepdims=True)
            y = dx * gain[...]
            dz = (y - n * jnp.mean(y * n, axis=1, keepdims=True)) * scale
            grad_o[at, :] = (d_one[at, :] + dz).astype(bf16)
            return carry

        lax.fori_loop(0, 2, some, 0)
        small_s[8:9, :] = gain_s[0:1, :]

    seen = [unit[2] for unit in units]
    for t in range(len(units) + steps):
        for k in range(steps):
            if 0 <= t - 1 - k < len(units):
                merge(t - 1 - k, k)
        if t < len(units):
            third = seen[t]
            if seen.index(third) == t and third not in seen[: TOKEN_TURN + 1][:t] and (t <= TOKEN_TURN):
                fetches[third].wait()
                rights[third][rows - 16 :, :] = tails[:, third * model : (third + 1) * model]
            begin(t)
        if t == len(units) - 1:
            small_start()
        if 0 <= t - len(units) < steps:
            small_step(t - len(units))
        if t == TOKEN_TURN:
            for copy in fetches[max(seen[: t + 1]) + 1 : 3]:
                copy.wait()
            for third in range(max(seen[: t + 1]) + 1, 3):
                rights[third][rows - 16 :, :] = tails[:, third * model : (third + 1) * model]
            token_grads()
    finish()
    small_finish()


def back_plan(n_units, steps, heads, early):
    plan = [[] for _ in range(2 * heads)]
    for i in range(n_units + steps):
        turn = 2 * i if i <= early else heads + i - early - 1
        turn = min(turn, 2 * heads - 1)
        for k in range(steps):
            if 0 <= i - 1 - k < n_units and not (i == early + 1 and k == 0):
                plan[turn].append((i - 1 - k, k))
        if i < n_units:
            plan[turn].append((i, -1))
        if i == early:
            plan[heads - 1].append((early, 0))
    return plan


def gather_parts(shape):
    rows, cols = shape
    half = rows // 2
    spare = cols * SPARE // 100 // 128 * 128 if cols >= 2048 else 0
    parts = [(i * half, half, 0, cols - spare) for i in (0, 1)]
    if spare:
        parts += [(i * half, half, cols - spare, spare) for i in (0, 1)]
    return parts


def gather_steps(sizes, shard, whole, own_sem, ssem, rsem):
    n_dp, n_seq = sizes
    index = {"dp": lax.axis_index("dp"), "seq": lax.axis_index("seq")}
    orders = [order[::-1] for order in bit_orders(n_dp, n_seq)]
    steps = len(orders[0])
    parts = gather_parts(shard.shape)

    def flipped(keys):
        other = dict(index)
        for axis, bit in keys:
            other[axis] = other[axis] + (1 - 2 * ((index[axis] // 2**bit) % 2)) * 2**bit
        return (other["dp"], other["seq"])

    def half_of(ref, half):
        top, height, left, wide = parts[half]
        return ref.at[pl.ds(top, height), pl.ds(left, wide)]

    def copy_of(half, path, k):
        order = orders[half]
        dp, seq = flipped([order[i] for i in path])
        dst = half_of(whole.at[dp * n_seq + seq], half)
        code = sum(2**i for i in path) + 2**k
        return pltpu.make_async_remote_copy(
            src_ref=dst if path else half_of(shard, half), dst_ref=dst,
            send_sem=ssem.at[half, code], recv_sem=rsem.at[half, code],
            device_id=flipped([order[k]]), device_id_type=MESH,
        )

    paths = sorted(
        (tuple(i for i in range(steps) if code >> i & 1) for code in range(2**steps)), key=lambda p: (len(p), p)
    )
    keep = pltpu.make_async_copy(shard, whole.at[index["dp"] * n_seq + index["seq"]], own_sem)

    def greet():
        barrier = pltpu.get_barrier_semaphore()
        for key in orders[0]:
            pl.semaphore_signal(barrier, inc=1, device_id=flipped([key]), device_id_type=MESH)
        return steps

    def level(hops):
        if hops == 0:
            keep.start()
        for path in paths:
            if len(path) == hops:
                for half in range(len(parts)):
                    if path:
                        copy_of(half, path[:-1], path[-1]).wait_recv()
                    for k in range((path[-1] if path else -1) + 1, steps):
                        copy_of(half, path, k).start()

    def finish():
        for path in paths:
            if path:
                for half in range(len(parts)):
                    copy_of(half, path[:-1], path[-1]).wait_send()
        keep.wait()

    return steps, greet, level, finish


def gather_kernel(sizes, shard, whole, *sems):
    steps, greet, level, finish = gather_steps(sizes, shard, whole, *sems)
    pl.semaphore_wait(pltpu.get_barrier_semaphore(), greet())
    for hops in range(steps + 1):
        level(hops)
    finish()


def gather_greet(sizes):
    index = {"dp": lax.axis_index("dp"), "seq": lax.axis_index("seq")}
    order = bit_orders(*sizes)[0]
    for axis, bit in order:
        other = dict(index)
        other[axis] = index[axis] + (1 - 2 * ((index[axis] // 2**bit) % 2)) * 2**bit
        pl.semaphore_signal(
            pltpu.get_barrier_semaphore(), inc=1, device_id=(other["dp"], other["seq"]), device_id_type=MESH
        )
    return len(order)


def gather_beside(sizes, turn, shards, wholes, sems, turns):
    plans = [
        gather_steps(sizes, shard, whole, *sems[3 * i : 3 * i + 3])
        for i, (shard, whole) in enumerate(zip(shards, wholes))
    ]
    if not plans:
        return
    for hops, when in enumerate(turns):
        @pl.when(turn == when)
        def _(hops=hops):
            for plan in plans:
                plan[2](hops)


def gather_rest(sizes, turn, shards, wholes, sems, done, final):
    plans = [
        gather_steps(sizes, shard, whole, *sems[3 * i : 3 * i + 3])
        for i, (shard, whole) in enumerate(zip(shards, wholes))
    ]
    if not plans:
        return

    @pl.when(turn == final)
    def _():
        for hops in range(done, plans[0][0] + 1):
            for plan in plans:
                plan[2](hops)
        for plan in plans:
            plan[3]()


def gather_sems(sizes, shard):
    sems = pltpu.SemaphoreType.DMA((len(gather_parts(shard.shape)), sizes[0] * sizes[1]))
    return [pltpu.SemaphoreType.DMA, sems, sems]


def whole_like(sizes, shard):
    return jax.ShapeDtypeStruct((sizes[0] * sizes[1],) + shard.shape, shard.dtype)


def flat_rows(whole):
    return whole.reshape((whole.shape[0] * whole.shape[1],) + whole.shape[2:])


def gather_rows(sizes, shard, cid):
    anywhere = pl.BlockSpec(memory_space=pl.ANY)
    whole = pl.pallas_call(
        functools.partial(gather_kernel, sizes),
        in_specs=[anywhere],
        out_specs=anywhere,
        out_shape=whole_like(sizes, shard),
        scratch_shapes=gather_sems(sizes, shard),
        compiler_params=pltpu.CompilerParams(collective_id=cid, has_side_effects=True),
        name="gather_rows",
    )(shard)
    return flat_rows(whole)


def from_behind(value, axis, steps):
    count = lax.axis_size(axis)
    first, last = (max(0, -steps), min(count, count - steps))
    return lax.ppermute(value, axis, [(source, source + steps) for source in range(first, last)])


def rms_scale(values, gain):
    return values * lax.rsqrt(jnp.mean(values * values, axis=-1, keepdims=True) + norm_eps) * gain


def doc_ids(lengths, positions):
    ends = jnp.cumsum(lengths)
    inside = (positions[:, None] >= ends[None, :]).astype(jnp.int32)
    return jnp.where(positions >= 0, jnp.sum(inside, axis=1), -1)


def contract_rows(left, right):
    return tn(left, right)


def contract_cols(left, right):
    return nt(left, right)


def local(
    n_dp, n_seq, tokens, doc_lengths, norm_gain, w_qkv, w_beta, conv_weight, head_gain, w_out, mlp_gain, w_mlp_in, w_down, grad_out,
):
    rows, model = tokens.shape
    heads = w_beta.shape[1]
    width = head_gain.shape[0]
    taps_n = conv_weight.shape[0]
    qkv = w_qkv.shape[1]
    chunk = min(128, rows)
    n_chunk = rows // chunk
    both = ("dp", "seq")

    sizes = (n_dp, n_seq)
    own_kernels = (model // (n_dp * n_seq)) % 32 == 0 and heads > (n_dp * n_seq).bit_length()
    w_d = lax.all_gather(w_down, both, axis=0, tiled=True)
    w_in = jnp.concatenate([w_qkv, jnp.pad(w_beta, ((0, 0), (0, 128 - heads)))], axis=1)
    if own_kernels:
        beside = [w_mlp_in]
        w_o = lax.all_gather(w_out, both, axis=0, tiled=True)
        w_in = gather_rows(sizes, w_in, 3)
    else:
        beside = []
        w_in, w_o, w_m = (lax.all_gather(w, both, axis=0, tiled=True) for w in (w_in, w_out, w_mlp_in))

    inputs = tokens.astype(f32)
    norm_one, pull_one = jax.vjp(rms_scale, inputs, norm_gain.astype(f32))
    xn1 = norm_one.astype(bf16)
    projected = nn(xn1, w_in)
    logits = projected[:, qkv : qkv + heads]
    start = lax.axis_index("seq") * rows
    docs_pad = doc_ids(doc_lengths[0], start - taps_n + 1 + jnp.arange(rows + taps_n - 1, dtype=jnp.int32))
    docs = docs_pad[taps_n - 1 :]
    by_chunk = docs.reshape(n_chunk, chunk)
    before = docs_pad[taps_n - 2 : taps_n - 2 + rows].reshape(n_chunk, chunk)[:, :1]
    aux = jnp.stack(
        [(by_chunk == before).reshape(-1), (by_chunk == by_chunk[:, -1:]).reshape(-1)]
        + [docs_pad[taps_n - 1 - b : taps_n - 1 - b + rows] == docs for b in (1, 2, 3)]
        + [docs < -5] * 3,
        axis=1,
    ).astype(f32)
    docs_c, docs_r = docs[:, None], docs[None, :]
    if own_kernels:
        halo = jnp.zeros((8, qkv), f32)
    else:
        received = from_behind(projected[rows - taps_n + 1 :, :qkv].astype(bf16), "seq", 1).astype(f32)
        halo = jnp.pad(received, ((8 - taps_n + 1, 0), (0, 0)))
    taps = jnp.pad(conv_weight.astype(f32), ((0, 8 - taps_n), (0, 0)))

    def third(block_rows):
        return [pl.BlockSpec((block_rows, width), lambda h, t=t: (0, t * heads + h)) for t in range(3)]

    def per_head(block_rows):
        return pl.BlockSpec((block_rows, width), lambda h: (0, h))

    def whole(shape):
        return pl.BlockSpec(shape, lambda h: (0,) * len(shape))

    state_block = pl.BlockSpec((1, width, width), lambda h: (h, 0, 0))
    params = pltpu.CompilerParams(vmem_limit_bytes=VMEM_LIMIT, dimension_semantics=("arbitrary",))
    cols = heads * width
    token_like = jax.ShapeDtypeStruct((rows, cols), f32)
    chunk_like = jax.ShapeDtypeStruct((rows, heads * chunk), f32)
    state_like = jax.ShapeDtypeStruct((n_chunk * width, cols), f32)
    common_specs = (
        third(rows) + third(8) + third(8)
        + [whole((rows, 8)), whole((rows, 1)), whole((1, rows)), whole((rows, heads))]
    )
    common = (projected,) * 3 + (halo,) * 3 + (taps,) * 3 + (aux, docs_c, docs_r, logits)
    chunk_block = pl.BlockSpec((rows, chunk), lambda h: (0, h))
    anywhere = pl.BlockSpec(memory_space=pl.ANY)
    maps_like = jax.ShapeDtypeStruct((heads, width, width), f32)
    cq, ck, cv, w_s, u_s, qt, o0, t_s, p_s, kk_s, dt, ft, seg_map, seg_turned, seg_add, *wholes = pl.pallas_call(
        functools.partial(local_kernel, sizes, chunk, len(beside)),
        grid=(heads,),
        in_specs=[anywhere] * (len(beside) + bool(beside)) + common_specs,
        out_specs=[per_head(rows)] * 7 + [chunk_block] * 3 + [per_head(n_chunk * width)] * 2 + [state_block] * 3
        + [anywhere] * len(beside) + ([whole((8, qkv))] if beside else []),
        out_shape=[token_like] * 7
        + [jax.ShapeDtypeStruct((rows, heads * chunk), bf16)] * 2 + [chunk_like] + [state_like] * 2 + [maps_like] * 3
        + [whole_like(sizes, w) for w in beside] + ([jax.ShapeDtypeStruct((8, qkv), f32)] if beside else []),
        scratch_shapes=[pltpu.VMEM((rows + 8, width), f32)]
        + ([pltpu.VMEM((8, qkv), f32), pltpu.SemaphoreType.DMA, pltpu.SemaphoreType.DMA] if beside else [])
        + [sem for w in beside for sem in gather_sems(sizes, w)],
        compiler_params=pltpu.CompilerParams(
            vmem_limit_bytes=VMEM_LIMIT, dimension_semantics=("arbitrary",),
            **(dict(collective_id=4, has_side_effects=True) if beside else {}),
        ),
        name="delta_local",
    )(*beside, *([projected] if beside else []), *common)
    if beside:
        *wholes, halo = wholes
        common = common[:3] + (halo,) * 3 + common[6:]
        (w_m,) = (flat_rows(w) for w in wholes)

    def relay(back, maps, adds, cid):
        return pl.pallas_call(
            functools.partial(relay_kernel, n_seq, back),
            in_specs=[pl.BlockSpec(memory_space=pltpu.VMEM)] * 2,
            out_specs=pl.BlockSpec(memory_space=pltpu.VMEM),
            out_shape=jax.ShapeDtypeStruct((heads, width, width), bf16),
            scratch_shapes=[
                pltpu.VMEM((heads, width, width), bf16),
                pltpu.SemaphoreType.DMA((heads,)),
                pltpu.SemaphoreType.DMA((heads,)),
            ],
            compiler_params=pltpu.CompilerParams(collective_id=cid, has_side_effects=True, vmem_limit_bytes=VMEM_LIMIT),
            name="relay_back" if back else "relay",
        )(maps, adds)

    state_in = relay(False, seg_map, seg_add, 0)
    gain_h = head_gain.astype(f32)[None, :]
    some = 2 if heads % 2 == 0 else 1

    def several(block_rows):
        return pl.BlockSpec((block_rows, some * width), lambda h: (0, h))

    z_s, mixed, head_out = pl.pallas_call(
        functools.partial(output_kernel, chunk),
        grid=(heads // some,),
        in_specs=[pl.BlockSpec((some, width, width), lambda h: (h, 0, 0))]
        + [several(n_chunk * width)] * 2 + [several(rows)] * 2 + [whole((1, width))],
        out_specs=[several(n_chunk * width), several(rows), several(rows)],
        out_shape=[state_like, token_like, jax.ShapeDtypeStruct((rows, cols), bf16)],
        compiler_params=params,
        name="delta_out",
    )(state_in, dt, ft, qt, o0, gain_h)

    hidden_one = inputs + nn(head_out, w_o)
    norm_two, pull_two = jax.vjp(rms_scale, hidden_one, mlp_gain.astype(f32))
    xn2 = norm_two.astype(bf16)
    gate_up = nn(xn2, w_m)
    inner = gate_up.shape[1] // 2
    gate, up = gate_up[:, :inner].astype(f32), gate_up[:, inner:].astype(f32)
    open_gate = jax.nn.sigmoid(gate)
    hidden = (gate * open_gate * up).astype(bf16)
    out = (hidden_one + nn(hidden, w_d)).astype(bf16)

    grad_in = grad_out.astype(f32)
    d_hidden = contract_cols(grad_out, w_d)
    d_gate = (d_hidden * up * (open_gate * (1.0 + gate * (1.0 - open_gate)))).astype(bf16)
    d_up = (d_hidden * (gate * open_gate)).astype(bf16)
    d_gate_up = jnp.concatenate([d_gate, d_up], axis=1)
    d_from_two, d_mlp_gain = pull_two(contract_cols(d_gate_up, w_m))
    d_hidden_one = grad_in + d_from_two
    d_att = d_hidden_one.astype(bf16)
    d_head = contract_cols(d_att, w_o)

    parts = [
        (hidden, grad_out, "stack", [(512, 0)] * 2),
        (xn2, d_gate_up, "plain", [(512, 2), (1024, 0)] * 3 + [(512, 2), (512, 0)]),
        (head_out, d_att, "plain", [(1024, 0)]),
    ]
    if own_kernels:
        parts[1] = parts[1][:3] + (B_COLS,)
        units, slots, grads_like, scratch = scatter_layout(
            sizes, parts, B_ORDER, {"plain": 2, "stack": 1}
        )
        steps = (n_dp * n_seq).bit_length() - 1
        plan = back_plan(len(units), steps, heads, 3)

        def late(spec):
            shape, index = spec.block_shape, spec.index_map
            return pl.BlockSpec(shape, lambda t: index(jnp.maximum(t - heads, 0)))

        def soon(spec):
            shape, index = spec.block_shape, spec.index_map
            return pl.BlockSpec(shape, lambda t: index(jnp.minimum(t, heads - 1)))

        def each(spec):
            shape, index = spec.block_shape, spec.index_map
            return pl.BlockSpec(shape, lambda t: index(jnp.where(t < heads, t, t - heads)))

        n_prod = len(parts)
        results = pl.pallas_call(
            functools.partial(back_scatter_kernel, sizes, chunk, heads, units, slots, plan, n_prod),
            grid=(2 * heads,),
            in_specs=[anywhere] * (2 * n_prod)
            + [soon(per_head(rows))] * 2 + [whole((1, width)), soon(per_head(rows)), each(per_head(n_chunk * width))]
            + [whole((heads, width, width))]
            + [late(spec) for spec in common_specs + [per_head(rows)] * 5 + [chunk_block] * 3 + [per_head(n_chunk * width)]],
            out_specs=[whole(like.shape) for like in grads_like]
            + [late(spec) for spec in [per_head(rows)] * 3 + [per_head(8)] * 3]
            + [whole((16, qkv)), whole((rows, heads)), whole((8, width))],
            out_shape=grads_like + [jax.ShapeDtypeStruct((rows, cols), bf16)] * 3
            + [jax.ShapeDtypeStruct((8, cols), f32)] * 3
            + [jax.ShapeDtypeStruct((16, qkv), bf16), jax.ShapeDtypeStruct((rows, heads), f32), jax.ShapeDtypeStruct((8, width), f32)],
            scratch_shapes=[pltpu.VMEM(p[0].shape, bf16) for p in parts]
            + [pltpu.VMEM((2, rows, 1024) if i == RINGED else p[1].shape, bf16) for i, p in enumerate(parts)]
            + [pltpu.SemaphoreType.DMA((n_prod, 2)), pltpu.SemaphoreType.DMA((2,))]
            + [pltpu.VMEM((model, rows), bf16)]
            + [
                pltpu.VMEM((heads, rows, width), bf16), pltpu.VMEM((heads, n_chunk * width, width), f32),
                pltpu.VMEM((heads, width, width), f32), pltpu.VMEM((heads, width, width), bf16),
                pltpu.VMEM((heads, width, width), bf16),
                pltpu.SemaphoreType.DMA((heads,)), pltpu.SemaphoreType.DMA((heads,)),
            ]
            + [pltpu.VMEM((rows + 8, width), f32)] + [pltpu.VMEM((rows + 16, width), f32)] * 3
            + [pltpu.VMEM((heads, 3, 8, width), f32)] * 2 + [pltpu.VMEM((heads, 3, 16, width), f32)]
            + [pltpu.SemaphoreType.DMA((heads,)), pltpu.SemaphoreType.DMA((heads,))]
            + scratch,
            compiler_params=pltpu.CompilerParams(
                collective_id=1, has_side_effects=True, vmem_limit_bytes=63 << 20, dimension_semantics=("arbitrary",)
            ),
            name="back_scatter",
        )(
            *[p[0] for p in parts], *[p[1] for p in parts], d_head, mixed, gain_h, qt, dt, seg_turned,
            *common, cq, ck, cv, w_s, u_s, t_s, p_s, kk_s, z_s,
        )
        (g_down, g_mlp, g_out), mains, tapped = results[:n_prod], results[n_prod : n_prod + 3], results[n_prod + 3 : n_prod + 6]
        tails, d_logits, d_head_gain = results[n_prod + 6 :]
        d_conv = jnp.concatenate(tapped, axis=1)[:taps_n]
        small = jnp.concatenate(
            [
                jnp.zeros((9, model), f32),
                d_mlp_gain[None],
                d_conv.reshape(-1, model),
                jnp.pad(d_head_gain[0:1], ((0, 0), (0, model - width))),
            ],
            axis=0,
        )
        count = small.shape[0]
        small = jnp.pad(small, ((0, -count % 8), (0, 0)))
        parts = [(xn1, main, "plain", cols_in) for main, cols_in in zip(mains, F_COLS)]
        units, slots, grads_like, scratch = scatter_layout(sizes, parts, None, {"plain": 3})
        vmem = pl.BlockSpec(memory_space=pltpu.VMEM)
        *g_in, small, grad_tokens = pl.pallas_call(
            functools.partial(final_kernel, sizes, units, slots),
            in_specs=[anywhere] * 4 + [vmem] * 7,
            out_specs=[vmem] * 5,
            out_shape=grads_like + [jax.ShapeDtypeStruct(small.shape, f32), jax.ShapeDtypeStruct((rows, model), bf16)],
            scratch_shapes=[pltpu.VMEM((rows, model), bf16)] * 3 + [pltpu.VMEM(w_in.shape, bf16)]
            + [pltpu.VMEM(small.shape, f32), pltpu.VMEM((8, model), f32), pltpu.SemaphoreType.DMA((4,))]
            + [pltpu.VMEM((model, rows), bf16)]
            + [pltpu.VMEM((2 * steps,) + small.shape, f32), pltpu.SemaphoreType.DMA((steps,)), pltpu.SemaphoreType.DMA((steps,))]
            + scratch,
            compiler_params=pltpu.CompilerParams(collective_id=2, has_side_effects=True, vmem_limit_bytes=63 << 20),
            name="final_scatter",
        )(
            *mains, w_in, tails, xn1, tokens, d_hidden_one, norm_gain.astype(f32)[None],
            jnp.pad(d_logits, ((0, 0), (0, 128 - heads))).astype(bf16), small,
        )
        g_in = jnp.concatenate(g_in, axis=1)
        mine = (lax.axis_index("dp") * n_seq + lax.axis_index("seq")) * (model // (n_dp * n_seq))
        g_beta = lax.dynamic_slice(small[:heads], (0, mine), (heads, model // (n_dp * n_seq))).T
        s_norm, s_mlp = small[heads], small[heads + 1]
        s_conv = small[heads + 2 : count - 1].reshape(taps_n, qkv)
        s_head = small[count - 1, :width]
    else:
        do, b_s, seed, d_head_gain = pl.pallas_call(
            functools.partial(seed_kernel, chunk),
            grid=(heads,),
            in_specs=[per_head(rows), per_head(rows), whole((1, width)), per_head(rows), per_head(n_chunk * width)],
            out_specs=[per_head(rows), per_head(n_chunk * width), state_block, whole((8, width))],
            out_shape=[token_like, state_like, jax.ShapeDtypeStruct((heads, width, width), f32), jax.ShapeDtypeStruct((8, width), f32)],
            compiler_params=params,
            name="delta_seed",
        )(d_head, mixed, gain_h, qt, dt)
        grad_end = relay(True, seg_turned, seed, 1)
        outs = pl.pallas_call(
            functools.partial(back_kernel, chunk),
            grid=(heads,),
            in_specs=common_specs + [per_head(rows)] * 5 + [chunk_block] * 3
            + [per_head(n_chunk * width), per_head(rows), per_head(n_chunk * width), per_head(n_chunk * width), state_block],
            out_specs=[per_head(rows)] * 3 + [per_head(8)] * 6 + [whole((rows, heads))],
            out_shape=[token_like] * 3 + [jax.ShapeDtypeStruct((8, cols), f32)] * 6 + [jax.ShapeDtypeStruct((rows, heads), f32)],
            scratch_shapes=[pltpu.VMEM((rows + 8, width), f32)] + [pltpu.VMEM((rows + 16, width), f32)] * 3,
            compiler_params=params,
            name="delta_back",
        )(*common, cq, ck, cv, w_s, u_s, t_s, p_s, kk_s, z_s, do, dt, b_s, grad_end)
        d_main = jnp.concatenate(outs[:3], axis=1)
        d_early = jnp.concatenate(outs[3:6], axis=1)
        d_conv = jnp.concatenate(outs[6:9], axis=1)[:taps_n]
        d_logits = outs[9]
        returned = from_behind(d_early[8 - taps_n + 1 :].astype(bf16), "seq", -1).astype(f32)
        d_projected = d_main + jnp.pad(returned, ((rows - taps_n + 1, 0), (0, 0)))
        d_proj_b = jnp.concatenate(
            [d_projected.astype(bf16), jnp.pad(d_logits.astype(bf16), ((0, 0), (0, 128 - heads)))], axis=1
        )
        d_from_one, d_norm_gain = pull_one(contract_cols(d_proj_b, w_in))
        grad_tokens = (d_hidden_one + d_from_one).astype(bf16)

        d_beta_rows = tn(d_logits.astype(bf16), xn1)
        g_down, g_mlp, g_out, g_in, g_beta = (
            lax.psum_scatter(grad, both, scatter_dimension=0, tiled=True)
            for grad in [contract_rows(left, right) for left, right, _, _ in parts]
            + [contract_rows(xn1, d_proj_b[:, :qkv]), d_beta_rows.T]
        )
        s_norm, s_conv, s_head, s_mlp = lax.psum((d_norm_gain, d_conv, d_head_gain[0], d_mlp_gain), both)
    return (out, grad_tokens, s_norm, g_in, g_beta, s_conv, s_head, g_out, s_mlp, g_mlp, g_down)


def solution(mesh):
    split = P(("dp", "seq"), None)
    placed = (split, P("dp", None), P(), split, split, P(), P(), split, P(), split, split, split)
    return jax.shard_map(
        functools.partial(local, mesh.shape["dp"], mesh.shape["seq"]),
        mesh=mesh,
        in_specs=placed,
        out_specs=(split, split, P(), split, split, P(), P(), split, P(), split, split),
        check_vma=False,
    )
```

```python
import functools

import jax
import jax.numpy as jnp
from jax import lax
from jax.experimental import pallas as pl
from jax.experimental.pallas import tpu as pltpu
from jax.sharding import PartitionSpec as P

norm_eps = 1e-05
unit_eps = 1e-06
MESH = pl.DeviceIdType.MESH
f32, bf16 = jnp.float32, jnp.bfloat16
HIGH = lax.Precision.HIGH
VMEM_LIMIT = 56 << 20
SPARE = 24
TURNS = (0, 1, 5)
RINGED = 1
B_COLS = [(1024, 0)] * 5 + [(512, 0)]
B_ORDER = [2, 3, 4, 0, 5, 1, 6, 8, 7]
TOKEN_TURN = 1
F_COLS = [[(1024, 0)], [(1024, 0)], [(512, 0), (512, 0)]]


def nn(a, b, prec=None):
    return lax.dot_general(a, b, (((1,), (0,)), ((), ())), precision=prec, preferred_element_type=f32)


def nt(a, b, prec=None):
    return lax.dot_general(a, b, (((1,), (1,)), ((), ())), precision=prec, preferred_element_type=f32)


def tn(a, b, prec=None):
    return lax.dot_general(a, b, (((0,), (0,)), ((), ())), precision=prec, preferred_element_type=f32)


def unit_lower_inverses(mats, row, col):
    size = mats[0].shape[0]
    block = min(8, size)
    eye = (row == col).astype(f32)
    near = row // block == col // block
    powers = [jnp.where(near, -a, 0.0) for a in mats]
    inverses = [eye + p for p in powers]
    reach = 2
    while reach < block:
        powers = [nn(p, p, HIGH) for p in powers]
        inverses = [t + nn(t, p, HIGH) for t, p in zip(inverses, powers)]
        reach *= 2
    while block < size:
        pairs = size // (2 * block)

        def lower(m, block=block, pairs=pairs):
            return jnp.concatenate([m[(2 * i + 1) * block : (2 * i + 2) * block] for i in range(pairs)], axis=0)

        def spread(m, fill, block=block, pairs=pairs):
            return jnp.concatenate(
                [x for i in range(pairs) for x in (fill[2 * i * block : (2 * i + 1) * block], m[i * block : (i + 1) * block])],
                axis=0,
            )

        off = (row // (2 * block) == col // (2 * block)) & (row // block == col // block + 1)
        lows = [lower(jnp.where(off, a, 0.0)) for a in mats]
        crossed = [nn(x, t, HIGH) for x, t in zip(lows, inverses)]
        zero = jnp.zeros((size, size), f32)
        below = [lower(t) for t in inverses]
        fixed = [x - nn(x, spread(y, zero), HIGH) for x, y in zip(below, crossed)]
        inverses = [spread(x, t) for x, t in zip(fixed, inverses)]
        block *= 2
    return inverses


def head_column(matrix, head):
    lane = lax.broadcasted_iota(jnp.int32, matrix.shape, 1)
    return jnp.sum(jnp.where(lane == head, matrix, 0.0), axis=1, keepdims=True)


def masks_of(docs_col, docs_row):
    size = docs_col.shape[0]
    row = lax.broadcasted_iota(jnp.int32, (size, size), 0)
    col = lax.broadcasted_iota(jnp.int32, (size, size), 1)
    same = docs_col == docs_row
    return row, col, same


def local_kernel(
    sizes, chunk, gathers, *refs,
):
    far = 1 if gathers else 0
    local_body(
        sizes, chunk, gathers, refs[:gathers], refs[gathers] if far else None, *refs[gathers + far :]
    )


def local_body(
    sizes, chunk, gathers, shards, far_rows, pq, pk, pv, hq, hk, hv, tq, tk, tv, aux, docs_c, docs_r, logits,
    cq, ck, cv, w_o, u_o, qt_o, o_o, t_o, p_o, kk_o, dt_o, ft_o, map_o, turned_o, add_o, *rest,
):
    head = pl.program_id(0)
    turns = TURNS
    if gathers:
        wholes, (halo_o, pad, halo_s, halo_ssem, halo_rsem), sems = rest[:gathers], rest[gathers : gathers + 5], rest[gathers + 5 :]
        segment, heads, span = lax.axis_index("seq"), pl.num_programs(0), pq.shape[1]
        tail = pltpu.make_async_remote_copy(
            src_ref=far_rows.at[pl.ds(pq.shape[0] - 8, 8), pl.ds(0, halo_s.shape[1])], dst_ref=halo_s,
            send_sem=halo_ssem, recv_sem=halo_rsem,
            device_id=(lax.axis_index("dp"), segment + 1), device_id_type=MESH,
        )

        @pl.when(head == 0)
        def _():
            pl.semaphore_wait(
                pltpu.get_barrier_semaphore(), gather_greet(sizes) + relay_greet(sizes[1], False)
            )

            @pl.when(segment < sizes[1] - 1)
            def _():
                tail.start()

        gather_beside(sizes, head, shards, wholes, sems, turns)

        @pl.when(head == 0)
        def _():
            @pl.when(segment == 0)
            def _():
                halo_s[...] = jnp.zeros(halo_s.shape, f32)

            @pl.when(segment > 0)
            def _():
                tail.wait_recv()

            halo_o[...] = halo_s[...]

        @pl.when((head == heads - 1) & (segment < sizes[1] - 1))
        def _():
            tail.wait_send()

        hq, hk, hv = (
            halo_s.at[:, pl.ds(pl.multiple_of((third * heads + head) * span, span), span)] for third in range(3)
        )
    else:
        pad, wholes, sems = rest[0], (), ()
    rows, width = pq.shape
    keeps = (aux[:, 2:3], aux[:, 3:4], aux[:, 4:5])
    acts = []
    for src, halo, taps, dst in ((pq, hq, tq, cq), (pk, hk, tk, ck), (pv, hv, tv, cv)):
        pad[0:8, :] = halo[...]
        pad[8 : 8 + rows, :] = src[...]
        conv = taps[3:4, :] * src[...]
        for back in (1, 2, 3):
            conv = conv + taps[3 - back : 4 - back, :] * (pad[8 - back : 8 - back + rows, :] * keeps[back - 1])
        dst[...] = conv
        acts.append(conv * jax.nn.sigmoid(conv))
    q = acts[0] * (lax.rsqrt(jnp.sum(acts[0] * acts[0], axis=1, keepdims=True) + unit_eps) * width ** (-0.5))
    k = acts[1] * lax.rsqrt(jnp.sum(acts[1] * acts[1], axis=1, keepdims=True) + unit_eps)
    v = acts[2]
    beta = jax.nn.sigmoid(head_column(logits[...], head))
    cont, last = aux[:, 0:1], aux[:, 1:2]
    n_chunk = rows // chunk
    cuts = [slice(c * chunk, (c + 1) * chunk) for c in range(n_chunk)]
    row = lax.broadcasted_iota(jnp.int32, (chunk, chunk), 0)
    col = lax.broadcasted_iota(jnp.int32, (chunk, chunk), 1)
    same = [docs_c[sl, :] == docs_r[:, sl] for sl in cuts]
    kks = [nt(k[sl], k[sl], HIGH) for sl in cuts]
    ps = [jnp.where(m & (row >= col), nt(q[sl], k[sl], HIGH), 0.0) for m, sl in zip(same, cuts)]
    ts = unit_lower_inverses(
        [jnp.where(m & (row > col), beta[sl] * kk, 0.0) for m, sl, kk in zip(same, cuts, kks)], row, col
    )
    rhs = [jnp.concatenate([(beta[sl] * cont[sl]) * k[sl], beta[sl] * v[sl]], axis=1) for sl in cuts]
    wus = [nn(t, r, HIGH) for t, r in zip(ts, rhs)]
    pwus = [nn(p, wu, HIGH) for p, wu in zip(ps, wus)]
    xs = [tn(last[sl] * k[sl], wu, HIGH) for sl, wu in zip(cuts, wus)]
    d_row = lax.broadcasted_iota(jnp.int32, (width, width), 0)
    d_col = lax.broadcasted_iota(jnp.int32, (width, width), 1)
    seg = None
    for c, sl in enumerate(cuts):
        cc = cont[sl]
        dt = jnp.where(d_row == d_col, cc[chunk - 1 : chunk], 0.0) - xs[c][:, :width]
        ft = xs[c][:, width:]
        w_o[sl, :] = wus[c][:, :width]
        u_o[sl, :] = wus[c][:, width:]
        qt_o[sl, :] = cc * q[sl] - pwus[c][:, :width]
        o_o[sl, :] = pwus[c][:, width:]
        t_o[sl, :] = ts[c].astype(bf16)
        p_o[sl, :] = ps[c].astype(bf16)
        kk_o[sl, :] = kks[c]
        dt_o[c * width : (c + 1) * width, :] = dt
        ft_o[c * width : (c + 1) * width, :] = ft
        if seg is None:
            seg = jnp.concatenate([dt, ft], axis=1)
        else:
            seg = nn(dt, seg, HIGH)
            seg = jnp.concatenate([seg[:, :width], seg[:, width:] + ft], axis=1)
    map_o[0] = seg[:, :width]
    turned_o[0] = seg[:, :width].T
    add_o[0] = seg[:, width:]
    gather_rest(sizes, head, shards, wholes, sems, len(turns), pl.num_programs(0) - 1)


def relay_ends(n_seq, back):
    s = lax.axis_index("seq")
    if back:
        return s == n_seq - 1, s == 0, s - 1, s + 1
    return s == 0, s == n_seq - 1, s + 1, s - 1


def relay_greet(n_seq, back):
    d = lax.axis_index("dp")
    first, final, ahead, behind = relay_ends(n_seq, back)
    barrier = pltpu.get_barrier_semaphore()

    @pl.when(jnp.logical_not(first))
    def _():
        pl.semaphore_signal(barrier, inc=1, device_id=(d, behind), device_id_type=MESH)

    @pl.when(jnp.logical_not(final))
    def _():
        pl.semaphore_signal(barrier, inc=1, device_id=(d, ahead), device_id_type=MESH)

    return jnp.where(first | final, 1, 2)


def relay_kernel(n_seq, back, *refs):
    pl.semaphore_wait(pltpu.get_barrier_semaphore(), relay_greet(n_seq, back))
    relay_body(n_seq, back, *refs)


def relay_body(n_seq, back, map_ref, add_ref, out_ref, send, ssem, rsem):
    d = lax.axis_index("dp")
    heads = map_ref.shape[0]
    first, final, ahead, behind = relay_ends(n_seq, back)

    def copy_of(h):
        return pltpu.make_async_remote_copy(
            src_ref=send.at[h], dst_ref=out_ref.at[h], send_sem=ssem.at[h], recv_sem=rsem.at[h],
            device_id=(d, ahead), device_id_type=MESH,
        )

    @pl.when(first)
    def _():
        out_ref[...] = jnp.zeros(out_ref.shape, out_ref.dtype)
        for h in range(heads):
            send[h] = add_ref[h].astype(bf16)
            copy_of(h).start()

    @pl.when(jnp.logical_not(first))
    def _():
        for h in range(heads):
            copy_of(h).wait_recv()
            send[h] = (nn(map_ref[h], out_ref[h].astype(f32), HIGH) + add_ref[h]).astype(bf16)

            @pl.when(jnp.logical_not(final))
            def _():
                copy_of(h).start()

    @pl.when(jnp.logical_not(final))
    def _():
        for h in range(heads):
            copy_of(h).wait_send()


def output_kernel(chunk, zin, dt, ft, qt, o0, gain, z_o, o_o, head_o):
    width = gain.shape[1]
    rows = qt.shape[0]
    sides = [slice(i * width, (i + 1) * width) for i in range(zin.shape[0])]
    states = [zin[i].astype(f32) for i in range(zin.shape[0])]
    for c in range(rows // chunk):
        sl = slice(c * chunk, (c + 1) * chunk)
        ds = slice(c * width, (c + 1) * width)
        for z, side in zip(states, sides):
            z_o[ds, side] = z
        outs = [o0[sl, side] + nn(qt[sl, side], z, HIGH) for z, side in zip(states, sides)]
        if c + 1 < rows // chunk:
            states = [nn(dt[ds, side], z, HIGH) + ft[ds, side] for z, side in zip(states, sides)]
        for o, side in zip(outs, sides):
            o_o[sl, side] = o
            scale = lax.rsqrt(jnp.mean(o * o, axis=1, keepdims=True) + norm_eps)
            head_o[sl, side] = (o * scale * gain[...]).astype(bf16)


def seed_kernel(chunk, *refs):
    seed_body(chunk, pl.program_id(0), *refs)


def seed_body(chunk, head, dh, o, gain, qt, dt, do_o, b_o, seed_o, dgain_o):
    rows, width = qt.shape
    ov, dhv = o[...], dh[...]
    scale = lax.rsqrt(jnp.mean(ov * ov, axis=1, keepdims=True) + norm_eps)
    n = ov * scale
    dg = jnp.sum(dhv * n, axis=0, keepdims=True)
    dgain_o[...] = jnp.where(head == 0, 0.0, dgain_o[...]) + jnp.broadcast_to(dg, dgain_o.shape)
    y = dhv * gain[...]
    do = (y - n * jnp.mean(y * n, axis=1, keepdims=True)) * scale
    do_o[...] = do.astype(do_o.dtype)
    g = None
    for c in reversed(range(rows // chunk)):
        sl = slice(c * chunk, (c + 1) * chunk)
        ds = slice(c * width, (c + 1) * width)
        b_o[ds, :] = tn(qt[sl, :], do[sl], HIGH)
        g = b_o[ds, :] if g is None else tn(dt[ds, :], g, HIGH) + b_o[ds, :]
    seed_o[0] = g


def back_kernel(chunk, *refs):
    back_body(chunk, pl.program_id(0), *refs)


def back_body(
    chunk, head, pq, pk, pv, hq, hk, hv, tq, tk, tv, aux, docs_c, docs_r, logits,
    cq, ck, cv, w_r, u_r, t_r, p_r, kk_r, z_r, do_r, dt_r, b_r, g_r,
    dpq, dpk, dpv, dhq, dhk, dhv, dtq, dtk, dtv, dlogit_o, pad, mask1, mask2, mask3, tails=(None,) * 3,
):
    rows, width = pq.shape
    cont, last = aux[:, 0:1], aux[:, 1:2]
    keeps = (aux[:, 2:3], aux[:, 3:4], aux[:, 4:5])
    scale = width ** (-0.5)
    beta = jax.nn.sigmoid(head_column(logits[...], head))
    sq, sk, sv = (jax.nn.sigmoid(x[...]) for x in (cq, ck, cv))
    aq, ak, v = cq[...] * sq, ck[...] * sk, cv[...] * sv
    iq = lax.rsqrt(jnp.sum(aq * aq, axis=1, keepdims=True) + unit_eps)
    ik = lax.rsqrt(jnp.sum(ak * ak, axis=1, keepdims=True) + unit_eps)
    uq, k = aq * iq, ak * ik
    q = uq * scale
    n_chunk = rows // chunk
    cuts = [slice(c * chunk, (c + 1) * chunk) for c in range(n_chunk)]
    blocks = [slice(c * width, (c + 1) * width) for c in range(n_chunk)]
    gs = [g_r[0].astype(f32)]
    for c in reversed(range(1, n_chunk)):
        gs.insert(0, tn(dt_r[blocks[c], :], gs[0]) + b_r[blocks[c], :])
    row = lax.broadcasted_iota(jnp.int32, (chunk, chunk), 0)
    col = lax.broadcasted_iota(jnp.int32, (chunk, chunk), 1)
    same = [docs_c[sl, :] == docs_r[:, sl] for sl in cuts]
    ks = [k[sl].astype(bf16) for sl in cuts]
    dos = [do_r[sl, :].astype(bf16) for sl in cuts]
    zs = [z_r[ds, :].astype(bf16) for ds in blocks]
    gbs = [g.astype(bf16) for g in gs]
    wkzs = [
        nn(jnp.concatenate([w_r[sl, :], k[sl]], axis=0), z_r[ds, :], HIGH) for sl, ds in zip(cuts, blocks)
    ]
    us = [(u_r[sl, :] - x[:chunk]).astype(bf16) for sl, x in zip(cuts, wkzs)]
    dus = [tn(p_r[sl, :].astype(bf16), do) for sl, do in zip(cuts, dos)]
    dus = [x + nn((last[sl] * k[sl]).astype(bf16), g) for x, sl, g in zip(dus, cuts, gbs)]
    drs = [tn(t_r[sl, :].astype(bf16), x.astype(bf16)) for sl, x in zip(cuts, dus)]
    ys = [
        nt(jnp.concatenate([do, dr.astype(bf16)], axis=0), jnp.concatenate([u, z], axis=0))
        for do, dr, u, z in zip(dos, drs, us, zs)
    ]
    dps = [jnp.where(m & (row >= col), y[:chunk, :chunk], 0.0) for m, y in zip(same, ys)]
    das = [jnp.where(m & (row > col), -y[chunk:, :chunk], 0.0) for m, y in zip(same, ys)]
    pbs = [
        jnp.concatenate([dp, beta[sl] * da], axis=0).astype(bf16) for dp, da, sl in zip(dps, das, cuts)
    ]
    paks = [nn(pb, kc) for pb, kc in zip(pbs, ks)]
    turns = [
        tn(pb, jnp.concatenate([q[sl].astype(bf16), kc], axis=0)) for pb, sl, kc in zip(pbs, cuts, ks)
    ]
    ugs = [nt(u, g) for u, g in zip(us, gbs)]
    dq = jnp.concatenate([cont[sl] * y[:chunk, chunk:] + x[:chunk] for sl, y, x in zip(cuts, ys, paks)], axis=0)
    dk = jnp.concatenate(
        [
            t + x[chunk:] + last[sl] * ug - (beta[sl] * cont[sl]) * y[chunk:, chunk:]
            for t, x, sl, ug, y in zip(turns, paks, cuts, ugs, ys)
        ],
        axis=0,
    )
    dv = jnp.concatenate([beta[sl] * dr for sl, dr in zip(cuts, drs)], axis=0)
    db = jnp.concatenate(
        [
            jnp.sum(dr * (v[sl] - cont[sl] * x[chunk:]), axis=1, keepdims=True)
            + jnp.sum(da * kk_r[sl, :], axis=1, keepdims=True)
            for dr, sl, x, da in zip(drs, cuts, wkzs, das)
        ],
        axis=0,
    )
    lane = lax.broadcasted_iota(jnp.int32, dlogit_o.shape, 1)
    dlogit_o[...] = jnp.where(lane == head, db * beta * (1.0 - beta), jnp.where(head == 0, 0.0, dlogit_o[...]))
    du_q = dq * scale
    da_q = (du_q - uq * jnp.sum(uq * du_q, axis=1, keepdims=True)) * iq
    da_k = (dk - k * jnp.sum(k * dk, axis=1, keepdims=True)) * ik
    for dact, sg, c_r, src, halo, taps, dst, dhalo, dtaps, tail in (
        (da_q, sq, cq, pq, hq, tq, dpq, dhq, dtq, tails[0]),
        (da_k, sk, ck, pk, hk, tk, dpk, dhk, dtk, tails[1]),
        (dv, sv, cv, pv, hv, tv, dpv, dhv, dtv, tails[2]),
    ):
        dconv = dact * (sg * (1.0 + c_r[...] * (1.0 - sg)))
        pad[0:8, :] = halo[...]
        pad[8 : 8 + rows, :] = src[...]
        zero = jnp.zeros((8, width), f32)
        total = taps[3:4, :] * dconv
        early = zero
        gtaps = [None] * 4
        gtaps[3] = jnp.sum(dconv * src[...], axis=0, keepdims=True)
        for back, mask in ((1, mask1), (2, mask2), (3, mask3)):
            kept = dconv * keeps[back - 1]
            gtaps[3 - back] = jnp.sum(kept * pad[8 - back : 8 - back + rows, :], axis=0, keepdims=True)
            mask[0:8, :] = zero
            mask[8 : 8 + rows, :] = kept
            mask[8 + rows : 16 + rows, :] = zero
            total = total + taps[3 - back : 4 - back, :] * mask[8 + back : 8 + back + rows, :]
            early = early + taps[3 - back : 4 - back, :] * mask[back : back + 8, :]
        dst[...] = total.astype(dst.dtype)
        dhalo[...] = early
        if tail is not None:
            tail[...] = total[rows - 16 :]
        dtaps[...] = jnp.concatenate(gtaps + [jnp.zeros((4, width), f32)], axis=0)


def bit_orders(n_dp, n_seq):
    dp_bits = [("dp", i) for i in range(n_dp.bit_length() - 1)]
    seq_bits = [("seq", i) for i in range(n_seq.bit_length() - 1)]
    return (
        seq_bits[:1] + dp_bits + seq_bits[1:],
        seq_bits[:1] + dp_bits[::-1] + seq_bits[1:],
        seq_bits + dp_bits,
        seq_bits + dp_bits[::-1],
    )


def scatter_steps(sizes, units, slots, lefts, rights, outs, scratch, turned=()):
    n_dp, n_seq = sizes
    scratch = list(scratch)
    orders = bit_orders(n_dp, n_seq)
    steps = len(orders[0])
    pool = [scratch.pop(0) for _ in range(2 * (1 + max(slots)))]
    own = [pool[2 * slots[u] + half] for u in range(len(units)) for half in (0, 1)]
    before = [max([w for w in range(u) if slots[w] == slots[u]], default=None) for u in range(len(units))]
    got = [[scratch.pop(0) for _ in range(steps)] for _ in range(2 * len(units))]
    ssem, rsem = scratch
    index = {"dp": lax.axis_index("dp"), "seq": lax.axis_index("seq")}

    def bit_of(axis, bit):
        return (index[axis] // 2**bit) % 2

    def partner(axis, bit):
        other = dict(index)
        other[axis] = index[axis] + (1 - 2 * bit_of(axis, bit)) * 2**bit
        return (other["dp"], other["seq"])

    def greet():
        for axis, bit in orders[0]:
            pl.semaphore_signal(
                pltpu.get_barrier_semaphore(), inc=1, device_id=partner(axis, bit), device_id_type=MESH
            )
        return steps

    def weights(order):
        return {key: 2 ** (steps - 1 - i) for i, key in enumerate(order)}

    def place(order, axis, value):
        w = weights(order)
        return sum(((value // 2**b) % 2) * w[(a, b)] for a, b in order if a == axis)

    def compute(u):
        kind, li, _, _, cols, _, _, first_order = units[u]
        left, (right, first) = lefts[li], rights(u)
        block = left.shape[0 if li in turned else 1] // (n_dp * n_seq)
        together = n_seq
        while together * block % 128:
            together *= 2
        half_cols = cols // 2

        def rows_of(m, carry):
            span = pl.ds(pl.multiple_of(m * (together * block), 128), together * block)
            some = right[:, first : first + cols]
            tile = nn(left[span, :], some) if li in turned else tn(left[:, span], some)
            for half in (0, 1):
                order, buf = orders[first_order + half], own[2 * u + half]
                for j in range(together):
                    piece = tile[j * block : (j + 1) * block, half * half_cols : (half + 1) * half_cols]
                    if kind == "stack":
                        piece = jnp.concatenate([piece[:, : cols // 4], piece[:, cols // 4 :]], axis=0)
                    base = place(order, "dp", m * (together // n_seq) + j // n_seq)
                    buf[base + place(order, "seq", j % n_seq)] = piece.astype(bf16)
            return carry

        lax.fori_loop(0, n_dp * n_seq // together, rows_of, 0)

    def copy_of(u, half, k):
        src = own[2 * u + half] if k == 0 else got[2 * u + half][k - 1]
        dst = got[2 * u + half][k]
        axis, bit = orders[units[u][7] + half][k]
        count = dst.shape[0]
        return pltpu.make_async_remote_copy(
            src_ref=src.at[pl.ds((1 - bit_of(axis, bit)) * count, count)], dst_ref=dst,
            send_sem=ssem.at[u, half, k], recv_sem=rsem.at[u, half, k],
            device_id=partner(axis, bit), device_id_type=MESH,
        )

    def merge(u, half, k):
        src = own[2 * u + half] if k == 0 else got[2 * u + half][k - 1]
        dst = got[2 * u + half][k]
        axis, bit = orders[units[u][7] + half][k]
        count = dst.shape[0]
        mine = bit_of(axis, bit) * count
        copy_of(u, half, k).wait_recv()
        if k < steps - 1:
            def add(i, carry):
                dst[i] = dst[i] + src[mine + i]
                return carry

            lax.fori_loop(0, count, add, 0)
            copy_of(u, half, k + 1).start()
        else:
            kind, _, _, first, cols, oi, to, _ = units[u]
            total = dst[0].astype(f32) + src[mine].astype(f32)
            start, wide = to + half * (cols // 2), cols // 2
            if kind == "stack":
                block = total.shape[0] // 2
                outs[oi][:, start : start + wide // 2] = total[:block]
                outs[oi][:, start + wide // 2 : start + wide] = total[block:]
            else:
                outs[oi][:, start : start + wide] = total

    def begin(u):
        if before[u] is not None:
            for half in (0, 1):
                copy_of(before[u], half, 0).wait_send()
        compute(u)
        for half in (0, 1):
            copy_of(u, half, 0).start()

    def both_merge(u, k):
        for half in (0, 1):
            merge(u, half, k)

    def finish():
        for k in range(steps):
            for u in range(len(units)):
                if k > 0 or u not in before:
                    for half in (0, 1):
                        copy_of(u, half, k).wait_send()

    return steps, partner, greet, begin, both_merge, finish


def turn_over(src, dst):
    span = 256

    def some(i, carry):
        at = pl.ds(pl.multiple_of(i * span, span), span)
        dst[at, :] = src[:, at].T
        return carry

    lax.fori_loop(0, src.shape[1] // span, some, 0)


def small_steps(sizes, partner, small_in, small_out, small_got, small_ssem, small_rsem):
    order = bit_orders(*sizes)[0]
    steps = len(order)

    def small_copy(k):
        return pltpu.make_async_remote_copy(
            src_ref=small_in if k == 0 else small_got.at[steps + k - 1], dst_ref=small_got.at[k],
            send_sem=small_ssem.at[k], recv_sem=small_rsem.at[k],
            device_id=partner(*order[k]), device_id_type=MESH,
        )

    def small_step(k):
        small_copy(k).wait_recv()
        mine = small_in[...] if k == 0 else small_got[steps + k - 1]
        if k < steps - 1:
            small_got[steps + k] = small_got[k] + mine
            small_copy(k + 1).start()
        else:
            small_out[...] = small_got[k] + mine

    def small_finish():
        for k in range(steps):
            small_copy(k).wait_send()

    return small_copy(0).start, small_step, small_finish


def scatter_layout(sizes, products, order, keep):
    n = sizes[0] * sizes[1]
    steps = n.bit_length() - 1
    units, outs = [], []
    for oi, (left, right, kind, cols) in enumerate(products):
        block = left.shape[1] // n
        outs.append(jax.ShapeDtypeStruct((block, right.shape[1]), f32))
        first = 0
        for wide, first_order in cols:
            units.append((kind, oi, oi, first, wide, oi, first, first_order))
            first += wide
    units = [units[i] for i in order or range(len(units))]
    shapes = []
    for kind, oi, _, _, wide, _, _, _ in units:
        block = outs[oi].shape[0]
        shapes.append((2 * block, wide // 4) if kind == "stack" else (block, wide // 2))
    pool, slots = [], []
    for u, shape in enumerate(shapes):
        alike = [i for i, kept in enumerate(pool) if kept == shape]
        if len(alike) < keep[units[u][0]]:
            slots.append(len(pool))
            pool.append(shape)
        else:
            used = [max(w for w in range(u) if slots[w] == i) for i in alike]
            slots.append(alike[used.index(min(used))])
    own = [pltpu.VMEM((n,) + s, bf16) for s in pool for _ in (0, 1)]
    got = [pltpu.VMEM((n >> (k + 1),) + s, bf16) for s in shapes for _ in (0, 1) for k in range(steps)]
    sems = pltpu.SemaphoreType.DMA((len(units), 2, steps))
    return units, slots, outs, own + got + [sems, sems]


def back_scatter_kernel(sizes, chunk, heads, units, slots, plan, n_prod, *refs):
    turn = pl.program_id(0)
    refs = list(refs)

    def take(count):
        got = refs[:count]
        del refs[:count]
        return got

    far_lefts, far_rights = take(n_prod), take(n_prod)
    dh, o, gain, qt, dt, turned = take(6)
    common, saved = take(13), take(9)
    outs, mains, tapped, tail_o, dlogit, dgain = take(n_prod), take(3), take(3), *take(3)
    lefts, rights, fetch, ring_sem, turn_s = take(n_prod), take(n_prod), *take(3)
    do_s, b_s, seed_s, g_s, send, relay_ssem, relay_rsem = take(7)
    pads = take(4)
    early_s, late_s, tail_s, halo_ssem, halo_rsem = take(5)
    ringed = [u for u, unit in enumerate(units) if unit[1] == RINGED]

    def right_of(u):
        if u in ringed:
            return rights[RINGED].at[ringed.index(u) % 2], 0
        return rights[units[u][2]], units[u][3]

    def ring_fetch(place):
        _, _, ri, first, wide, _, _, _ = units[ringed[place]]
        return pltpu.make_async_copy(
            far_rights[ri].at[:, pl.ds(first, wide)],
            rights[ri].at[place % 2, :, pl.ds(0, wide)],
            ring_sem.at[place % 2],
        )

    steps, partner, greet, begin, merge, finish = scatter_steps(
        sizes, units, slots, [turn_s if i == RINGED else left for i, left in enumerate(lefts)],
        right_of, outs, refs, (RINGED,),
    )

    def fetches(i):
        copies = [pltpu.make_async_copy(far_lefts[i], lefts[i], fetch.at[i, 0])]
        if i != RINGED:
            copies.append(pltpu.make_async_copy(far_rights[i], rights[i], fetch.at[i, 1]))
        return copies

    segment = lax.axis_index("seq")

    def halo_copy(head):
        return pltpu.make_async_remote_copy(
            src_ref=early_s.at[head], dst_ref=late_s.at[head], send_sem=halo_ssem.at[head], recv_sem=halo_rsem.at[head],
            device_id=(lax.axis_index("dp"), segment - 1), device_id_type=MESH,
        )

    seen = [unit[1] for unit in units]
    arrival = sorted(range(n_prod), key=seen.index)

    @pl.when(turn == 0)
    def _():
        for i in arrival:
            for copy in fetches(i):
                copy.start()
        for place in (0, 1):
            ring_fetch(place).start()
        pl.semaphore_wait(pltpu.get_barrier_semaphore(), greet() + relay_greet(sizes[1], True))

    @pl.when(turn < heads)
    def _():
        seed_body(
            chunk, turn, dh, o, gain, qt, dt, do_s.at[turn], b_s.at[turn], seed_s.at[pl.ds(turn, 1)], dgain
        )

    @pl.when(turn == heads)
    def _():
        relay_body(sizes[1], True, turned, seed_s, g_s, send, relay_ssem, relay_rsem)

    for t, events in enumerate(plan):
        if events:
            @pl.when(turn == t)
            def _(events=events):
                for u, k in events:
                    if k < 0:
                        if seen.index(seen[u]) == u:
                            for copy in fetches(seen[u]):
                                copy.wait()
                            if seen[u] == RINGED:
                                turn_over(lefts[RINGED], turn_s)
                        if u in ringed:
                            ring_fetch(ringed.index(u)).wait()
                        begin(u)
                        if u in ringed and ringed.index(u) + 2 < len(ringed):
                            ring_fetch(ringed.index(u) + 2).start()
                    else:
                        merge(u, k)

    @pl.when(turn >= heads)
    def _():
        head = turn - heads
        back_body(
            chunk, head, *common, *saved, do_s.at[head], dt, b_s.at[head], g_s.at[pl.ds(head, 1)],
            *mains, *[early_s.at[head, third] for third in range(3)], *tapped, dlogit, *pads,
            tails=[tail_s.at[head, third] for third in range(3)],
        )

        @pl.when(segment > 0)
        def _():
            halo_copy(head).start()

    @pl.when(turn == 2 * heads - 1)
    def _():
        width = late_s.shape[3]

        @pl.when(segment == sizes[1] - 1)
        def _():
            late_s[...] = jnp.zeros(late_s.shape, f32)

        @pl.when(segment < sizes[1] - 1)
        def _():
            for head in range(heads):
                halo_copy(head).wait_recv()

        for head in range(heads):
            for third in range(3):
                tail = tail_s[head, third]
                tail = jnp.concatenate([tail[:8], tail[8:] + late_s[head, third]], axis=0)
                tail_o[:, (third * heads + head) * width : (third * heads + head + 1) * width] = tail.astype(bf16)

        @pl.when(segment > 0)
        def _():
            for head in range(heads):
                halo_copy(head).wait_send()

        finish()


def final_kernel(sizes, units, slots, *refs):
    refs = list(refs)

    def take(count):
        got = refs[:count]
        del refs[:count]
        return got

    far, (far_w, tails, xn1, tokens, d_one, gain, dlogit, small_in) = take(3), take(8)
    outs, (small_out, grad_o) = take(3), take(2)
    rights, (weight, small_s, gain_s, fetch, turn_s) = take(3), take(5)
    small_scratch = take(3)
    rows, model = xn1.shape
    steps, partner, greet, begin, merge, finish = scatter_steps(
        sizes, units, slots, [turn_s] * 3, lambda u: (rights[units[u][2]], units[u][3]), outs, refs, (0, 1, 2)
    )
    small_start, small_step, small_finish = small_steps(sizes, partner, small_s, small_out, *small_scratch)
    fetches = [pltpu.make_async_copy(a, b, fetch.at[i]) for i, (a, b) in enumerate(zip(far + [far_w], rights + [weight]))]
    for copy in fetches:
        copy.start()
    turn_over(xn1, turn_s)
    pl.semaphore_wait(pltpu.get_barrier_semaphore(), greet())
    small_s[...] = small_in[...]
    small_s[0:8, :] = tn(dlogit[...], xn1[...])[0:8]

    def token_grads():
        part = rows // 2
        fetches[3].wait()
        gain_s[...] = jnp.zeros(gain_s.shape, f32)

        def some(i, carry):
            at = pl.ds(pl.multiple_of(i * part, 16), part)
            dx = nt(dlogit[at, :], weight[:, 3 * model :])
            for third in range(3):
                dx = dx + nt(rights[third][at, :], weight[:, third * model : (third + 1) * model])
            x = tokens[at, :].astype(f32)
            scale = lax.rsqrt(jnp.mean(x * x, axis=1, keepdims=True) + norm_eps)
            n = x * scale
            gain_s[0:1, :] += jnp.sum(dx * n, axis=0, keepdims=True)
            y = dx * gain[...]
            dz = (y - n * jnp.mean(y * n, axis=1, keepdims=True)) * scale
            grad_o[at, :] = (d_one[at, :] + dz).astype(bf16)
            return carry

        lax.fori_loop(0, 2, some, 0)
        small_s[8:9, :] = gain_s[0:1, :]

    seen = [unit[2] for unit in units]
    for t in range(len(units) + steps):
        for k in range(steps):
            if 0 <= t - 1 - k < len(units):
                merge(t - 1 - k, k)
        if t < len(units):
            third = seen[t]
            if seen.index(third) == t and third not in seen[: TOKEN_TURN + 1][:t] and (t <= TOKEN_TURN):
                fetches[third].wait()
                rights[third][rows - 16 :, :] = tails[:, third * model : (third + 1) * model]
            begin(t)
        if t == len(units) - 1:
            small_start()
        if 0 <= t - len(units) < steps:
            small_step(t - len(units))
        if t == TOKEN_TURN:
            for copy in fetches[max(seen[: t + 1]) + 1 : 3]:
                copy.wait()
            for third in range(max(seen[: t + 1]) + 1, 3):
                rights[third][rows - 16 :, :] = tails[:, third * model : (third + 1) * model]
            token_grads()
    finish()
    small_finish()


def back_plan(n_units, steps, heads, early):
    plan = [[] for _ in range(2 * heads)]
    for i in range(n_units + steps):
        turn = 2 * i if i <= early else heads + i - early - 1
        turn = min(turn, 2 * heads - 1)
        for k in range(steps):
            if 0 <= i - 1 - k < n_units and not (i == early + 1 and k == 0):
                plan[turn].append((i - 1 - k, k))
        if i < n_units:
            plan[turn].append((i, -1))
        if i == early:
            plan[heads - 1].append((early, 0))
    return plan


def gather_parts(shape):
    rows, cols = shape
    half = rows // 2
    spare = cols * SPARE // 100 // 128 * 128 if cols >= 2048 else 0
    parts = [(i * half, half, 0, cols - spare) for i in (0, 1)]
    if spare:
        parts += [(i * half, half, cols - spare, spare) for i in (0, 1)]
    return parts


def gather_steps(sizes, shard, whole, own_sem, ssem, rsem):
    n_dp, n_seq = sizes
    index = {"dp": lax.axis_index("dp"), "seq": lax.axis_index("seq")}
    orders = [order[::-1] for order in bit_orders(n_dp, n_seq)]
    steps = len(orders[0])
    parts = gather_parts(shard.shape)

    def flipped(keys):
        other = dict(index)
        for axis, bit in keys:
            other[axis] = other[axis] + (1 - 2 * ((index[axis] // 2**bit) % 2)) * 2**bit
        return (other["dp"], other["seq"])

    def half_of(ref, half):
        top, height, left, wide = parts[half]
        return ref.at[pl.ds(top, height), pl.ds(left, wide)]

    def copy_of(half, path, k):
        order = orders[half]
        dp, seq = flipped([order[i] for i in path])
        dst = half_of(whole.at[dp * n_seq + seq], half)
        code = sum(2**i for i in path) + 2**k
        return pltpu.make_async_remote_copy(
            src_ref=dst if path else half_of(shard, half), dst_ref=dst,
            send_sem=ssem.at[half, code], recv_sem=rsem.at[half, code],
            device_id=flipped([order[k]]), device_id_type=MESH,
        )

    paths = sorted(
        (tuple(i for i in range(steps) if code >> i & 1) for code in range(2**steps)), key=lambda p: (len(p), p)
    )
    keep = pltpu.make_async_copy(shard, whole.at[index["dp"] * n_seq + index["seq"]], own_sem)

    def greet():
        barrier = pltpu.get_barrier_semaphore()
        for key in orders[0]:
            pl.semaphore_signal(barrier, inc=1, device_id=flipped([key]), device_id_type=MESH)
        return steps

    def level(hops):
        if hops == 0:
            keep.start()
        for path in paths:
            if len(path) == hops:
                for half in range(len(parts)):
                    if path:
                        copy_of(half, path[:-1], path[-1]).wait_recv()
                    for k in range((path[-1] if path else -1) + 1, steps):
                        copy_of(half, path, k).start()

    def finish():
        for path in paths:
            if path:
                for half in range(len(parts)):
                    copy_of(half, path[:-1], path[-1]).wait_send()
        keep.wait()

    return steps, greet, level, finish


def gather_kernel(sizes, shard, whole, *sems):
    steps, greet, level, finish = gather_steps(sizes, shard, whole, *sems)
    pl.semaphore_wait(pltpu.get_barrier_semaphore(), greet())
    for hops in range(steps + 1):
        level(hops)
    finish()


def gather_greet(sizes):
    index = {"dp": lax.axis_index("dp"), "seq": lax.axis_index("seq")}
    order = bit_orders(*sizes)[0]
    for axis, bit in order:
        other = dict(index)
        other[axis] = index[axis] + (1 - 2 * ((index[axis] // 2**bit) % 2)) * 2**bit
        pl.semaphore_signal(
            pltpu.get_barrier_semaphore(), inc=1, device_id=(other["dp"], other["seq"]), device_id_type=MESH
        )
    return len(order)


def gather_beside(sizes, turn, shards, wholes, sems, turns):
    plans = [
        gather_steps(sizes, shard, whole, *sems[3 * i : 3 * i + 3])
        for i, (shard, whole) in enumerate(zip(shards, wholes))
    ]
    if not plans:
        return
    for hops, when in enumerate(turns):
        @pl.when(turn == when)
        def _(hops=hops):
            for plan in plans:
                plan[2](hops)


def gather_rest(sizes, turn, shards, wholes, sems, done, final):
    plans = [
        gather_steps(sizes, shard, whole, *sems[3 * i : 3 * i + 3])
        for i, (shard, whole) in enumerate(zip(shards, wholes))
    ]
    if not plans:
        return

    @pl.when(turn == final)
    def _():
        for hops in range(done, plans[0][0] + 1):
            for plan in plans:
                plan[2](hops)
        for plan in plans:
            plan[3]()


def gather_sems(sizes, shard):
    sems = pltpu.SemaphoreType.DMA((len(gather_parts(shard.shape)), sizes[0] * sizes[1]))
    return [pltpu.SemaphoreType.DMA, sems, sems]


def whole_like(sizes, shard):
    return jax.ShapeDtypeStruct((sizes[0] * sizes[1],) + shard.shape, shard.dtype)


def flat_rows(whole):
    return whole.reshape((whole.shape[0] * whole.shape[1],) + whole.shape[2:])


def gather_rows(sizes, shard, cid):
    anywhere = pl.BlockSpec(memory_space=pl.ANY)
    whole = pl.pallas_call(
        functools.partial(gather_kernel, sizes),
        in_specs=[anywhere],
        out_specs=anywhere,
        out_shape=whole_like(sizes, shard),
        scratch_shapes=gather_sems(sizes, shard),
        compiler_params=pltpu.CompilerParams(collective_id=cid, has_side_effects=True),
        name="gather_rows",
    )(shard)
    return flat_rows(whole)


def from_behind(value, axis, steps):
    count = lax.axis_size(axis)
    first, last = (max(0, -steps), min(count, count - steps))
    return lax.ppermute(value, axis, [(source, source + steps) for source in range(first, last)])


def rms_scale(values, gain):
    return values * lax.rsqrt(jnp.mean(values * values, axis=-1, keepdims=True) + norm_eps) * gain


def doc_ids(lengths, positions):
    ends = jnp.cumsum(lengths)
    inside = (positions[:, None] >= ends[None, :]).astype(jnp.int32)
    return jnp.where(positions >= 0, jnp.sum(inside, axis=1), -1)


def contract_rows(left, right):
    return tn(left, right)


def contract_cols(left, right):
    return nt(left, right)


def local(
    n_dp, n_seq, tokens, doc_lengths, norm_gain, w_qkv, w_beta, conv_weight, head_gain, w_out, mlp_gain, w_mlp_in, w_down, grad_out,
):
    rows, model = tokens.shape
    heads = w_beta.shape[1]
    width = head_gain.shape[0]
    taps_n = conv_weight.shape[0]
    qkv = w_qkv.shape[1]
    chunk = min(128, rows)
    n_chunk = rows // chunk
    both = ("dp", "seq")

    sizes = (n_dp, n_seq)
    own_kernels = (model // (n_dp * n_seq)) % 32 == 0 and heads > (n_dp * n_seq).bit_length()
    w_d = lax.all_gather(w_down, both, axis=0, tiled=True)
    w_in = jnp.concatenate([w_qkv, jnp.pad(w_beta, ((0, 0), (0, 128 - heads)))], axis=1)
    if own_kernels:
        beside = [w_mlp_in]
        w_o = lax.all_gather(w_out, both, axis=0, tiled=True)
        w_in = gather_rows(sizes, w_in, 3)
    else:
        beside = []
        w_in, w_o, w_m = (lax.all_gather(w, both, axis=0, tiled=True) for w in (w_in, w_out, w_mlp_in))

    inputs = tokens.astype(f32)
    norm_one, pull_one = jax.vjp(rms_scale, inputs, norm_gain.astype(f32))
    xn1 = norm_one.astype(bf16)
    projected = nn(xn1, w_in)
    logits = projected[:, qkv : qkv + heads]
    start = lax.axis_index("seq") * rows
    docs_pad = doc_ids(doc_lengths[0], start - taps_n + 1 + jnp.arange(rows + taps_n - 1, dtype=jnp.int32))
    docs = docs_pad[taps_n - 1 :]
    by_chunk = docs.reshape(n_chunk, chunk)
    before = docs_pad[taps_n - 2 : taps_n - 2 + rows].reshape(n_chunk, chunk)[:, :1]
    aux = jnp.stack(
        [(by_chunk == before).reshape(-1), (by_chunk == by_chunk[:, -1:]).reshape(-1)]
        + [docs_pad[taps_n - 1 - b : taps_n - 1 - b + rows] == docs for b in (1, 2, 3)]
        + [docs < -5] * 3,
        axis=1,
    ).astype(f32)
    docs_c, docs_r = docs[:, None], docs[None, :]
    if own_kernels:
        halo = jnp.zeros((8, qkv), f32)
    else:
        received = from_behind(projected[rows - taps_n + 1 :, :qkv].astype(bf16), "seq", 1).astype(f32)
        halo = jnp.pad(received, ((8 - taps_n + 1, 0), (0, 0)))
    taps = jnp.pad(conv_weight.astype(f32), ((0, 8 - taps_n), (0, 0)))

    def third(block_rows):
        return [pl.BlockSpec((block_rows, width), lambda h, t=t: (0, t * heads + h)) for t in range(3)]

    def per_head(block_rows):
        return pl.BlockSpec((block_rows, width), lambda h: (0, h))

    def whole(shape):
        return pl.BlockSpec(shape, lambda h: (0,) * len(shape))

    state_block = pl.BlockSpec((1, width, width), lambda h: (h, 0, 0))
    params = pltpu.CompilerParams(vmem_limit_bytes=VMEM_LIMIT, dimension_semantics=("arbitrary",))
    cols = heads * width
    token_like = jax.ShapeDtypeStruct((rows, cols), f32)
    chunk_like = jax.ShapeDtypeStruct((rows, heads * chunk), f32)
    state_like = jax.ShapeDtypeStruct((n_chunk * width, cols), f32)
    common_specs = (
        third(rows) + third(8) + third(8)
        + [whole((rows, 8)), whole((rows, 1)), whole((1, rows)), whole((rows, heads))]
    )
    common = (projected,) * 3 + (halo,) * 3 + (taps,) * 3 + (aux, docs_c, docs_r, logits)
    chunk_block = pl.BlockSpec((rows, chunk), lambda h: (0, h))
    anywhere = pl.BlockSpec(memory_space=pl.ANY)
    maps_like = jax.ShapeDtypeStruct((heads, width, width), f32)
    cq, ck, cv, w_s, u_s, qt, o0, t_s, p_s, kk_s, dt, ft, seg_map, seg_turned, seg_add, *wholes = pl.pallas_call(
        functools.partial(local_kernel, sizes, chunk, len(beside)),
        grid=(heads,),
        in_specs=[anywhere] * (len(beside) + bool(beside)) + common_specs,
        out_specs=[per_head(rows)] * 7 + [chunk_block] * 3 + [per_head(n_chunk * width)] * 2 + [state_block] * 3
        + [anywhere] * len(beside) + ([whole((8, qkv))] if beside else []),
        out_shape=[token_like] * 7
        + [jax.ShapeDtypeStruct((rows, heads * chunk), bf16)] * 2 + [chunk_like] + [state_like] * 2 + [maps_like] * 3
        + [whole_like(sizes, w) for w in beside] + ([jax.ShapeDtypeStruct((8, qkv), f32)] if beside else []),
        scratch_shapes=[pltpu.VMEM((rows + 8, width), f32)]
        + ([pltpu.VMEM((8, qkv), f32), pltpu.SemaphoreType.DMA, pltpu.SemaphoreType.DMA] if beside else [])
        + [sem for w in beside for sem in gather_sems(sizes, w)],
        compiler_params=pltpu.CompilerParams(
            vmem_limit_bytes=VMEM_LIMIT, dimension_semantics=("arbitrary",),
            **(dict(collective_id=4, has_side_effects=True) if beside else {}),
        ),
        name="delta_local",
    )(*beside, *([projected] if beside else []), *common)
    if beside:
        *wholes, halo = wholes
        common = common[:3] + (halo,) * 3 + common[6:]
        (w_m,) = (flat_rows(w) for w in wholes)

    def relay(back, maps, adds, cid):
        return pl.pallas_call(
            functools.partial(relay_kernel, n_seq, back),
            in_specs=[pl.BlockSpec(memory_space=pltpu.VMEM)] * 2,
            out_specs=pl.BlockSpec(memory_space=pltpu.VMEM),
            out_shape=jax.ShapeDtypeStruct((heads, width, width), bf16),
            scratch_shapes=[
                pltpu.VMEM((heads, width, width), bf16),
                pltpu.SemaphoreType.DMA((heads,)),
                pltpu.SemaphoreType.DMA((heads,)),
            ],
            compiler_params=pltpu.CompilerParams(collective_id=cid, has_side_effects=True, vmem_limit_bytes=VMEM_LIMIT),
            name="relay_back" if back else "relay",
        )(maps, adds)

    state_in = relay(False, seg_map, seg_add, 0)
    gain_h = head_gain.astype(f32)[None, :]
    some = 4 if heads % 4 == 0 else 1

    def several(block_rows):
        return pl.BlockSpec((block_rows, some * width), lambda h: (0, h))

    z_s, mixed, head_out = pl.pallas_call(
        functools.partial(output_kernel, chunk),
        grid=(heads // some,),
        in_specs=[pl.BlockSpec((some, width, width), lambda h: (h, 0, 0))]
        + [several(n_chunk * width)] * 2 + [several(rows)] * 2 + [whole((1, width))],
        out_specs=[several(n_chunk * width), several(rows), several(rows)],
        out_shape=[state_like, token_like, jax.ShapeDtypeStruct((rows, cols), bf16)],
        compiler_params=params,
        name="delta_out",
    )(state_in, dt, ft, qt, o0, gain_h)

    hidden_one = inputs + nn(head_out, w_o)
    norm_two, pull_two = jax.vjp(rms_scale, hidden_one, mlp_gain.astype(f32))
    xn2 = norm_two.astype(bf16)
    gate_up = nn(xn2, w_m)
    inner = gate_up.shape[1] // 2
    gate, up = gate_up[:, :inner].astype(f32), gate_up[:, inner:].astype(f32)
    open_gate = jax.nn.sigmoid(gate)
    hidden = (gate * open_gate * up).astype(bf16)
    out = (hidden_one + nn(hidden, w_d)).astype(bf16)

    grad_in = grad_out.astype(f32)
    d_hidden = contract_cols(grad_out, w_d)
    d_gate = (d_hidden * up * (open_gate * (1.0 + gate * (1.0 - open_gate)))).astype(bf16)
    d_up = (d_hidden * (gate * open_gate)).astype(bf16)
    d_gate_up = jnp.concatenate([d_gate, d_up], axis=1)
    d_from_two, d_mlp_gain = pull_two(contract_cols(d_gate_up, w_m))
    d_hidden_one = grad_in + d_from_two
    d_att = d_hidden_one.astype(bf16)
    d_head = contract_cols(d_att, w_o)

    parts = [
        (hidden, grad_out, "stack", [(512, 0)] * 2),
        (xn2, d_gate_up, "plain", [(512, 2), (1024, 0)] * 3 + [(512, 2), (512, 0)]),
        (head_out, d_att, "plain", [(1024, 0)]),
    ]
    if own_kernels:
        parts[1] = parts[1][:3] + (B_COLS,)
        units, slots, grads_like, scratch = scatter_layout(
            sizes, parts, B_ORDER, {"plain": 2, "stack": 1}
        )
        steps = (n_dp * n_seq).bit_length() - 1
        plan = back_plan(len(units), steps, heads, 3)

        def late(spec):
            shape, index = spec.block_shape, spec.index_map
            return pl.BlockSpec(shape, lambda t: index(jnp.maximum(t - heads, 0)))

        def soon(spec):
            shape, index = spec.block_shape, spec.index_map
            return pl.BlockSpec(shape, lambda t: index(jnp.minimum(t, heads - 1)))

        def each(spec):
            shape, index = spec.block_shape, spec.index_map
            return pl.BlockSpec(shape, lambda t: index(jnp.where(t < heads, t, t - heads)))

        n_prod = len(parts)
        results = pl.pallas_call(
            functools.partial(back_scatter_kernel, sizes, chunk, heads, units, slots, plan, n_prod),
            grid=(2 * heads,),
            in_specs=[anywhere] * (2 * n_prod)
            + [soon(per_head(rows))] * 2 + [whole((1, width)), soon(per_head(rows)), each(per_head(n_chunk * width))]
            + [whole((heads, width, width))]
            + [late(spec) for spec in common_specs + [per_head(rows)] * 5 + [chunk_block] * 3 + [per_head(n_chunk * width)]],
            out_specs=[whole(like.shape) for like in grads_like]
            + [late(spec) for spec in [per_head(rows)] * 3 + [per_head(8)] * 3]
            + [whole((16, qkv)), whole((rows, heads)), whole((8, width))],
            out_shape=grads_like + [jax.ShapeDtypeStruct((rows, cols), bf16)] * 3
            + [jax.ShapeDtypeStruct((8, cols), f32)] * 3
            + [jax.ShapeDtypeStruct((16, qkv), bf16), jax.ShapeDtypeStruct((rows, heads), f32), jax.ShapeDtypeStruct((8, width), f32)],
            scratch_shapes=[pltpu.VMEM(p[0].shape, bf16) for p in parts]
            + [pltpu.VMEM((2, rows, 1024) if i == RINGED else p[1].shape, bf16) for i, p in enumerate(parts)]
            + [pltpu.SemaphoreType.DMA((n_prod, 2)), pltpu.SemaphoreType.DMA((2,))]
            + [pltpu.VMEM((model, rows), bf16)]
            + [
                pltpu.VMEM((heads, rows, width), bf16), pltpu.VMEM((heads, n_chunk * width, width), f32),
                pltpu.VMEM((heads, width, width), f32), pltpu.VMEM((heads, width, width), bf16),
                pltpu.VMEM((heads, width, width), bf16),
                pltpu.SemaphoreType.DMA((heads,)), pltpu.SemaphoreType.DMA((heads,)),
            ]
            + [pltpu.VMEM((rows + 8, width), f32)] + [pltpu.VMEM((rows + 16, width), f32)] * 3
            + [pltpu.VMEM((heads, 3, 8, width), f32)] * 2 + [pltpu.VMEM((heads, 3, 16, width), f32)]
            + [pltpu.SemaphoreType.DMA((heads,)), pltpu.SemaphoreType.DMA((heads,))]
            + scratch,
            compiler_params=pltpu.CompilerParams(
                collective_id=1, has_side_effects=True, vmem_limit_bytes=63 << 20, dimension_semantics=("arbitrary",)
            ),
            name="back_scatter",
        )(
            *[p[0] for p in parts], *[p[1] for p in parts], d_head, mixed, gain_h, qt, dt, seg_turned,
            *common, cq, ck, cv, w_s, u_s, t_s, p_s, kk_s, z_s,
        )
        (g_down, g_mlp, g_out), mains, tapped = results[:n_prod], results[n_prod : n_prod + 3], results[n_prod + 3 : n_prod + 6]
        tails, d_logits, d_head_gain = results[n_prod + 6 :]
        d_conv = jnp.concatenate(tapped, axis=1)[:taps_n]
        small = jnp.concatenate(
            [
                jnp.zeros((9, model), f32),
                d_mlp_gain[None],
                d_conv.reshape(-1, model),
                jnp.pad(d_head_gain[0:1], ((0, 0), (0, model - width))),
            ],
            axis=0,
        )
        count = small.shape[0]
        small = jnp.pad(small, ((0, -count % 8), (0, 0)))
        parts = [(xn1, main, "plain", cols_in) for main, cols_in in zip(mains, F_COLS)]
        units, slots, grads_like, scratch = scatter_layout(sizes, parts, None, {"plain": 3})
        vmem = pl.BlockSpec(memory_space=pltpu.VMEM)
        *g_in, small, grad_tokens = pl.pallas_call(
            functools.partial(final_kernel, sizes, units, slots),
            in_specs=[anywhere] * 4 + [vmem] * 7,
            out_specs=[vmem] * 5,
            out_shape=grads_like + [jax.ShapeDtypeStruct(small.shape, f32), jax.ShapeDtypeStruct((rows, model), bf16)],
            scratch_shapes=[pltpu.VMEM((rows, model), bf16)] * 3 + [pltpu.VMEM(w_in.shape, bf16)]
            + [pltpu.VMEM(small.shape, f32), pltpu.VMEM((8, model), f32), pltpu.SemaphoreType.DMA((4,))]
            + [pltpu.VMEM((model, rows), bf16)]
            + [pltpu.VMEM((2 * steps,) + small.shape, f32), pltpu.SemaphoreType.DMA((steps,)), pltpu.SemaphoreType.DMA((steps,))]
            + scratch,
            compiler_params=pltpu.CompilerParams(collective_id=2, has_side_effects=True, vmem_limit_bytes=63 << 20),
            name="final_scatter",
        )(
            *mains, w_in, tails, xn1, tokens, d_hidden_one, norm_gain.astype(f32)[None],
            jnp.pad(d_logits, ((0, 0), (0, 128 - heads))).astype(bf16), small,
        )
        g_in = jnp.concatenate(g_in, axis=1)
        mine = (lax.axis_index("dp") * n_seq + lax.axis_index("seq")) * (model // (n_dp * n_seq))
        g_beta = lax.dynamic_slice(small[:heads], (0, mine), (heads, model // (n_dp * n_seq))).T
        s_norm, s_mlp = small[heads], small[heads + 1]
        s_conv = small[heads + 2 : count - 1].reshape(taps_n, qkv)
        s_head = small[count - 1, :width]
    else:
        do, b_s, seed, d_head_gain = pl.pallas_call(
            functools.partial(seed_kernel, chunk),
            grid=(heads,),
            in_specs=[per_head(rows), per_head(rows), whole((1, width)), per_head(rows), per_head(n_chunk * width)],
            out_specs=[per_head(rows), per_head(n_chunk * width), state_block, whole((8, width))],
            out_shape=[token_like, state_like, jax.ShapeDtypeStruct((heads, width, width), f32), jax.ShapeDtypeStruct((8, width), f32)],
            compiler_params=params,
            name="delta_seed",
        )(d_head, mixed, gain_h, qt, dt)
        grad_end = relay(True, seg_turned, seed, 1)
        outs = pl.pallas_call(
            functools.partial(back_kernel, chunk),
            grid=(heads,),
            in_specs=common_specs + [per_head(rows)] * 5 + [chunk_block] * 3
            + [per_head(n_chunk * width), per_head(rows), per_head(n_chunk * width), per_head(n_chunk * width), state_block],
            out_specs=[per_head(rows)] * 3 + [per_head(8)] * 6 + [whole((rows, heads))],
            out_shape=[token_like] * 3 + [jax.ShapeDtypeStruct((8, cols), f32)] * 6 + [jax.ShapeDtypeStruct((rows, heads), f32)],
            scratch_shapes=[pltpu.VMEM((rows + 8, width), f32)] + [pltpu.VMEM((rows + 16, width), f32)] * 3,
            compiler_params=params,
            name="delta_back",
        )(*common, cq, ck, cv, w_s, u_s, t_s, p_s, kk_s, z_s, do, dt, b_s, grad_end)
        d_main = jnp.concatenate(outs[:3], axis=1)
        d_early = jnp.concatenate(outs[3:6], axis=1)
        d_conv = jnp.concatenate(outs[6:9], axis=1)[:taps_n]
        d_logits = outs[9]
        returned = from_behind(d_early[8 - taps_n + 1 :].astype(bf16), "seq", -1).astype(f32)
        d_projected = d_main + jnp.pad(returned, ((rows - taps_n + 1, 0), (0, 0)))
        d_proj_b = jnp.concatenate(
            [d_projected.astype(bf16), jnp.pad(d_logits.astype(bf16), ((0, 0), (0, 128 - heads)))], axis=1
        )
        d_from_one, d_norm_gain = pull_one(contract_cols(d_proj_b, w_in))
        grad_tokens = (d_hidden_one + d_from_one).astype(bf16)

        d_beta_rows = tn(d_logits.astype(bf16), xn1)
        g_down, g_mlp, g_out, g_in, g_beta = (
            lax.psum_scatter(grad, both, scatter_dimension=0, tiled=True)
            for grad in [contract_rows(left, right) for left, right, _, _ in parts]
            + [contract_rows(xn1, d_proj_b[:, :qkv]), d_beta_rows.T]
        )
        s_norm, s_conv, s_head, s_mlp = lax.psum((d_norm_gain, d_conv, d_head_gain[0], d_mlp_gain), both)
    return (out, grad_tokens, s_norm, g_in, g_beta, s_conv, s_head, g_out, s_mlp, g_mlp, g_down)


def solution(mesh):
    split = P(("dp", "seq"), None)
    placed = (split, P("dp", None), P(), split, split, P(), P(), split, P(), split, split, split)
    return jax.shard_map(
        functools.partial(local, mesh.shape["dp"], mesh.shape["seq"]),
        mesh=mesh,
        in_specs=placed,
        out_specs=(split, split, P(), split, split, P(), P(), split, P(), split, split),
        check_vma=False,
    )
```
